128 devices in a mesh: layer: 8 (over x, core), row: 4 (over z), col: 4 (over y).
Axes of the slice: x: 4, y: 4, z: 4, core: 2. Of those that a mesh axis runs over, the one named last changes fastest.
Arguments:
- grad_tiles: bfloat16 [1792, 128, 1152], P(('layer', 'row', 'col')), parts along dimension 0, may hold values from -6 to 6
- tile_ids: int32 [1792], P(('layer', 'row', 'col')), parts along dimension 0, may hold values from 0 to 223, as said below
- momentum: float32 [28672, 9216], P(('layer', 'row'), 'col'), parts along dimension 0, may hold values from -60 to 60
Outputs:
- new_momentum: float32 [28672, 9216], P(('layer', 'row'), 'col'), parts along dimension 0
- update: bfloat16 [28672, 9216], P(('layer', 'row'), 'col'), parts along dimension 0
The draws below stay inside these ranges and needn't reach their ends.
There are 8 independent parts, one for each index of `layer`. The reference program is written for one: setup_inputs(seed, part) draws one part's arguments, and reference() takes and returns one part's arrays. A program takes and returns all parts, laid end to end along the dimension named above; each array names one. Nothing has to cross between parts.
Inputs may be any that keep to these rules, and one draw needn't show every extreme that they name: tile_ids is a permutation of 0 to 223. The owner of a tile is the device whose block of the 3584 x 9216 matrix (rows split over row, columns over col) contains it; the 14 tiles of one device belong to 14 different owners.
All inputs are finite; a program needn't handle non-finite values.
Results may differ from the reference program's by a relative error of at most 0.0058.
Values may be sent and summed in bfloat16 or wider, within the bound.
No kernel may reach another device: no remote copies, remote signals or barrier semaphores. Data moves between devices by JAX's collectives and lax.ppermute only.
A program may use at most 192 MiB of HBM per device.

```python
import math
import jax
import jax.numpy as jnp

ROWS = 3584
COLS = 9216
BLOCK = 128
TILE_COLS = 1152
TILES_DEV = 14
TILES = 224
N_ROW = 4
N_COL = 4


def draw_tile_ids(key, part):
    key = jax.random.fold_in(key, 11)
    key_pi, key_sigma, key_offset, key_order = jax.random.split(key, 4)
    groups = N_ROW * N_COL
    tile_count = TILES_DEV
    owner_blocks = ROWS // N_ROW // BLOCK
    source_perm = jax.random.permutation(key_pi, groups)
    owner_perm = jax.random.permutation(key_sigma, groups)
    offsets = jax.random.permutation(key_offset, groups)[:tile_count]
    slot_order = jax.random.permutation(key_order, tile_count)
    owner_inverse = jnp.argsort(owner_perm).astype(jnp.int32)
    sources = jnp.arange(groups, dtype=jnp.int32)[:, None]
    places = slot_order[None, :].astype(jnp.int32)
    shifted = (source_perm[sources] - offsets[places]) % groups
    owners = owner_inverse[shifted]
    grid_row = owners // N_COL
    grid_col = owners % N_COL
    tile_row = grid_row * owner_blocks + places // 2
    tile_half = grid_col * 2 + places % 2
    ids = tile_row * (2 * N_COL) + tile_half
    return ids.reshape(-1).astype(jnp.int32)


def draw_momentum(key, part):
    key = jax.random.fold_in(key, 23)
    key_rows, key_cols, key_base = jax.random.split(key, 3)
    row_scale = jnp.exp(jax.random.uniform(key_rows, (ROWS, 1), jnp.float32) * math.log(10.0))
    col_scale = jnp.exp(jax.random.uniform(key_cols, (1, COLS), jnp.float32) * math.log(10.0))
    base = jnp.clip(jax.random.normal(key_base, (ROWS, COLS), jnp.float32), -6.0, 6.0)
    return (0.1 * base * row_scale * col_scale).astype(jnp.float32)


def steps_of(key, extent, cuts, smallest, largest):
    def one(dim, parts):
        steps = jax.random.uniform(jax.random.fold_in(jax.random.fold_in(key, 6), dim), (parts,), jnp.float32, smallest / len(cuts), largest / len(cuts))
        return jnp.repeat(jnp.exp(steps), extent[dim] // parts).reshape((-1,) + (1,) * (len(extent) - dim - 1))

    factor_of = one(*cuts[0])
    for cut in cuts[1:]:
        factor_of = factor_of * one(*cut)
    return factor_of


def gaussian(stream_key, shape, deviation, most, cuts=(), held_as=jnp.bfloat16):
    entries = deviation * jax.random.normal(stream_key, shape, jnp.float32)
    if cuts:
        entries = entries * steps_of(stream_key, shape, cuts, -0.22, 0.18)
    return jnp.clip(entries, -most, most).astype(held_as)


def setup_inputs(seed: int = 0, part: int = 0) -> dict:
    key_list = jax.random.split(jax.random.key(seed), 4)
    part_keys = jax.random.split(jax.random.fold_in(key_list[3], part), 4)
    return {
        "grad_tiles": gaussian(part_keys[0], (TILES, BLOCK, TILE_COLS), 1.0, 6.0, ((0, 16),)),
        "tile_ids": draw_tile_ids(jax.random.fold_in(jax.random.fold_in(key_list[3], part), 71), part),
        "momentum": draw_momentum(jax.random.fold_in(jax.random.fold_in(key_list[3], part), 71), part),
    }


MOMENTUM_RATE = 0.95
COEF_LINEAR = 3.4445
COEF_CUBIC = -4.775
COEF_QUINTIC = 2.0315
EPSILON = 1e-06

def reference(grad_tiles, tile_ids, momentum):
    order = jnp.argsort(tile_ids)
    tiles = grad_tiles[order].astype(jnp.float32)
    halves = 2 * N_COL
    gradient = tiles.reshape(ROWS // BLOCK, halves, BLOCK, TILE_COLS).transpose(0, 2, 1, 3).reshape(ROWS, COLS)
    new_momentum = MOMENTUM_RATE * momentum + gradient
    direction = gradient + MOMENTUM_RATE * new_momentum
    rounded = direction.astype(jnp.bfloat16)
    gram = jnp.dot(rounded, rounded.T, preferred_element_type=jnp.float32)
    total = jnp.sum(jnp.square(rounded.astype(jnp.float32)))
    factor = math.sqrt(ROWS) / (2.0 * (jnp.sqrt(total) + EPSILON))
    scaled = (factor * factor * gram).astype(jnp.bfloat16)
    square = jnp.dot(scaled, scaled, preferred_element_type=jnp.float32)
    poly = (COEF_CUBIC * scaled.astype(jnp.float32) + COEF_QUINTIC * square).astype(jnp.bfloat16)
    product = jnp.dot(poly, rounded, preferred_element_type=jnp.float32)
    update = (math.sqrt(COLS) * factor * (COEF_LINEAR * rounded.astype(jnp.float32) + product)).astype(jnp.bfloat16)
    return (new_momentum, update)
```

```python
import math

import jax
import jax.numpy as jnp
from jax import lax
from jax.experimental import pallas as pl
from jax.experimental.pallas import tpu as pltpu
from jax.sharding import Mesh
from jax.sharding import PartitionSpec as P

ROWS = 3584
COLS = 9216
MOMENTUM_RATE = 0.95
COEF_LINEAR = 3.4445
COEF_CUBIC = -4.775
COEF_QUINTIC = 2.0315
EPSILON = 1e-06

HEIGHT = 896
HALF = 1152
TILE = 128
SLOT = 1168
SIDE = 256
BLOCKS = ROWS // SIDE
HALF_BLOCKS = BLOCKS // 2
CHUNK = HALF_BLOCKS * SIDE
PARTS = ((0, 608), (608, 592), (1200, 592))
WIDE = 640
AROUND = ROWS + CHUNK
BACK_ROWS = 4032

AXES = ("x", "core", "zm", "zl", "y")
PLANE = ("zm", "zl", "y")
BF16 = jnp.bfloat16
F32 = jnp.float32
MIB = 1 << 20
ANY = pl.BlockSpec(memory_space=pl.ANY)
VMEM = pl.BlockSpec(memory_space=pltpu.VMEM)
SMEM = pl.BlockSpec(memory_space=pltpu.SMEM)


def cost(flops, size):
    return pl.CostEstimate(flops=int(flops), bytes_accessed=int(size), transcendentals=0)


def move(x, route):
    pairs = []
    for c in range(2):
        for m in range(2):
            for a in range(2):
                for y in range(4):
                    c2, m2, a2, y2 = route(c, m, a, y)
                    pairs.append((((c * 2 + m) * 2 + a) * 4 + y, ((c2 * 2 + m2) * 2 + a2) * 4 + y2 % 4))
    return lax.ppermute(x, AXES[1:], pairs)


def up(x):
    return move(x, lambda c, m, a, y: (c, m, a, y + 1))


def down(x):
    return move(x, lambda c, m, a, y: (c, m, a, y + 3))


def across(x):
    return move(x, lambda c, m, a, y: (c, m, 1 - a, y))


def swap(x):
    return move(x, lambda c, m, a, y: (1 - c, m, a, y))


def pack_kernel(details, tiles, out):
    @pl.loop(0, out.shape[0])
    def _(o):
        slot = details[o]
        for j in range(HALF // TILE):
            out[o, j * TILE : (j + 1) * TILE, :] = tiles[slot, :, j * TILE : (j + 1) * TILE]
        place = jnp.full((SLOT - HALF, TILE), details[16 + o], jnp.int32)
        out[o, HALF:, :] = place.astype(F32).astype(BF16)


def pack(details, tiles):
    n = details.shape[0] // 2
    return pl.pallas_call(
        pack_kernel,
        in_specs=[SMEM, VMEM],
        out_specs=VMEM,
        out_shape=jax.ShapeDtypeStruct((n, SLOT, TILE), BF16),
        compiler_params=pltpu.CompilerParams(vmem_limit_bytes=32 * MIB),
        cost_estimate=cost(0, 2 * n * SLOT * TILE * 2),
    )(details, tiles)


def momentum_kernel(info, tile, old, *refs):
    new, out = refs[-2:]
    for j in range(HALF // TILE):
        columns = slice(j * TILE, (j + 1) * TILE)
        g = tile[0, columns, :].astype(F32)
        fresh = MOMENTUM_RATE * old[:, columns] + g
        new[:, columns] = fresh
        out[:, columns] = (g + MOMENTUM_RATE * fresh).astype(BF16)


def update_momentum(info, arrived, momentum, turn, so_far):
    def half(s):
        return (turn + s[14]) % 2

    more = () if so_far is None else (so_far,)
    return pl.pallas_call(
        momentum_kernel,
        grid_spec=pltpu.PrefetchScalarGridSpec(
            num_scalar_prefetch=1,
            grid=(HEIGHT // TILE,),
            in_specs=[
                pl.BlockSpec((1, SLOT, TILE), lambda r, s: (s[2 * r + half(s)], 0, 0)),
                pl.BlockSpec((TILE, HALF), lambda r, s: (r, half(s))),
            ]
            + [ANY] * len(more),
            out_specs=[
                pl.BlockSpec((TILE, HALF), lambda r, s: (r, half(s))),
                pl.BlockSpec((TILE, HALF), lambda r, s: (r, 0)),
            ],
        ),
        out_shape=[
            jax.ShapeDtypeStruct(momentum.shape, F32),
            jax.ShapeDtypeStruct((HEIGHT, HALF), BF16),
        ],
        input_output_aliases={3: 0} if more else {},
        cost_estimate=cost(0, HEIGHT * HALF * 12),
    )(info, arrived, momentum, *more)


def panel_rows(info, which):
    c, a = info[0], info[2]
    other, t = divmod(which, 2)
    core = 1 - c if other else c
    return 2 * core + (a + t) % 2


def chip_at(info, flip, dy):
    a, y = info[2], info[3]
    return (1 - a if flip else a) * 4 + (y + dy) % 4


def load_all(copies, sems):
    copies = [pltpu.make_async_copy(src, dst, sems.at[i]) for i, (src, dst) in enumerate(copies)]
    for copy in copies:
        copy.start()
    for copy in copies:
        copy.wait()


def gram_kernel(dests, info, *refs):
    blocks, outs = refs[:4], refs[4:-2]
    panel, sems = refs[-2:]
    starts = [pl.multiple_of(panel_rows(info, i) * HEIGHT, HEIGHT) for i in range(4)]
    load_all([(blocks[i], panel.at[pl.ds(starts[i], HEIGHT)]) for i in range(4)], sems)

    def term(b, d):
        left = panel[pl.ds(pl.multiple_of(b * SIDE, SIDE), SIDE)]
        right = panel[pl.ds(pl.multiple_of((b + d) % BLOCKS * SIDE, SIDE), SIDE)]
        return lax.dot_general(left, right, (((1,), (1,)), ((), ())), preferred_element_type=F32)

    base = HALF_BLOCKS * info[0]
    if len(dests) == 1:
        d = chip_at(info, *dests[0])
        for b in range(HALF_BLOCKS):
            block = term(base + b, d).astype(BF16)
            for out, (row, size) in zip(outs, PARTS):
                low, high = max(row, b * SIDE), min(row + size, (b + 1) * SIDE)
                if low < high:
                    out[low - row : high - row] = block[low - b * SIDE : high - b * SIDE]
    else:

        @pl.loop(0, HALF_BLOCKS)
        def _(b):
            for dest, out in zip(dests, outs):
                block = term(base + b, chip_at(info, *dest))
                out[pl.ds(pl.multiple_of(b * SIDE, SIDE), SIDE)] = block.astype(out.dtype)


def gram_chunks(info, blocks, dests, shapes):
    return pl.pallas_call(
        lambda *refs: gram_kernel(dests, *refs),
        in_specs=[SMEM] + [ANY] * 4,
        out_specs=[VMEM] * len(shapes),
        out_shape=shapes,
        scratch_shapes=[pltpu.VMEM((ROWS, HALF), BF16), pltpu.SemaphoreType.DMA((4,))],
        compiler_params=pltpu.CompilerParams(vmem_limit_bytes=48 * MIB),
        cost_estimate=cost(len(dests) * 2 * CHUNK * SIDE * HALF, 8.3e6 + len(dests) * CHUNK * SIDE * 4),
    )(info, *blocks)


def chunk(dtype=BF16, rows=CHUNK):
    return jax.ShapeDtypeStruct((rows, SIDE), dtype)


def second_sums_kernel(p1, p2, p3, r1, r2, r3, q1, q2, q3):
    for own, got, out, (row, size) in zip((p1, p2, p3), (r1, r2, r3), (q1, q2, q3), PARTS):
        if row:
            out[:row] = own[:row].astype(BF16)
        out[row : row + size] = (own[row : row + size] + got[...].astype(F32)).astype(BF16)
        if row + size < CHUNK:
            out[row + size :] = own[row + size :].astype(BF16)


def third_sums_kernel(p1, p2, g1, g2, g3, v1, v2):
    v1[...] = (p1[...] + (g1[...].astype(F32) + g3[...].astype(F32))).astype(BF16)
    v2[...] = (p2[...] + g2[...].astype(F32)).astype(BF16)


def last_sums_kernel(p, v1, v2, v3, out):
    total = p[...] + (v1[...].astype(F32) + v2[...].astype(F32) + v3[...].astype(F32))
    out[...] = total.astype(BF16)


def in_vmem(kernel, shapes, *args):
    size = sum(x.size * x.dtype.itemsize for x in args)
    return pl.pallas_call(
        kernel,
        in_specs=[VMEM] * len(args),
        out_specs=[VMEM] * len(shapes),
        out_shape=shapes,
        compiler_params=pltpu.CompilerParams(vmem_limit_bytes=32 * MIB),
        cost_estimate=cost(0, size),
    )(*args)


def turn_kernel(info, *refs):
    blocks, out, held, sems = refs[:4], refs[4], refs[5], refs[6]
    shift = pl.multiple_of(512 * info[0], TILE)
    load_all([(blocks[i].at[:, pl.ds(shift, WIDE)], held.at[i]) for i in range(4)], sems)
    for i in range(4):
        start = pl.multiple_of(panel_rows(info, i) * HEIGHT, TILE)
        for r in range(HEIGHT // TILE):
            piece = held[i, r * TILE : (r + 1) * TILE, :].T
            out[:, pl.ds(pl.multiple_of(start + r * TILE, TILE), TILE)] = piece
    out[:, ROWS:] = out[:, :CHUNK]


def turned_panel(info, blocks):
    return pl.pallas_call(
        turn_kernel,
        in_specs=[SMEM] + [ANY] * 4,
        out_specs=VMEM,
        out_shape=jax.ShapeDtypeStruct((WIDE, AROUND), BF16),
        scratch_shapes=[pltpu.VMEM((4, HEIGHT, WIDE), BF16), pltpu.SemaphoreType.DMA((4,))],
        compiler_params=pltpu.CompilerParams(vmem_limit_bytes=32 * MIB),
        cost_estimate=cost(0, 1.2e7),
    )(info, *blocks)


SOURCES = ((0, 0), (0, 3), (0, 1), (1, 0), (1, 1), (1, 3), (0, 2), (1, 2))


def apply_kernel(info, *refs):
    own, ends, swapped = refs[:7], refs[7:10], refs[10:14]
    turned = refs[14]
    outs = refs[15:19]
    direct, flipped, panel, mixed, stage, sems, panel_sem, out_sems = refs[19:]
    c, a = info[0], info[2]
    panel_copy = pltpu.make_async_copy(turned, panel, panel_sem)
    panel_copy.start()
    pieces = [(c, ref, 0, rel) for ref, rel in zip(own, SOURCES)]
    pieces += [(1 - c, swapped[0], 0, SOURCES[0]), (1 - c, swapped[3], 0, SOURCES[7])]
    pieces += [(1 - c, swapped[1 + n // 3], n % 3 * CHUNK, SOURCES[1 + n]) for n in range(6)]
    for n, (core, ref, row, rel) in enumerate(pieces):
        d = chip_at(info, *rel)

        @pl.loop(0, HALF_BLOCKS)
        def _(b):
            i = (core * HALF_BLOCKS + b + d) % BLOCKS
            src = ref.at[pl.ds(pl.multiple_of(row + b * SIDE, SIDE), SIDE)]
            pltpu.make_async_copy(src, direct.at[i, pl.ds(pl.multiple_of((7 - d) * SIDE, SIDE), SIDE)], sems.at[n]).start()

    d = chip_at(info, *SOURCES[7])
    last = []
    for ref, (row, size) in zip(ends, PARTS):
        for b in range(HALF_BLOCKS):
            low, high = max(row, b * SIDE), min(row + size, (b + 1) * SIDE)
            if low < high:
                i = (c * HALF_BLOCKS + b + d) % BLOCKS
                start = pl.multiple_of((7 - d) * SIDE + low - b * SIDE, 16)
                src = ref.at[low - row : high - row]
                last.append(pltpu.make_async_copy(src, direct.at[i, pl.ds(start, high - low)], sems.at[15 + len(last)]))
    for copy in last:
        copy.start()
    for n in range(15):
        whole = direct.at[0:HALF_BLOCKS, 0:SIDE]
        pltpu.make_async_copy(whole, whole, sems.at[n]).wait()
    for copy in last:
        copy.wait()
    panel_copy.wait()

    total = jnp.zeros((), F32)
    on = lax.broadcasted_iota(jnp.int32, (SIDE, SIDE), 0) == lax.broadcasted_iota(jnp.int32, (SIDE, SIDE), 1)
    diagonal = jnp.zeros((SIDE, SIDE), F32)
    for i in range(BLOCKS):
        diagonal += direct[i, 7 * SIDE :, :].astype(F32)
    total = jnp.sum(jnp.where(on, diagonal, 0.0))
    total = jnp.full((1, SIDE), total, F32)
    factor = math.sqrt(ROWS) / (2.0 * (jnp.sqrt(total) + EPSILON))
    square = factor * factor

    def product(i, x):
        first = pl.ds(pl.multiple_of((i + 7) % BLOCKS * SIDE, SIDE), 8 * SIDE)
        rest = pl.ds(pl.multiple_of((i + 1) % BLOCKS * SIDE, SIDE), 6 * SIDE)
        result = jnp.dot(x[:, first], direct[i], preferred_element_type=F32)
        result += jnp.dot(x[:, rest], flipped[i], preferred_element_type=F32)
        return result * square

    @pl.loop(0, BLOCKS)
    def _(i):
        for e in range(1, 7):
            far = (i + e) % BLOCKS
            flipped[i, (e - 1) * SIDE : e * SIDE, :] = direct[far, (7 - e) * SIDE : (8 - e) * SIDE, :].T
        columns = pl.ds(pl.multiple_of(i * SIDE, SIDE), SIDE)
        mix = COEF_CUBIC * panel[:, columns].astype(F32) + COEF_QUINTIC * product(i, panel)
        mix = mix.astype(BF16)
        mixed[:, columns] = mix

        @pl.when(i < HALF_BLOCKS)
        def _():
            mixed[:, pl.ds(pl.multiple_of(i * SIDE + ROWS, SIDE), SIDE)] = mix

    scale = math.sqrt(COLS) * factor
    sends = []
    for turn in range(2):
        half = 1 - c if turn else c

        @pl.loop(0, HALF_BLOCKS)
        def _(b):
            i = half * HALF_BLOCKS + b
            columns = pl.ds(pl.multiple_of(i * SIDE, SIDE), SIDE)
            result = scale * (COEF_LINEAR * panel[:, columns].astype(F32) + product(i, mixed))
            stage[turn, pl.ds(pl.multiple_of(b * SIDE, SIDE), SIDE)] = result.astype(BF16).T

        for side in range(2):
            out = outs[2 * turn + side]
            owner = 1 - a if side else a
            start = pl.multiple_of(owner * HEIGHT, 128)
            for j in range(4):
                columns = pl.ds(pl.multiple_of((j + c) * TILE, TILE), TILE)
                sends.append((stage.at[turn, pl.ds(start, HEIGHT), columns], out.at[pl.ds(j * HEIGHT, HEIGHT)]))
            columns = pl.ds(pl.multiple_of(4 * (1 - c) * TILE, TILE), TILE)
            shared = pl.ds(pl.multiple_of(start + 448 * c, 64), 448)
            sends.append((stage.at[turn, shared, columns], out.at[pl.ds(4 * HEIGHT, 448)]))
            for k in range(len(sends) - 5, len(sends)):
                sends[k] = pltpu.make_async_copy(*sends[k], out_sems.at[k])
                sends[k].start()
    for copy in sends:
        copy.wait()


def apply_poly(info, own, ends, swapped, turned):
    return pl.pallas_call(
        apply_kernel,
        in_specs=[SMEM] + [ANY] * 15,
        out_specs=[ANY] * 4,
        out_shape=[jax.ShapeDtypeStruct((BACK_ROWS, TILE), BF16)] * 4,
        scratch_shapes=[
            pltpu.VMEM((BLOCKS, 8 * SIDE, SIDE), BF16),
            pltpu.VMEM((BLOCKS, 6 * SIDE, SIDE), BF16),
            pltpu.VMEM((WIDE, AROUND), BF16),
            pltpu.VMEM((WIDE, AROUND), BF16),
            pltpu.VMEM((2, CHUNK, WIDE), BF16),
            pltpu.SemaphoreType.DMA((32,)),
            pltpu.SemaphoreType.DMA,
            pltpu.SemaphoreType.DMA((20,)),
        ],
        compiler_params=pltpu.CompilerParams(vmem_limit_bytes=58 * MIB),
        cost_estimate=cost(4 * ROWS * ROWS * WIDE, 3e7),
    )(info, *own, *ends, *swapped, turned)


def unpack_kernel(info, r0, r1, r2, r3, update):
    m, a = info[1], info[2]
    for s, got in enumerate((r0, r1, r2, r3)):
        core = 1 - m if s >= 2 else m
        side = 1 - a if s % 2 else a
        for j in range(4):
            start = pl.multiple_of((9 * side + j + 5 * core) * TILE, TILE)
            update[:, pl.ds(start, TILE)] = got[j * HEIGHT : (j + 1) * HEIGHT]
        start = pl.multiple_of((9 * side + 4) * TILE, TILE)
        rows = pl.ds(pl.multiple_of(448 * core, 64), 448)
        update[rows, pl.ds(start, TILE)] = got[4 * HEIGHT :]


def unpack(info, parts):
    return pl.pallas_call(
        unpack_kernel,
        in_specs=[SMEM] + [VMEM] * 4,
        out_specs=VMEM,
        out_shape=jax.ShapeDtypeStruct((HEIGHT, 2304), BF16),
        compiler_params=pltpu.CompilerParams(vmem_limit_bytes=32 * MIB),
        cost_estimate=cost(0, 8.3e6),
    )(info, *parts)


def on_device(grad_tiles, tile_ids, momentum):
    core, zm, zl, y = (lax.axis_index(name) for name in AXES[1:])
    info = jnp.stack([core, zm, zl, y]).astype(jnp.int32)
    tile_count = grad_tiles.shape[0]

    owners = tile_ids // 8 // 7 * 4 + tile_ids % 8 // 2
    places = tile_ids // 8 % 7 * 2 + tile_ids % 2
    matches = owners[:, None] == jnp.arange(16, dtype=jnp.int32)[None, :]
    slots = jnp.sum(jnp.where(matches, jnp.arange(tile_count, dtype=jnp.int32)[:, None], 0), axis=0)
    labels = jnp.sum(jnp.where(matches, places[:, None] + 1, 0), axis=0) - 1
    packed = pack(jnp.concatenate([slots, labels]), grad_tiles)
    arrived = lax.all_to_all(packed, PLANE, split_axis=0, concat_axis=0, tiled=True)

    got_labels = arrived[:, HALF, 0].astype(jnp.int32)
    found = got_labels[None, :] == jnp.arange(tile_count, dtype=jnp.int32)[:, None]
    sources = jnp.sum(jnp.where(found, jnp.arange(16, dtype=jnp.int32)[None, :], 0), axis=1)
    details = jnp.concatenate([sources, zl[None].astype(jnp.int32)])
    new_momentum, half0 = update_momentum(details, arrived, momentum, 0, None)
    new_momentum, half1 = update_momentum(details, arrived, momentum, 1, new_momentum)

    got0 = move(half0, lambda c, m, a, y: (m, c, a, y))
    got1 = move(half1, lambda c, m, a, y: (m, c, 1 - a, y))
    blocks = (got0, got1, swap(got0), swap(got1))

    far = gram_chunks(info, blocks, ((1, 2),), [chunk(BF16, size) for _, size in PARTS])
    far0, far1, far2 = up(far[0]), down(far[1]), across(far[2])
    terms = gram_chunks(info, blocks, ((1, 1), (1, 3), (0, 2)), [chunk(F32)] * 3)
    q1, q2, q3 = in_vmem(second_sums_kernel, [chunk()] * 3, *terms, far0, far1, far2)
    g1, g2, g3 = across(q1), down(q2), up(q3)
    later, _ = lax.optimization_barrier((blocks, q1))
    nearest, beside, below, center = gram_chunks(
        info, later, ((0, 1), (1, 0), (0, 3), (0, 0)), [chunk(F32), chunk(F32), chunk(), chunk(F32)]
    )
    near = down(below)
    v1, v2 = in_vmem(third_sums_kernel, [chunk()] * 2, nearest, beside, g1, g2, g3)
    w1, w2 = up(v1), across(v2)
    later, _ = lax.optimization_barrier((blocks, v1))
    turned = turned_panel(info, later)
    (mine,) = in_vmem(last_sums_kernel, [chunk()], center, w1, w2, near)

    low, high, pair = up(mine), down(mine), across(mine)
    a1, a2, a3 = across(high), up(pair), down(high)
    ends = tuple(
        send(x[row : row + size]) for send, x, (row, size) in zip((down, up, across), (a1, a2, a3), PARTS)
    )
    swapped = (
        swap(mine),
        swap(jnp.concatenate([low, high, pair])),
        swap(jnp.concatenate([a1, a2, a3])),
        swap(jnp.concatenate(ends)),
    )
    sent = apply_poly(info, (mine, low, high, pair, a1, a2, a3), ends, swapped, turned)

    parts = (
        move(sent[0], lambda c, m, a, y: (m, c, a, y)),
        move(sent[1], lambda c, m, a, y: (m, c, 1 - a, y)),
        move(sent[2], lambda c, m, a, y: (m, 1 - c, a, y)),
        move(sent[3], lambda c, m, a, y: (m, 1 - c, 1 - a, y)),
    )
    return new_momentum, unpack(info, parts)


def solution(mesh):
    fine = Mesh(mesh.devices.reshape(4, 2, 2, 2, 4), AXES)
    tall = P(("x", "core", "zm", "zl"), "y")
    return jax.shard_map(
        on_device,
        mesh=fine,
        in_specs=(P(AXES, None, None), P(AXES), tall),
        out_specs=(tall, tall),
        check_vma=False,
    )
```

```python
import math

import jax
import jax.numpy as jnp
from jax import lax
from jax.experimental import pallas as pl
from jax.experimental.pallas import tpu as pltpu
from jax.sharding import Mesh
from jax.sharding import PartitionSpec as P

ROWS = 3584
COLS = 9216
MOMENTUM_RATE = 0.95
COEF_LINEAR = 3.4445
COEF_CUBIC = -4.775
COEF_QUINTIC = 2.0315
EPSILON = 1e-06

HEIGHT = 896
HALF = 1152
TILE = 128
PART = 64
SENT = HALF // TILE * PART
LABEL = 16
SIDE = 256
BLOCKS = ROWS // SIDE
HALF_BLOCKS = BLOCKS // 2
CHUNK = HALF_BLOCKS * SIDE
PARTS = ((0, 608), (608, 592), (1200, 592))
WIDE = 640
AROUND = ROWS + CHUNK
BACK_ROWS = 4032

AXES = ("x", "core", "zm", "zl", "y")
PLANE = ("zm", "zl", "y")
BF16 = jnp.bfloat16
F32 = jnp.float32
MIB = 1 << 20
ANY = pl.BlockSpec(memory_space=pl.ANY)
HBM = pl.BlockSpec(memory_space=pltpu.HBM)
VMEM = pl.BlockSpec(memory_space=pltpu.VMEM)
SMEM = pl.BlockSpec(memory_space=pltpu.SMEM)


def cost(flops, size):
    return pl.CostEstimate(flops=int(flops), bytes_accessed=int(size), transcendentals=0)


def move(x, route):
    pairs = []
    for c in range(2):
        for m in range(2):
            for a in range(2):
                for y in range(4):
                    c2, m2, a2, y2 = route(c, m, a, y)
                    pairs.append((((c * 2 + m) * 2 + a) * 4 + y, ((c2 * 2 + m2) * 2 + a2) * 4 + y2 % 4))
    return lax.ppermute(x, AXES[1:], pairs)


def up(x):
    return move(x, lambda c, m, a, y: (c, m, a, y + 1))


def down(x):
    return move(x, lambda c, m, a, y: (c, m, a, y + 3))


def across(x):
    return move(x, lambda c, m, a, y: (c, m, 1 - a, y))


def swap(x):
    return move(x, lambda c, m, a, y: (1 - c, m, a, y))


def pack_kernel(details, tiles, upper, lower, held, first, second, sems, out_sems):
    load_all([(tiles.at[i], held.at[i]) for i in range(tiles.shape[0])], sems)

    def copies(o):
        return (
            pltpu.make_async_copy(first.at[o], upper.at[o], out_sems.at[0, o]),
            pltpu.make_async_copy(second.at[o], lower.at[o], out_sems.at[1, o]),
        )

    @pl.loop(0, upper.shape[0])
    def _(o):
        slot = details[o]
        for j in range(HALF // TILE):
            piece = held[slot, :, j * TILE : (j + 1) * TILE]
            first[o, j * PART : (j + 1) * PART, :] = piece[:PART]
            second[o, j * PART : (j + 1) * PART, :] = piece[PART:]
        place = jnp.full((LABEL, TILE), details[16 + o], jnp.int32)
        first[o, SENT:, :] = place.astype(F32).astype(BF16)
        for copy in copies(o):
            copy.start()

    @pl.loop(0, upper.shape[0])
    def _(o):
        for copy in copies(o):
            copy.wait()


def pack(details, tiles):
    n = details.shape[0] // 2
    shapes = [(n, SENT + LABEL, TILE), (n, SENT, TILE)]
    return pl.pallas_call(
        pack_kernel,
        in_specs=[SMEM, HBM],
        out_specs=[HBM] * 2,
        out_shape=[jax.ShapeDtypeStruct(shape, BF16) for shape in shapes],
        scratch_shapes=[pltpu.VMEM(tiles.shape, BF16)]
        + [pltpu.VMEM(shape, BF16) for shape in shapes]
        + [pltpu.SemaphoreType.DMA((tiles.shape[0],)), pltpu.SemaphoreType.DMA((2, n))],
        compiler_params=pltpu.CompilerParams(vmem_limit_bytes=32 * MIB),
        cost_estimate=cost(0, 4 * n * SENT * TILE * 2),
    )(details, tiles)


def momentum_kernel(part, info, arrived, momentum, *refs):
    new, half0, half1, tile, old, fresh, rounded, in_sems, out_sems = refs[-9:]
    n = HEIGHT // TILE

    def place(t, r):
        half = (t + info[14]) % 2
        columns = pl.ds(pl.multiple_of(half * HALF, TILE), HALF)
        return pl.ds(pl.multiple_of(r * TILE + part * PART, PART), PART), columns

    def reads(t, r):
        source = info[2 * r + (t + info[14]) % 2]
        i = t * n + r
        return (
            pltpu.make_async_copy(momentum.at[place(t, r)], old.at[i], in_sems.at[0, i]),
            pltpu.make_async_copy(arrived.at[source, 0:SENT], tile.at[i], in_sems.at[1, i]),
        )

    def writes(t, r):
        i = t * n + r
        out = (half0, half1)[t].at[r]
        return (
            pltpu.make_async_copy(fresh.at[i], new.at[place(t, r)], out_sems.at[0, i]),
            pltpu.make_async_copy(rounded.at[i], out, out_sems.at[1, i]),
        )

    for t in range(2):
        for r in range(n):
            for copy in reads(t, r):
                copy.start()
    for t in range(2):

        @pl.loop(0, n)
        def _(r):
            i = t * n + r
            for copy in reads(t, r):
                copy.wait()
            for j in range(HALF // TILE):
                columns = slice(j * TILE, (j + 1) * TILE)
                g = tile[i, j * PART : (j + 1) * PART, :].astype(F32)
                later = MOMENTUM_RATE * old[i, :, columns] + g
                fresh[i, :, columns] = later
                rounded[i, :, columns] = (g + MOMENTUM_RATE * later).astype(BF16)
            for copy in writes(t, r):
                copy.start()

    for t in range(2):

        @pl.loop(0, n)
        def _(r):
            for copy in writes(t, r):
                copy.wait()


def update_momentum(info, arrived, momentum, part, so_far):
    more = () if so_far is None else (so_far,)
    n = 2 * HEIGHT // TILE
    return pl.pallas_call(
        lambda *refs: momentum_kernel(part, *refs),
        in_specs=[SMEM] + [HBM] * (2 + len(more)),
        out_specs=[HBM] * 3,
        out_shape=[
            jax.ShapeDtypeStruct(momentum.shape, F32),
            jax.ShapeDtypeStruct((n // 2, PART, HALF), BF16),
            jax.ShapeDtypeStruct((n // 2, PART, HALF), BF16),
        ],
        scratch_shapes=[
            pltpu.VMEM((n, SENT, TILE), BF16),
            pltpu.VMEM((n, PART, HALF), F32),
            pltpu.VMEM((n, PART, HALF), F32),
            pltpu.VMEM((n, PART, HALF), BF16),
            pltpu.SemaphoreType.DMA((2, n)),
            pltpu.SemaphoreType.DMA((2, n)),
        ],
        input_output_aliases={3: 0} if more else {},
        compiler_params=pltpu.CompilerParams(vmem_limit_bytes=32 * MIB),
        cost_estimate=cost(0, HEIGHT * HALF * 12),
    )(info, arrived, momentum, *more)


def panel_copies(info, blocks, panel, columns=None):
    c, a = info[0], info[2]
    copies = []
    for i, block in enumerate(blocks):
        other, t, part = i // 4, i // 2 % 2, i % 2
        core = 1 - c if other else c
        z = 2 * core + (a + t) % 2
        src = block if columns is None else block.at[:, :, columns]
        copies.append((src, panel.at[pl.ds(z * (HEIGHT // TILE), HEIGHT // TILE), part]))
    return copies


def panel_shape(width):
    return pltpu.VMEM((ROWS // TILE, TILE // PART, PART, width), BF16)


def chip_at(info, flip, dy):
    a, y = info[2], info[3]
    return (1 - a if flip else a) * 4 + (y + dy) % 4


def load_all(copies, sems):
    copies = [pltpu.make_async_copy(src, dst, sems.at[i]) for i, (src, dst) in enumerate(copies)]
    for copy in copies:
        copy.start()
    for copy in copies:
        copy.wait()


def gram_kernel(dests, info, *refs):
    blocks, outs = refs[:8], refs[8:-2]
    panel, sems = refs[-2:]
    load_all(panel_copies(info, blocks, panel), sems)

    def term(b, d):
        left = panel[pl.ds(2 * b, 2)].reshape(SIDE, HALF)
        right = panel[pl.ds(2 * ((b + d) % BLOCKS), 2)].reshape(SIDE, HALF)
        return lax.dot_general(left, right, (((1,), (1,)), ((), ())), preferred_element_type=F32)

    base = HALF_BLOCKS * info[0]
    if len(dests) == 1:
        d = chip_at(info, *dests[0])
        for b in range(HALF_BLOCKS):
            block = term(base + b, d).astype(BF16)
            for out, (row, size) in zip(outs, PARTS):
                low, high = max(row, b * SIDE), min(row + size, (b + 1) * SIDE)
                if low < high:
                    out[low - row : high - row] = block[low - b * SIDE : high - b * SIDE]
    else:

        @pl.loop(0, HALF_BLOCKS)
        def _(b):
            for dest, out in zip(dests, outs):
                block = term(base + b, chip_at(info, *dest))
                out[pl.ds(pl.multiple_of(b * SIDE, SIDE), SIDE)] = block.astype(out.dtype)


def gram_chunks(info, blocks, dests, shapes):
    return pl.pallas_call(
        lambda *refs: gram_kernel(dests, *refs),
        in_specs=[SMEM] + [HBM] * 8,
        out_specs=[VMEM] * len(shapes),
        out_shape=shapes,
        scratch_shapes=[panel_shape(HALF), pltpu.SemaphoreType.DMA((8,))],
        compiler_params=pltpu.CompilerParams(vmem_limit_bytes=24 * MIB),
        cost_estimate=cost(len(dests) * 2 * CHUNK * SIDE * HALF, 8.3e6 + len(dests) * CHUNK * SIDE * 4),
    )(info, *blocks)


def chunk(dtype=BF16, rows=CHUNK):
    return jax.ShapeDtypeStruct((rows, SIDE), dtype)


def second_sums_kernel(p1, p2, p3, r1, r2, r3, q1, q2, q3):
    for own, got, out, (row, size) in zip((p1, p2, p3), (r1, r2, r3), (q1, q2, q3), PARTS):
        if row:
            out[:row] = own[:row].astype(BF16)
        out[row : row + size] = (own[row : row + size] + got[...].astype(F32)).astype(BF16)
        if row + size < CHUNK:
            out[row + size :] = own[row + size :].astype(BF16)


def third_sums_kernel(p1, p2, g1, g2, g3, v1, v2):
    v1[...] = (p1[...] + (g1[...].astype(F32) + g3[...].astype(F32))).astype(BF16)
    v2[...] = (p2[...] + g2[...].astype(F32)).astype(BF16)


def last_sums_kernel(p, v1, v2, v3, turned, out):
    total = p[...] + (v1[...].astype(F32) + v2[...].astype(F32) + v3[...].astype(F32))
    out[...] = total.astype(BF16)


def in_vmem(kernel, shapes, *args, after=()):
    size = sum(x.size * x.dtype.itemsize for x in args)
    return pl.pallas_call(
        kernel,
        in_specs=[VMEM] * len(args) + [ANY] * len(after),
        out_specs=[VMEM] * len(shapes),
        out_shape=shapes,
        compiler_params=pltpu.CompilerParams(vmem_limit_bytes=16 * MIB),
        cost_estimate=cost(0, size),
    )(*args, *after)


def turn_kernel(info, *refs):
    blocks, out, held, sems = refs[:8], refs[8], refs[9], refs[10]
    shift = pl.multiple_of(512 * info[0], TILE)
    load_all(panel_copies(info, blocks, held, pl.ds(shift, WIDE)), sems)
    for r in range(ROWS // TILE):
        out[:, r * TILE : (r + 1) * TILE] = held[r].reshape(TILE, WIDE).T
    out[:, ROWS:] = out[:, :CHUNK]


def turned_panel(info, blocks):
    return pl.pallas_call(
        turn_kernel,
        in_specs=[SMEM] + [HBM] * 8,
        out_specs=VMEM,
        out_shape=jax.ShapeDtypeStruct((WIDE, AROUND), BF16),
        scratch_shapes=[panel_shape(WIDE), pltpu.SemaphoreType.DMA((8,))],
        compiler_params=pltpu.CompilerParams(vmem_limit_bytes=24 * MIB),
        cost_estimate=cost(0, 1.2e7),
    )(info, *blocks)


SOURCES = ((0, 0), (0, 3), (0, 1), (1, 0), (1, 1), (1, 3), (0, 2), (1, 2))


def apply_kernel(info, *refs):
    own, ends, swapped = refs[:7], refs[7:10], refs[10:14]
    turned = refs[14]
    outs, rest_direct, rest_flipped, all_mixed, scales = refs[15:17], *refs[17:21]
    direct, flipped, panel, mixed, stage, sems, panel_sem, out_sems, keep_sems = refs[21:]
    c = info[0]
    panel_copy = pltpu.make_async_copy(turned, panel, panel_sem)
    panel_copy.start()
    pieces = [(c, ref, 0, rel) for ref, rel in zip(own, SOURCES)]
    pieces += [(1 - c, swapped[0], 0, SOURCES[0]), (1 - c, swapped[3], 0, SOURCES[7])]
    pieces += [(1 - c, swapped[1 + n // 3], n % 3 * CHUNK, SOURCES[1 + n]) for n in range(6)]
    for n, (core, ref, row, rel) in enumerate(pieces):
        d = chip_at(info, *rel)

        @pl.loop(0, HALF_BLOCKS)
        def _(b):
            i = (core * HALF_BLOCKS + b + d) % BLOCKS
            src = ref.at[pl.ds(pl.multiple_of(row + b * SIDE, SIDE), SIDE)]
            pltpu.make_async_copy(src, direct.at[i, pl.ds(pl.multiple_of((7 - d) * SIDE, SIDE), SIDE)], sems.at[n]).start()

    d = chip_at(info, *SOURCES[7])
    last = []
    for ref, (row, size) in zip(ends, PARTS):
        for b in range(HALF_BLOCKS):
            low, high = max(row, b * SIDE), min(row + size, (b + 1) * SIDE)
            if low < high:
                i = (c * HALF_BLOCKS + b + d) % BLOCKS
                start = pl.multiple_of((7 - d) * SIDE + low - b * SIDE, 16)
                src = ref.at[low - row : high - row]
                last.append(pltpu.make_async_copy(src, direct.at[i, pl.ds(start, high - low)], sems.at[15 + len(last)]))
    for copy in last:
        copy.start()
    for n in range(15):
        whole = direct.at[0:HALF_BLOCKS, 0:SIDE]
        pltpu.make_async_copy(whole, whole, sems.at[n]).wait()
    for copy in last:
        copy.wait()
    panel_copy.wait()

    total = jnp.zeros((), F32)
    on = lax.broadcasted_iota(jnp.int32, (SIDE, SIDE), 0) == lax.broadcasted_iota(jnp.int32, (SIDE, SIDE), 1)
    diagonal = jnp.zeros((SIDE, SIDE), F32)
    for i in range(BLOCKS):
        diagonal += direct[i, 7 * SIDE :, :].astype(F32)
    total = jnp.sum(jnp.where(on, diagonal, 0.0))
    total = jnp.full((1, SIDE), total, F32)
    factor = math.sqrt(ROWS) / (2.0 * (jnp.sqrt(total) + EPSILON))
    square = factor * factor

    def product(i, x):
        return gram_times(i, x, direct.at[i], flipped.at[i]) * square

    @pl.loop(0, BLOCKS)
    def _(i):
        for e in range(1, 7):
            far = (i + e) % BLOCKS
            flipped[i, (e - 1) * SIDE : e * SIDE, :] = direct[far, (7 - e) * SIDE : (8 - e) * SIDE, :].T
        columns = pl.ds(pl.multiple_of(i * SIDE, SIDE), SIDE)
        mix = COEF_CUBIC * panel[:, columns].astype(F32) + COEF_QUINTIC * product(i, panel)
        mix = mix.astype(BF16)
        mixed[:, columns] = mix

        @pl.when(i < HALF_BLOCKS)
        def _():
            mixed[:, pl.ds(pl.multiple_of(i * SIDE + ROWS, SIDE), SIDE)] = mix

    other = (1 - c) * HALF_BLOCKS
    scale = math.sqrt(COLS) * factor
    scales[...] = jnp.concatenate([scale] * 4 + [square] * 4)
    keeps = [
        pltpu.make_async_copy(direct.at[pl.ds(other, HALF_BLOCKS)], rest_direct, keep_sems.at[0]),
        pltpu.make_async_copy(flipped.at[pl.ds(other, HALF_BLOCKS)], rest_flipped, keep_sems.at[1]),
        pltpu.make_async_copy(mixed, all_mixed, keep_sems.at[2]),
    ]
    for copy in keeps:
        copy.start()

    @pl.loop(0, HALF_BLOCKS)
    def _(b):
        i = c * HALF_BLOCKS + b
        columns = pl.ds(pl.multiple_of(i * SIDE, SIDE), SIDE)
        result = scale * (COEF_LINEAR * panel[:, columns].astype(F32) + product(i, mixed))
        stage[pl.ds(pl.multiple_of(b * SIDE, SIDE), SIDE)] = result.astype(BF16).T

    send_back(info, stage, outs, out_sems)
    for copy in keeps:
        copy.wait()


def gram_times(i, x, direct, flipped):
    first = pl.ds(pl.multiple_of((i + 7) % BLOCKS * SIDE, SIDE), 8 * SIDE)
    rest = pl.ds(pl.multiple_of((i + 1) % BLOCKS * SIDE, SIDE), 6 * SIDE)
    result = jnp.dot(x[:, first], direct[...], preferred_element_type=F32)
    return result + jnp.dot(x[:, rest], flipped[...], preferred_element_type=F32)


def send_back(info, stage, outs, sems):
    c, a = info[0], info[2]
    sends = []
    for side, out in enumerate(outs):
        owner = 1 - a if side else a
        start = pl.multiple_of(owner * HEIGHT, 128)
        for j in range(4):
            columns = pl.ds(pl.multiple_of((j + c) * TILE, TILE), TILE)
            sends.append((stage.at[pl.ds(start, HEIGHT), columns], out.at[pl.ds(j * HEIGHT, HEIGHT)]))
        columns = pl.ds(pl.multiple_of(4 * (1 - c) * TILE, TILE), TILE)
        shared = pl.ds(pl.multiple_of(start + 448 * c, 64), 448)
        sends.append((stage.at[shared, columns], out.at[pl.ds(4 * HEIGHT, 448)]))
    load_all(sends, sems)


def rest_kernel(info, direct, flipped, panel, all_mixed, scales, out0, out1, mixed, stage, sems):
    b = pl.program_id(0)

    @pl.when(b == 0)
    def _():
        load_all([(all_mixed, mixed)], sems)

    i = (1 - info[0]) * HALF_BLOCKS + b
    product = gram_times(i, mixed, direct.at[0], flipped.at[0]) * scales[4:5]
    result = scales[0:1] * (COEF_LINEAR * panel[...].astype(F32) + product)
    stage[pl.ds(pl.multiple_of(b * SIDE, SIDE), SIDE)] = result.astype(BF16).T

    @pl.when(b == HALF_BLOCKS - 1)
    def _():
        send_back(info, stage, (out0, out1), sems)


def apply_rest(info, direct, flipped, mixed, scales, turned):
    return pl.pallas_call(
        rest_kernel,
        grid_spec=pltpu.PrefetchScalarGridSpec(
            num_scalar_prefetch=1,
            grid=(HALF_BLOCKS,),
            in_specs=[
                pl.BlockSpec((1, 8 * SIDE, SIDE), lambda b, s: (b, 0, 0)),
                pl.BlockSpec((1, 6 * SIDE, SIDE), lambda b, s: (b, 0, 0)),
                pl.BlockSpec((WIDE, SIDE), lambda b, s: (0, (1 - s[0]) * HALF_BLOCKS + b)),
                HBM,
                VMEM,
            ],
            out_specs=[HBM] * 2,
            scratch_shapes=[pltpu.VMEM((WIDE, AROUND), BF16), pltpu.VMEM((CHUNK, WIDE), BF16), pltpu.SemaphoreType.DMA((10,))],
        ),
        out_shape=[jax.ShapeDtypeStruct((BACK_ROWS, TILE), BF16)] * 2,
        compiler_params=pltpu.CompilerParams(vmem_limit_bytes=40 * MIB),
        cost_estimate=cost(ROWS * ROWS * WIDE, 2e7),
    )(info, direct, flipped, turned, mixed, scales)


def apply_poly(info, own, ends, swapped, turned):
    return pl.pallas_call(
        apply_kernel,
        in_specs=[SMEM] + [HBM] * 15,
        out_specs=[HBM] * 5 + [VMEM],
        out_shape=[jax.ShapeDtypeStruct((BACK_ROWS, TILE), BF16)] * 2
        + [
            jax.ShapeDtypeStruct((HALF_BLOCKS, 8 * SIDE, SIDE), BF16),
            jax.ShapeDtypeStruct((HALF_BLOCKS, 6 * SIDE, SIDE), BF16),
            jax.ShapeDtypeStruct((WIDE, AROUND), BF16),
            jax.ShapeDtypeStruct((8, SIDE), F32),
        ],
        scratch_shapes=[
            pltpu.VMEM((BLOCKS, 8 * SIDE, SIDE), BF16),
            pltpu.VMEM((BLOCKS, 6 * SIDE, SIDE), BF16),
            pltpu.VMEM((WIDE, AROUND), BF16),
            pltpu.VMEM((WIDE, AROUND), BF16),
            pltpu.VMEM((CHUNK, WIDE), BF16),
            pltpu.SemaphoreType.DMA((32,)),
            pltpu.SemaphoreType.DMA,
            pltpu.SemaphoreType.DMA((10,)),
            pltpu.SemaphoreType.DMA((3,)),
        ],
        compiler_params=pltpu.CompilerParams(vmem_limit_bytes=58 * MIB),
        cost_estimate=cost(3 * ROWS * ROWS * WIDE, 4e7),
    )(info, *own, *ends, *swapped, turned)


def unpack_kernel(info, r0, r1, r2, r3, update):
    m, a = info[1], info[2]
    for s, got in enumerate((r0, r1, r2, r3)):
        core = 1 - m if s >= 2 else m
        side = 1 - a if s % 2 else a
        for j in range(4):
            start = pl.multiple_of((9 * side + j + 5 * core) * TILE, TILE)
            update[:, pl.ds(start, TILE)] = got[j * HEIGHT : (j + 1) * HEIGHT]
        start = pl.multiple_of((9 * side + 4) * TILE, TILE)
        rows = pl.ds(pl.multiple_of(448 * core, 64), 448)
        update[rows, pl.ds(start, TILE)] = got[4 * HEIGHT :]


def unpack(info, parts):
    return pl.pallas_call(
        unpack_kernel,
        in_specs=[SMEM] + [VMEM] * 4,
        out_specs=VMEM,
        out_shape=jax.ShapeDtypeStruct((HEIGHT, 2304), BF16),
        compiler_params=pltpu.CompilerParams(vmem_limit_bytes=32 * MIB),
        cost_estimate=cost(0, 8.3e6),
    )(info, *parts)


def on_device(grad_tiles, tile_ids, momentum):
    core, zm, zl, y = (lax.axis_index(name) for name in AXES[1:])
    info = jnp.stack([core, zm, zl, y]).astype(jnp.int32)
    tile_count = grad_tiles.shape[0]

    owners = tile_ids // 8 // 7 * 4 + tile_ids % 8 // 2
    places = tile_ids // 8 % 7 * 2 + tile_ids % 2
    matches = owners[:, None] == jnp.arange(16, dtype=jnp.int32)[None, :]
    slots = jnp.sum(jnp.where(matches, jnp.arange(tile_count, dtype=jnp.int32)[:, None], 0), axis=0)
    labels = jnp.sum(jnp.where(matches, places[:, None] + 1, 0), axis=0) - 1
    upper, lower = pack(jnp.concatenate([slots, labels]), grad_tiles)
    upper = lax.all_to_all(upper, PLANE, split_axis=0, concat_axis=0, tiled=True)
    lower, _ = lax.optimization_barrier((lower, upper))
    lower = lax.all_to_all(lower, PLANE, split_axis=0, concat_axis=0, tiled=True)

    got_labels = upper[:, SENT, 0].astype(jnp.int32)
    found = got_labels[None, :] == jnp.arange(tile_count, dtype=jnp.int32)[:, None]
    sources = jnp.sum(jnp.where(found, jnp.arange(16, dtype=jnp.int32)[None, :], 0), axis=1)
    details = jnp.concatenate([sources, zl[None].astype(jnp.int32)])
    new_momentum, *halves0 = update_momentum(details, upper, momentum, 0, None)
    new_momentum, *halves1 = update_momentum(details, lower, momentum, 1, new_momentum)

    def to_panel(halves):
        half0, half1 = halves
        return (
            move(half0, lambda c, m, a, y: (m, c, a, y)),
            move(half1, lambda c, m, a, y: (m, c, 1 - a, y)),
        )

    got0, got1 = to_panel(halves0), to_panel(halves1)
    blocks = (got0[0], got1[0], got0[1], got1[1])
    blocks += tuple(swap(x) for x in blocks)

    far = gram_chunks(info, blocks, ((1, 2),), [chunk(BF16, size) for _, size in PARTS])
    far0, far1, far2 = up(far[0]), down(far[1]), across(far[2])
    terms = gram_chunks(info, blocks, ((1, 1), (1, 3), (0, 2)), [chunk(F32)] * 3)
    q1, q2, q3 = in_vmem(second_sums_kernel, [chunk()] * 3, *terms, far0, far1, far2)
    g1, g2, g3 = across(q1), down(q2), up(q3)
    later, _ = lax.optimization_barrier((blocks, q1))
    nearest, beside, below, center = gram_chunks(
        info, later, ((0, 1), (1, 0), (0, 3), (0, 0)), [chunk(F32), chunk(F32), chunk(), chunk(F32)]
    )
    near = down(below)
    v1, v2 = in_vmem(third_sums_kernel, [chunk()] * 2, nearest, beside, g1, g2, g3)
    w1, w2 = up(v1), across(v2)
    later, _ = lax.optimization_barrier((blocks, v1))
    turned = turned_panel(info, later)
    (mine,) = in_vmem(last_sums_kernel, [chunk()], center, w1, w2, near, after=(turned,))

    low, high, pair = up(mine), down(mine), across(mine)
    a1, a2, a3 = across(high), up(pair), down(high)
    ends = tuple(
        send(x[row : row + size]) for send, x, (row, size) in zip((down, up, across), (a1, a2, a3), PARTS)
    )
    swapped = (
        swap(mine),
        swap(jnp.concatenate([low, high, pair])),
        swap(jnp.concatenate([a1, a2, a3])),
        swap(jnp.concatenate(ends)),
    )
    *sent, direct, flipped, mixed, scales = apply_poly(info, (mine, low, high, pair, a1, a2, a3), ends, swapped, turned)
    sent += apply_rest(info, direct, flipped, mixed, scales, turned)

    parts = (
        move(sent[0], lambda c, m, a, y: (m, c, a, y)),
        move(sent[1], lambda c, m, a, y: (m, c, 1 - a, y)),
        move(sent[2], lambda c, m, a, y: (m, 1 - c, a, y)),
        move(sent[3], lambda c, m, a, y: (m, 1 - c, 1 - a, y)),
    )
    return new_momentum, unpack(info, parts)


def solution(mesh):
    fine = Mesh(mesh.devices.reshape(4, 2, 2, 2, 4), AXES)
    tall = P(("x", "core", "zm", "zl"), "y")
    return jax.shard_map(
        on_device,
        mesh=fine,
        in_specs=(P(AXES, None, None), P(AXES), tall),
        out_specs=(tall, tall),
        check_vma=False,
    )
```

```python
import math

import jax
import jax.numpy as jnp
from jax import lax
from jax.experimental import pallas as pl
from jax.experimental.pallas import tpu as pltpu
from jax.sharding import Mesh
from jax.sharding import PartitionSpec as P

ROWS = 3584
COLS = 9216
MOMENTUM_RATE = 0.95
COEF_LINEAR = 3.4445
COEF_CUBIC = -4.775
COEF_QUINTIC = 2.0315
EPSILON = 1e-06

HEIGHT = 896
HALF = 1152
TILE = 128
SPLIT = ((0, 80), (80, 48))
LABEL = 16
SIDE = 256
BLOCKS = ROWS // SIDE
HALF_BLOCKS = BLOCKS // 2
CHUNK = HALF_BLOCKS * SIDE
PARTS = ((0, 608), (608, 592), (1200, 592))
WIDE = 640
SHARE = 576
AROUND = ROWS + CHUNK
BACK_ROWS = 4032

AXES = ("x", "core", "zm", "zl", "y")
PLANE = ("zm", "zl", "y")
BF16 = jnp.bfloat16
F32 = jnp.float32
MIB = 1 << 20
ANY = pl.BlockSpec(memory_space=pl.ANY)
HBM = pl.BlockSpec(memory_space=pltpu.HBM)
VMEM = pl.BlockSpec(memory_space=pltpu.VMEM)
SMEM = pl.BlockSpec(memory_space=pltpu.SMEM)


def cost(flops, size):
    return pl.CostEstimate(flops=int(flops), bytes_accessed=int(size), transcendentals=0)


def move(x, route):
    pairs = []
    for c in range(2):
        for m in range(2):
            for a in range(2):
                for y in range(4):
                    c2, m2, a2, y2 = route(c, m, a, y)
                    pairs.append((((c * 2 + m) * 2 + a) * 4 + y, ((c2 * 2 + m2) * 2 + a2) * 4 + y2 % 4))
    return lax.ppermute(x, AXES[1:], pairs)


def up(x):
    return move(x, lambda c, m, a, y: (c, m, a, y + 1))


def down(x):
    return move(x, lambda c, m, a, y: (c, m, a, y + 3))


def across(x):
    return move(x, lambda c, m, a, y: (c, m, 1 - a, y))


def swap(x):
    return move(x, lambda c, m, a, y: (1 - c, m, a, y))


def pack_kernel(details, tiles, upper, lower, held, first, second, sems, out_sems):
    load_all([(tiles.at[i], held.at[i]) for i in range(tiles.shape[0])], sems)

    def copies(o):
        return (
            pltpu.make_async_copy(first.at[o], upper.at[o], out_sems.at[0, o]),
            pltpu.make_async_copy(second.at[o], lower.at[o], out_sems.at[1, o]),
        )

    @pl.loop(0, upper.shape[0])
    def _(o):
        slot = details[o]
        for j in range(HALF // TILE):
            piece = held[slot, :, j * TILE : (j + 1) * TILE]
            for (row, size), out in zip(SPLIT, (first, second)):
                out[o, j * size : (j + 1) * size, :] = piece[row : row + size]
        place = jnp.full((LABEL, TILE), details[16 + o], jnp.int32)
        first[o, first.shape[1] - LABEL :, :] = place.astype(F32).astype(BF16)
        for copy in copies(o):
            copy.start()

    @pl.loop(0, upper.shape[0])
    def _(o):
        for copy in copies(o):
            copy.wait()


def pack(details, tiles):
    n = details.shape[0] // 2
    rows = [HALF // TILE * size for _, size in SPLIT]
    shapes = [(n, rows[0] + LABEL, TILE), (n, rows[1], TILE)]
    return pl.pallas_call(
        pack_kernel,
        in_specs=[SMEM, HBM],
        out_specs=[HBM] * 2,
        out_shape=[jax.ShapeDtypeStruct(shape, BF16) for shape in shapes],
        scratch_shapes=[pltpu.VMEM(tiles.shape, BF16)]
        + [pltpu.VMEM(shape, BF16) for shape in shapes]
        + [pltpu.SemaphoreType.DMA((tiles.shape[0],)), pltpu.SemaphoreType.DMA((2, n))],
        compiler_params=pltpu.CompilerParams(vmem_limit_bytes=62 * MIB),
        cost_estimate=cost(0, 4 * tiles.size),
    )(details, tiles)


def momentum_kernel(part, info, arrived, momentum, *refs):
    new, half0, half1, tile, old, fresh, rounded, in_sems, out_sems = refs[-9:]
    n = HEIGHT // TILE
    row, size = SPLIT[part]

    def place(t, r):
        half = (t + info[14]) % 2
        columns = pl.ds(pl.multiple_of(half * HALF, TILE), HALF)
        return pl.ds(pl.multiple_of(r * TILE + row, 16), size), columns

    def reads(t, r):
        source = info[2 * r + (t + info[14]) % 2]
        i = t * n + r
        return (
            pltpu.make_async_copy(momentum.at[place(t, r)], old.at[i], in_sems.at[0, i]),
            pltpu.make_async_copy(arrived.at[source, 0 : HALF // TILE * size], tile.at[i], in_sems.at[1, i]),
        )

    def writes(t, r):
        i = t * n + r
        out = (half0, half1)[t].at[r]
        return (
            pltpu.make_async_copy(fresh.at[i], new.at[place(t, r)], out_sems.at[0, i]),
            pltpu.make_async_copy(rounded.at[i], out, out_sems.at[1, i]),
        )

    for t in range(2):
        for r in range(n):
            for copy in reads(t, r):
                copy.start()
    for t in range(2):

        @pl.loop(0, n)
        def _(r):
            i = t * n + r
            for copy in reads(t, r):
                copy.wait()
            for j in range(HALF // TILE):
                columns = slice(j * TILE, (j + 1) * TILE)
                g = tile[i, j * size : (j + 1) * size, :].astype(F32)
                later = MOMENTUM_RATE * old[i, :, columns] + g
                fresh[i, :, columns] = later
                rounded[i, :, columns] = (g + MOMENTUM_RATE * later).astype(BF16)
            for copy in writes(t, r):
                copy.start()

    for t in range(2):

        @pl.loop(0, n)
        def _(r):
            for copy in writes(t, r):
                copy.wait()


def update_momentum(info, arrived, momentum, part, so_far):
    more = () if so_far is None else (so_far,)
    n = 2 * HEIGHT // TILE
    size = SPLIT[part][1]
    return pl.pallas_call(
        lambda *refs: momentum_kernel(part, *refs),
        in_specs=[SMEM] + [HBM] * (2 + len(more)),
        out_specs=[HBM] * 3,
        out_shape=[
            jax.ShapeDtypeStruct(momentum.shape, F32),
            jax.ShapeDtypeStruct((n // 2, size, HALF), BF16),
            jax.ShapeDtypeStruct((n // 2, size, HALF), BF16),
        ],
        scratch_shapes=[
            pltpu.VMEM((n, HALF // TILE * size, TILE), BF16),
            pltpu.VMEM((n, size, HALF), F32),
            pltpu.VMEM((n, size, HALF), F32),
            pltpu.VMEM((n, size, HALF), BF16),
            pltpu.SemaphoreType.DMA((2, n)),
            pltpu.SemaphoreType.DMA((2, n)),
        ],
        input_output_aliases={3: 0} if more else {},
        compiler_params=pltpu.CompilerParams(vmem_limit_bytes=62 * MIB),
        cost_estimate=cost(0, HEIGHT * HALF * 12),
    )(info, arrived, momentum, *more)


def panel_copies(info, blocks, panel, columns=None):
    c, a = info[0], info[2]
    copies = []
    for i, block in enumerate(blocks):
        other, t, part = i // 4, i // 2 % 2, i % 2
        core = 1 - c if other else c
        z = 2 * core + (a + t) % 2
        src = block if columns is None else block.at[:, :, columns]
        row, size = SPLIT[part]
        rows = pl.ds(z * (HEIGHT // TILE), HEIGHT // TILE)
        copies.append((src, panel.at[rows, row : row + size]))
    return copies


def panel_shape(width):
    return pltpu.VMEM((ROWS // TILE, TILE, width), BF16)


def chip_at(info, flip, dy):
    a, y = info[2], info[3]
    return (1 - a if flip else a) * 4 + (y + dy) % 4


def load_all(copies, sems):
    copies = [pltpu.make_async_copy(src, dst, sems.at[i]) for i, (src, dst) in enumerate(copies)]
    for copy in copies:
        copy.start()
    for copy in copies:
        copy.wait()


def gram_kernel(dests, info, *refs):
    blocks, outs = refs[:8], refs[8:-2]
    panel, sems = refs[-2:]
    load_all(panel_copies(info, blocks, panel), sems)

    def term(b, d):
        left = panel[pl.ds(2 * b, 2)].reshape(SIDE, HALF)
        right = panel[pl.ds(2 * ((b + d) % BLOCKS), 2)].reshape(SIDE, HALF)
        return lax.dot_general(left, right, (((1,), (1,)), ((), ())), preferred_element_type=F32)

    base = HALF_BLOCKS * info[0]
    if len(dests) == 1:
        d = chip_at(info, *dests[0])
        for b in range(HALF_BLOCKS):
            block = term(base + b, d).astype(BF16)
            for out, (row, size) in zip(outs, PARTS):
                low, high = max(row, b * SIDE), min(row + size, (b + 1) * SIDE)
                if low < high:
                    out[low - row : high - row] = block[low - b * SIDE : high - b * SIDE]
    else:

        @pl.loop(0, HALF_BLOCKS)
        def _(b):
            for dest, out in zip(dests, outs):
                block = term(base + b, chip_at(info, *dest))
                out[pl.ds(pl.multiple_of(b * SIDE, SIDE), SIDE)] = block.astype(out.dtype)


def gram_chunks(info, blocks, dests, shapes):
    return pl.pallas_call(
        lambda *refs: gram_kernel(dests, *refs),
        in_specs=[SMEM] + [HBM] * 8,
        out_specs=[VMEM] * len(shapes),
        out_shape=shapes,
        scratch_shapes=[panel_shape(HALF), pltpu.SemaphoreType.DMA((8,))],
        compiler_params=pltpu.CompilerParams(vmem_limit_bytes=24 * MIB),
        cost_estimate=cost(len(dests) * 2 * CHUNK * SIDE * HALF, 8.3e6 + len(dests) * CHUNK * SIDE * 4),
    )(info, *blocks)


def chunk(dtype=BF16, rows=CHUNK):
    return jax.ShapeDtypeStruct((rows, SIDE), dtype)


def second_sums_kernel(p1, p2, p3, r1, r2, r3, q1, q2, q3):
    for own, got, out, (row, size) in zip((p1, p2, p3), (r1, r2, r3), (q1, q2, q3), PARTS):
        if row:
            out[:row] = own[:row].astype(BF16)
        out[row : row + size] = (own[row : row + size] + got[...].astype(F32)).astype(BF16)
        if row + size < CHUNK:
            out[row + size :] = own[row + size :].astype(BF16)


def third_sums_kernel(p1, p2, g1, g2, g3, v1, v2):
    v1[...] = (p1[...] + (g1[...].astype(F32) + g3[...].astype(F32))).astype(BF16)
    v2[...] = (p2[...] + g2[...].astype(F32)).astype(BF16)


def last_sums_kernel(p, v1, v2, v3, turned, out):
    total = p[...] + (v1[...].astype(F32) + v2[...].astype(F32) + v3[...].astype(F32))
    out[...] = total.astype(BF16)


def in_vmem(kernel, shapes, *args, after=()):
    size = sum(x.size * x.dtype.itemsize for x in args)
    return pl.pallas_call(
        kernel,
        in_specs=[VMEM] * len(args) + [ANY] * len(after),
        out_specs=[VMEM] * len(shapes),
        out_shape=shapes,
        compiler_params=pltpu.CompilerParams(vmem_limit_bytes=16 * MIB),
        cost_estimate=cost(0, size),
    )(*args, *after)


def turn_kernel(info, *refs):
    blocks, out, held, flat, sems = refs[:8], *refs[8:]
    c = info[0]
    shift = pl.multiple_of(512 * c, TILE)
    load_all(panel_copies(info, blocks, held, pl.ds(shift, WIDE)), sems)
    for r in range(ROWS // TILE):
        flat[:, r * TILE : (r + 1) * TILE] = held[r].T
    out[:512, :ROWS] = flat[pl.ds(pl.multiple_of(128 * c, 64), 512), :]
    out[512:, :ROWS] = flat[pl.ds(pl.multiple_of(512 - 448 * c, 64), 64), :]
    out[:, ROWS:] = out[:, :CHUNK]


def turned_panel(info, blocks):
    return pl.pallas_call(
        turn_kernel,
        in_specs=[SMEM] + [HBM] * 8,
        out_specs=VMEM,
        out_shape=jax.ShapeDtypeStruct((SHARE, AROUND), BF16),
        scratch_shapes=[panel_shape(WIDE), pltpu.VMEM((WIDE, ROWS), BF16), pltpu.SemaphoreType.DMA((8,))],
        compiler_params=pltpu.CompilerParams(vmem_limit_bytes=24 * MIB),
        cost_estimate=cost(0, 1.2e7),
    )(info, *blocks)


SOURCES = ((0, 0), (0, 3), (0, 1), (1, 0), (1, 1), (1, 3), (0, 2), (1, 2))


def apply_kernel(info, *refs):
    own, ends, swapped = refs[:7], refs[7:10], refs[10:14]
    turned = refs[14]
    outs, rest_direct, rest_flipped, all_mixed, scales = refs[15:17], *refs[17:21]
    direct, flipped, panel, mixed, stage, extra, sems, panel_sem, out_sems, keep_sems = refs[21:]
    c = info[0]
    panel_copy = pltpu.make_async_copy(turned, panel, panel_sem)
    panel_copy.start()
    pieces = [(c, ref, 0, rel) for ref, rel in zip(own, SOURCES)]
    pieces += [(1 - c, swapped[0], 0, SOURCES[0]), (1 - c, swapped[3], 0, SOURCES[7])]
    pieces += [(1 - c, swapped[1 + n // 3], n % 3 * CHUNK, SOURCES[1 + n]) for n in range(6)]
    for n, (core, ref, row, rel) in enumerate(pieces):
        d = chip_at(info, *rel)

        @pl.loop(0, HALF_BLOCKS)
        def _(b):
            i = (core * HALF_BLOCKS + b + d) % BLOCKS
            src = ref.at[pl.ds(pl.multiple_of(row + b * SIDE, SIDE), SIDE)]
            pltpu.make_async_copy(src, direct.at[i, pl.ds(pl.multiple_of((7 - d) * SIDE, SIDE), SIDE)], sems.at[n]).start()

    d = chip_at(info, *SOURCES[7])
    last = []
    for ref, (row, size) in zip(ends, PARTS):
        for b in range(HALF_BLOCKS):
            low, high = max(row, b * SIDE), min(row + size, (b + 1) * SIDE)
            if low < high:
                i = (c * HALF_BLOCKS + b + d) % BLOCKS
                start = pl.multiple_of((7 - d) * SIDE + low - b * SIDE, 16)
                src = ref.at[low - row : high - row]
                last.append(pltpu.make_async_copy(src, direct.at[i, pl.ds(start, high - low)], sems.at[15 + len(last)]))
    for copy in last:
        copy.start()
    for n in range(15):
        whole = direct.at[0:HALF_BLOCKS, 0:SIDE]
        pltpu.make_async_copy(whole, whole, sems.at[n]).wait()
    for copy in last:
        copy.wait()
    panel_copy.wait()

    total = jnp.zeros((), F32)
    on = lax.broadcasted_iota(jnp.int32, (SIDE, SIDE), 0) == lax.broadcasted_iota(jnp.int32, (SIDE, SIDE), 1)
    diagonal = jnp.zeros((SIDE, SIDE), F32)
    for i in range(BLOCKS):
        diagonal += direct[i, 7 * SIDE :, :].astype(F32)
    total = jnp.sum(jnp.where(on, diagonal, 0.0))
    total = jnp.full((1, SIDE), total, F32)
    factor = math.sqrt(ROWS) / (2.0 * (jnp.sqrt(total) + EPSILON))
    square = factor * factor

    def product(i, x):
        return gram_times(i, x, direct.at[i], flipped.at[i]) * square

    @pl.loop(0, BLOCKS)
    def _(i):
        for e in range(1, 7):
            far = (i + e) % BLOCKS
            flipped[i, (e - 1) * SIDE : e * SIDE, :] = direct[far, (7 - e) * SIDE : (8 - e) * SIDE, :].T
        columns = pl.ds(pl.multiple_of(i * SIDE, SIDE), SIDE)
        mix = COEF_CUBIC * panel[:, columns].astype(F32) + COEF_QUINTIC * product(i, panel)
        mix = mix.astype(BF16)
        mixed[:, columns] = mix

        @pl.when(i < HALF_BLOCKS)
        def _():
            mixed[:, pl.ds(pl.multiple_of(i * SIDE + ROWS, SIDE), SIDE)] = mix

    other = (1 - c) * HALF_BLOCKS
    scale = math.sqrt(COLS) * factor
    scales[...] = jnp.concatenate([scale] * 4 + [square] * 4)
    keeps = [
        pltpu.make_async_copy(direct.at[pl.ds(other, HALF_BLOCKS)], rest_direct, keep_sems.at[0]),
        pltpu.make_async_copy(flipped.at[pl.ds(other, HALF_BLOCKS)], rest_flipped, keep_sems.at[1]),
        pltpu.make_async_copy(mixed, all_mixed, keep_sems.at[2]),
    ]
    for copy in keeps:
        copy.start()

    @pl.loop(0, HALF_BLOCKS)
    def _(b):
        i = c * HALF_BLOCKS + b
        columns = pl.ds(pl.multiple_of(i * SIDE, SIDE), SIDE)
        result = scale * (COEF_LINEAR * panel[:, columns].astype(F32) + product(i, mixed))
        stage[pl.ds(pl.multiple_of(b * SIDE, SIDE), SIDE)] = result.astype(BF16).T

    send_back(info, stage, extra, outs, out_sems)
    for copy in keeps:
        copy.wait()


def gram_times(i, x, direct, flipped):
    first = pl.ds(pl.multiple_of((i + 7) % BLOCKS * SIDE, SIDE), 8 * SIDE)
    rest = pl.ds(pl.multiple_of((i + 1) % BLOCKS * SIDE, SIDE), 6 * SIDE)
    result = jnp.dot(x[:, first], direct[...], preferred_element_type=F32)
    return result + jnp.dot(x[:, rest], flipped[...], preferred_element_type=F32)


def send_back(info, stage, extra, outs, sems):
    a = info[2]
    sends = []
    for side, out in enumerate(outs):
        owner = 1 - a if side else a
        start = pl.multiple_of(owner * HEIGHT, 128)
        for j in range(4):
            rows = pl.ds(start, HEIGHT)
            sends.append((stage.at[rows, j * TILE : (j + 1) * TILE], out.at[pl.ds(j * HEIGHT, HEIGHT)]))
        halves = [stage[pl.ds(pl.multiple_of(start + row, 64), 448), 512:] for row in (0, 448)]
        extra[side] = jnp.concatenate(halves, axis=1)
        sends.append((extra.at[side], out.at[pl.ds(4 * HEIGHT, 448)]))
    load_all(sends, sems)


def rest_kernel(info, direct, flipped, panel, all_mixed, scales, out0, out1, mixed, stage, extra, sems):
    b = pl.program_id(0)

    @pl.when(b == 0)
    def _():
        load_all([(all_mixed, mixed)], sems)

    i = (1 - info[0]) * HALF_BLOCKS + b
    product = gram_times(i, mixed, direct.at[0], flipped.at[0]) * scales[4:5]
    result = scales[0:1] * (COEF_LINEAR * panel[...].astype(F32) + product)
    stage[pl.ds(pl.multiple_of(b * SIDE, SIDE), SIDE)] = result.astype(BF16).T

    @pl.when(b == HALF_BLOCKS - 1)
    def _():
        send_back(info, stage, extra, (out0, out1), sems)


def apply_rest(info, direct, flipped, mixed, scales, turned):
    return pl.pallas_call(
        rest_kernel,
        grid_spec=pltpu.PrefetchScalarGridSpec(
            num_scalar_prefetch=1,
            grid=(HALF_BLOCKS,),
            in_specs=[
                pl.BlockSpec((1, 8 * SIDE, SIDE), lambda b, s: (b, 0, 0)),
                pl.BlockSpec((1, 6 * SIDE, SIDE), lambda b, s: (b, 0, 0)),
                pl.BlockSpec((SHARE, SIDE), lambda b, s: (0, (1 - s[0]) * HALF_BLOCKS + b)),
                HBM,
                VMEM,
            ],
            out_specs=[HBM] * 2,
            scratch_shapes=[
                pltpu.VMEM((SHARE, AROUND), BF16),
                pltpu.VMEM((CHUNK, SHARE), BF16),
                pltpu.VMEM((2, 448, TILE), BF16),
                pltpu.SemaphoreType.DMA((10,)),
            ],
        ),
        out_shape=[jax.ShapeDtypeStruct((BACK_ROWS, TILE), BF16)] * 2,
        compiler_params=pltpu.CompilerParams(vmem_limit_bytes=62 * MIB),
        cost_estimate=cost(ROWS * ROWS * SHARE, 2e7),
    )(info, direct, flipped, turned, mixed, scales)


def apply_poly(info, own, ends, swapped, turned):
    return pl.pallas_call(
        apply_kernel,
        in_specs=[SMEM] + [HBM] * 15,
        out_specs=[HBM] * 5 + [VMEM],
        out_shape=[jax.ShapeDtypeStruct((BACK_ROWS, TILE), BF16)] * 2
        + [
            jax.ShapeDtypeStruct((HALF_BLOCKS, 8 * SIDE, SIDE), BF16),
            jax.ShapeDtypeStruct((HALF_BLOCKS, 6 * SIDE, SIDE), BF16),
            jax.ShapeDtypeStruct((SHARE, AROUND), BF16),
            jax.ShapeDtypeStruct((8, SIDE), F32),
        ],
        scratch_shapes=[
            pltpu.VMEM((BLOCKS, 8 * SIDE, SIDE), BF16),
            pltpu.VMEM((BLOCKS, 6 * SIDE, SIDE), BF16),
            pltpu.VMEM((SHARE, AROUND), BF16),
            pltpu.VMEM((SHARE, AROUND), BF16),
            pltpu.VMEM((CHUNK, SHARE), BF16),
            pltpu.VMEM((2, 448, TILE), BF16),
            pltpu.SemaphoreType.DMA((32,)),
            pltpu.SemaphoreType.DMA,
            pltpu.SemaphoreType.DMA((10,)),
            pltpu.SemaphoreType.DMA((3,)),
        ],
        compiler_params=pltpu.CompilerParams(vmem_limit_bytes=58 * MIB),
        cost_estimate=cost(3 * ROWS * ROWS * SHARE, 4e7),
    )(info, *own, *ends, *swapped, turned)


def unpack_kernel(info, r0, r1, r2, r3, update):
    m, a = info[1], info[2]
    for s, got in enumerate((r0, r1, r2, r3)):
        core = 1 - m if s >= 2 else m
        side = 1 - a if s % 2 else a
        for j in range(4):
            start = pl.multiple_of((9 * side + j + 5 * core) * TILE, TILE)
            update[:, pl.ds(start, TILE)] = got[j * HEIGHT : (j + 1) * HEIGHT]
    for s, (one, two) in enumerate(((r0, r2), (r1, r3))):
        side = 1 - a if s else a
        one, two = one[4 * HEIGHT :], two[4 * HEIGHT :]
        low, high = jnp.where(m == 0, one, two), jnp.where(m == 0, two, one)
        tile = pl.ds(pl.multiple_of((9 * side + 4) * TILE, TILE), TILE)
        update[:448, tile] = jnp.concatenate([low[:, :64], high[:, :64]], axis=1)
        update[448:, tile] = jnp.concatenate([low[:, 64:], high[:, 64:]], axis=1)


def unpack(info, parts):
    return pl.pallas_call(
        unpack_kernel,
        in_specs=[SMEM] + [VMEM] * 4,
        out_specs=VMEM,
        out_shape=jax.ShapeDtypeStruct((HEIGHT, 2304), BF16),
        compiler_params=pltpu.CompilerParams(vmem_limit_bytes=32 * MIB),
        cost_estimate=cost(0, 8.3e6),
    )(info, *parts)


def on_device(grad_tiles, tile_ids, momentum):
    core, zm, zl, y = (lax.axis_index(name) for name in AXES[1:])
    info = jnp.stack([core, zm, zl, y]).astype(jnp.int32)
    tile_count = grad_tiles.shape[0]

    owners = tile_ids // 8 // 7 * 4 + tile_ids % 8 // 2
    places = tile_ids // 8 % 7 * 2 + tile_ids % 2
    matches = owners[:, None] == jnp.arange(16, dtype=jnp.int32)[None, :]
    slots = jnp.sum(jnp.where(matches, jnp.arange(tile_count, dtype=jnp.int32)[:, None], 0), axis=0)
    labels = jnp.sum(jnp.where(matches, places[:, None] + 1, 0), axis=0) - 1
    upper, lower = pack(jnp.concatenate([slots, labels]), grad_tiles)
    upper = lax.all_to_all(upper, PLANE, split_axis=0, concat_axis=0, tiled=True)
    lower, _ = lax.optimization_barrier((lower, upper))
    lower = lax.all_to_all(lower, PLANE, split_axis=0, concat_axis=0, tiled=True)

    got_labels = upper[:, -1, 0].astype(jnp.int32)
    found = got_labels[None, :] == jnp.arange(tile_count, dtype=jnp.int32)[:, None]
    sources = jnp.sum(jnp.where(found, jnp.arange(16, dtype=jnp.int32)[None, :], 0), axis=1)
    details = jnp.concatenate([sources, zl[None].astype(jnp.int32)])
    new_momentum, *halves0 = update_momentum(details, upper, momentum, 0, None)
    new_momentum, *halves1 = update_momentum(details, lower, momentum, 1, new_momentum)

    def to_panel(halves):
        half0, half1 = halves
        return (
            move(half0, lambda c, m, a, y: (m, c, a, y)),
            move(half1, lambda c, m, a, y: (m, c, 1 - a, y)),
        )

    got0, got1 = to_panel(halves0), to_panel(halves1)
    blocks = (got0[0], got1[0], got0[1], got1[1])
    blocks += tuple(swap(x) for x in blocks)

    far = gram_chunks(info, blocks, ((1, 2),), [chunk(BF16, size) for _, size in PARTS])
    far0, far1, far2 = up(far[0]), down(far[1]), across(far[2])
    terms = gram_chunks(info, blocks, ((1, 1), (1, 3), (0, 2)), [chunk(F32)] * 3)
    q1, q2, q3 = in_vmem(second_sums_kernel, [chunk()] * 3, *terms, far0, far1, far2)
    g1, g2, g3 = across(q1), down(q2), up(q3)
    later, _ = lax.optimization_barrier((blocks, q1))
    nearest, beside, below, center = gram_chunks(
        info, later, ((0, 1), (1, 0), (0, 3), (0, 0)), [chunk(F32), chunk(F32), chunk(), chunk(F32)]
    )
    near = down(below)
    v1, v2 = in_vmem(third_sums_kernel, [chunk()] * 2, nearest, beside, g1, g2, g3)
    w1, w2 = up(v1), across(v2)
    later, _ = lax.optimization_barrier((blocks, v1))
    turned = turned_panel(info, later)
    (mine,) = in_vmem(last_sums_kernel, [chunk()], center, w1, w2, near, after=(turned,))

    low, high, pair = up(mine), down(mine), across(mine)
    a1, a2, a3 = across(high), up(pair), down(high)
    ends = tuple(
        send(x[row : row + size]) for send, x, (row, size) in zip((down, up, across), (a1, a2, a3), PARTS)
    )
    swapped = (
        swap(mine),
        swap(jnp.concatenate([low, high, pair])),
        swap(jnp.concatenate([a1, a2, a3])),
        swap(jnp.concatenate(ends)),
    )
    *sent, direct, flipped, mixed, scales = apply_poly(info, (mine, low, high, pair, a1, a2, a3), ends, swapped, turned)
    sent += apply_rest(info, direct, flipped, mixed, scales, turned)

    parts = (
        move(sent[0], lambda c, m, a, y: (m, c, a, y)),
        move(sent[1], lambda c, m, a, y: (m, c, 1 - a, y)),
        move(sent[2], lambda c, m, a, y: (m, 1 - c, a, y)),
        move(sent[3], lambda c, m, a, y: (m, 1 - c, 1 - a, y)),
    )
    return new_momentum, unpack(info, parts)


def solution(mesh):
    fine = Mesh(mesh.devices.reshape(4, 2, 2, 2, 4), AXES)
    tall = P(("x", "core", "zm", "zl"), "y")
    return jax.shard_map(
        on_device,
        mesh=fine,
        in_specs=(P(AXES, None, None), P(AXES), tall),
        out_specs=(tall, tall),
        check_vma=False,
    )
```

```python
import math

import jax
import jax.numpy as jnp
from jax import lax
from jax.experimental import pallas as pl
from jax.experimental.pallas import tpu as pltpu
from jax.sharding import Mesh
from jax.sharding import PartitionSpec as P

ROWS = 3584
COLS = 9216
MOMENTUM_RATE = 0.95
COEF_LINEAR = 3.4445
COEF_CUBIC = -4.775
COEF_QUINTIC = 2.0315
EPSILON = 1e-06

HEIGHT = 896
HALF = 1152
TILE = 128
SPLIT = ((0, 80), (80, 48))
LABEL = 16
SIDE = 256
BLOCKS = ROWS // SIDE
HALF_BLOCKS = BLOCKS // 2
CHUNK = HALF_BLOCKS * SIDE
PARTS = ((0, 608), (608, 592), (1200, 592))
WIDE = 640
SHARE = 576
AROUND = ROWS + CHUNK
BACK_ROWS = 4032

AXES = ("x", "core", "zm", "zl", "y")
PLANE = ("zm", "zl", "y")
BF16 = jnp.bfloat16
F32 = jnp.float32
MIB = 1 << 20
ANY = pl.BlockSpec(memory_space=pl.ANY)
HBM = pl.BlockSpec(memory_space=pltpu.HBM)
VMEM = pl.BlockSpec(memory_space=pltpu.VMEM)
SMEM = pl.BlockSpec(memory_space=pltpu.SMEM)


def cost(flops, size):
    return pl.CostEstimate(flops=int(flops), bytes_accessed=int(size), transcendentals=0)


def move(x, route):
    pairs = []
    for c in range(2):
        for m in range(2):
            for a in range(2):
                for y in range(4):
                    c2, m2, a2, y2 = route(c, m, a, y)
                    pairs.append((((c * 2 + m) * 2 + a) * 4 + y, ((c2 * 2 + m2) * 2 + a2) * 4 + y2 % 4))
    return lax.ppermute(x, AXES[1:], pairs)


def up(x):
    return move(x, lambda c, m, a, y: (c, m, a, y + 1))


def down(x):
    return move(x, lambda c, m, a, y: (c, m, a, y + 3))


def across(x):
    return move(x, lambda c, m, a, y: (c, m, 1 - a, y))


def swap(x):
    return move(x, lambda c, m, a, y: (1 - c, m, a, y))


def pack_kernel(ids, tiles, upper, lower, slots, places, held, first, second, sems, out_sems):
    n = tiles.shape[0]
    loads = [pltpu.make_async_copy(tiles.at[i], held.at[i], sems.at[i]) for i in range(n)]
    for load in loads:
        load.start()
    for o in range(upper.shape[0]):
        slots[o] = 0
        places[o] = -1

    @pl.loop(0, n)
    def _(i):
        row, column = ids[i] // 8, ids[i] % 8
        owner = row // 7 * 4 + column // 2
        slots[owner] = i
        places[owner] = row % 7 * 2 + column % 2

    for load in loads:
        load.wait()

    def copies(o):
        return (
            pltpu.make_async_copy(first.at[o], upper.at[o], out_sems.at[0, o]),
            pltpu.make_async_copy(second.at[o], lower.at[o], out_sems.at[1, o]),
        )

    @pl.loop(0, upper.shape[0])
    def _(o):
        slot = slots[o]
        for j in range(HALF // TILE):
            piece = held[slot, :, j * TILE : (j + 1) * TILE]
            for (row, size), out in zip(SPLIT, (first, second)):
                out[o, j * size : (j + 1) * size, :] = piece[row : row + size]
        place = jnp.full((LABEL, TILE), places[o], jnp.int32)
        first[o, first.shape[1] - LABEL :, :] = place.astype(F32).astype(BF16)
        for copy in copies(o):
            copy.start()

    @pl.loop(0, upper.shape[0])
    def _(o):
        for copy in copies(o):
            copy.wait()


def pack(ids, tiles):
    n = 16
    rows = [HALF // TILE * size for _, size in SPLIT]
    shapes = [(n, rows[0] + LABEL, TILE), (n, rows[1], TILE)]
    return pl.pallas_call(
        pack_kernel,
        in_specs=[SMEM, HBM],
        out_specs=[HBM] * 2,
        out_shape=[jax.ShapeDtypeStruct(shape, BF16) for shape in shapes],
        scratch_shapes=[pltpu.SMEM((n,), jnp.int32)] * 2
        + [pltpu.VMEM(tiles.shape, BF16)]
        + [pltpu.VMEM(shape, BF16) for shape in shapes]
        + [pltpu.SemaphoreType.DMA((tiles.shape[0],)), pltpu.SemaphoreType.DMA((2, n))],
        compiler_params=pltpu.CompilerParams(vmem_limit_bytes=62 * MIB),
        cost_estimate=cost(0, 4 * tiles.size),
    )(ids, tiles)


def momentum_kernel(part, info, arrived, momentum, *refs):
    new, half0, half1, tile, old, fresh, rounded, in_sems, out_sems = refs[-9:]
    n = HEIGHT // TILE
    row, size = SPLIT[part]

    def place(t, r):
        half = (t + info[14]) % 2
        columns = pl.ds(pl.multiple_of(half * HALF, TILE), HALF)
        return pl.ds(pl.multiple_of(r * TILE + row, 16), size), columns

    def reads(t, r):
        source = info[2 * r + (t + info[14]) % 2]
        i = t * n + r
        return (
            pltpu.make_async_copy(momentum.at[place(t, r)], old.at[i], in_sems.at[0, i]),
            pltpu.make_async_copy(arrived.at[source, 0 : HALF // TILE * size], tile.at[i], in_sems.at[1, i]),
        )

    def writes(t, r):
        i = t * n + r
        out = (half0, half1)[t].at[r]
        return (
            pltpu.make_async_copy(fresh.at[i], new.at[place(t, r)], out_sems.at[0, i]),
            pltpu.make_async_copy(rounded.at[i], out, out_sems.at[1, i]),
        )

    for t in range(2):
        for r in range(n):
            for copy in reads(t, r):
                copy.start()
    for t in range(2):

        @pl.loop(0, n)
        def _(r):
            i = t * n + r
            for copy in reads(t, r):
                copy.wait()
            for j in range(HALF // TILE):
                columns = slice(j * TILE, (j + 1) * TILE)
                g = tile[i, j * size : (j + 1) * size, :].astype(F32)
                later = MOMENTUM_RATE * old[i, :, columns] + g
                fresh[i, :, columns] = later
                rounded[i, :, columns] = (g + MOMENTUM_RATE * later).astype(BF16)
            for copy in writes(t, r):
                copy.start()

    for t in range(2):

        @pl.loop(0, n)
        def _(r):
            for copy in writes(t, r):
                copy.wait()


def update_momentum(info, arrived, momentum, part, so_far):
    more = () if so_far is None else (so_far,)
    n = 2 * HEIGHT // TILE
    size = SPLIT[part][1]
    return pl.pallas_call(
        lambda *refs: momentum_kernel(part, *refs),
        in_specs=[SMEM] + [HBM] * (2 + len(more)),
        out_specs=[HBM] * 3,
        out_shape=[
            jax.ShapeDtypeStruct(momentum.shape, F32),
            jax.ShapeDtypeStruct((n // 2, size, HALF), BF16),
            jax.ShapeDtypeStruct((n // 2, size, HALF), BF16),
        ],
        scratch_shapes=[
            pltpu.VMEM((n, HALF // TILE * size, TILE), BF16),
            pltpu.VMEM((n, size, HALF), F32),
            pltpu.VMEM((n, size, HALF), F32),
            pltpu.VMEM((n, size, HALF), BF16),
            pltpu.SemaphoreType.DMA((2, n)),
            pltpu.SemaphoreType.DMA((2, n)),
        ],
        input_output_aliases={3: 0} if more else {},
        compiler_params=pltpu.CompilerParams(vmem_limit_bytes=62 * MIB),
        cost_estimate=cost(0, HEIGHT * HALF * 12),
    )(info, arrived, momentum, *more)


def panel_copies(info, blocks, panel, columns=None):
    c, a = info[0], info[2]
    copies = []
    for i, block in enumerate(blocks):
        other, t, part = i // 4, i // 2 % 2, i % 2
        core = 1 - c if other else c
        z = 2 * core + (a + t) % 2
        src = block if columns is None else block.at[:, :, columns]
        row, size = SPLIT[part]
        rows = pl.ds(z * (HEIGHT // TILE), HEIGHT // TILE)
        copies.append((src, panel.at[rows, row : row + size]))
    return copies


def panel_shape(width):
    return pltpu.VMEM((ROWS // TILE, TILE, width), BF16)


def chip_at(info, flip, dy):
    a, y = info[2], info[3]
    return (1 - a if flip else a) * 4 + (y + dy) % 4


def load_all(copies, sems):
    copies = [pltpu.make_async_copy(src, dst, sems.at[i]) for i, (src, dst) in enumerate(copies)]
    for copy in copies:
        copy.start()
    for copy in copies:
        copy.wait()


def gram_kernel(dests, info, *refs):
    blocks, outs = refs[:8], refs[8:-2]
    panel, sems = refs[-2:]
    load_all(panel_copies(info, blocks, panel), sems)

    def term(b, d):
        left = panel[pl.ds(2 * b, 2)].reshape(SIDE, HALF)
        right = panel[pl.ds(2 * ((b + d) % BLOCKS), 2)].reshape(SIDE, HALF)
        return lax.dot_general(left, right, (((1,), (1,)), ((), ())), preferred_element_type=F32)

    base = HALF_BLOCKS * info[0]
    if len(dests) == 1:
        d = chip_at(info, *dests[0])
        for b in range(HALF_BLOCKS):
            block = term(base + b, d).astype(BF16)
            for out, (row, size) in zip(outs, PARTS):
                low, high = max(row, b * SIDE), min(row + size, (b + 1) * SIDE)
                if low < high:
                    out[low - row : high - row] = block[low - b * SIDE : high - b * SIDE]
    else:

        @pl.loop(0, HALF_BLOCKS)
        def _(b):
            for dest, out in zip(dests, outs):
                block = term(base + b, chip_at(info, *dest))
                out[pl.ds(pl.multiple_of(b * SIDE, SIDE), SIDE)] = block.astype(out.dtype)


def gram_chunks(info, blocks, dests, shapes):
    return pl.pallas_call(
        lambda *refs: gram_kernel(dests, *refs),
        in_specs=[SMEM] + [HBM] * 8,
        out_specs=[VMEM] * len(shapes),
        out_shape=shapes,
        scratch_shapes=[panel_shape(HALF), pltpu.SemaphoreType.DMA((8,))],
        compiler_params=pltpu.CompilerParams(vmem_limit_bytes=24 * MIB),
        cost_estimate=cost(len(dests) * 2 * CHUNK * SIDE * HALF, 8.3e6 + len(dests) * CHUNK * SIDE * 4),
    )(info, *blocks)


def chunk(dtype=BF16, rows=CHUNK):
    return jax.ShapeDtypeStruct((rows, SIDE), dtype)


def second_sums_kernel(p1, p2, p3, r1, r2, r3, q1, q2, q3):
    for own, got, out, (row, size) in zip((p1, p2, p3), (r1, r2, r3), (q1, q2, q3), PARTS):
        if row:
            out[:row] = own[:row].astype(BF16)
        out[row : row + size] = (own[row : row + size] + got[...].astype(F32)).astype(BF16)
        if row + size < CHUNK:
            out[row + size :] = own[row + size :].astype(BF16)


def third_sums_kernel(p1, p2, g1, g2, g3, v1, v2):
    v1[...] = (p1[...] + (g1[...].astype(F32) + g3[...].astype(F32))).astype(BF16)
    v2[...] = (p2[...] + g2[...].astype(F32)).astype(BF16)


def last_sums_kernel(p, v1, v2, v3, turned, out):
    total = p[...] + (v1[...].astype(F32) + v2[...].astype(F32) + v3[...].astype(F32))
    out[...] = total.astype(BF16)


def in_vmem(kernel, shapes, *args, after=()):
    size = sum(x.size * x.dtype.itemsize for x in args)
    return pl.pallas_call(
        kernel,
        in_specs=[VMEM] * len(args) + [ANY] * len(after),
        out_specs=[VMEM] * len(shapes),
        out_shape=shapes,
        compiler_params=pltpu.CompilerParams(vmem_limit_bytes=16 * MIB),
        cost_estimate=cost(0, size),
    )(*args, *after)


def turn_kernel(info, *refs):
    blocks, out, held, flat, sems = refs[:8], *refs[8:]
    c = info[0]
    shift = pl.multiple_of(512 * c, TILE)
    load_all(panel_copies(info, blocks, held, pl.ds(shift, WIDE)), sems)
    for r in range(ROWS // TILE):
        flat[:, r * TILE : (r + 1) * TILE] = held[r].T
    out[:512, :ROWS] = flat[pl.ds(pl.multiple_of(128 * c, 64), 512), :]
    out[512:, :ROWS] = flat[pl.ds(pl.multiple_of(512 - 448 * c, 64), 64), :]
    out[:, ROWS:] = out[:, :CHUNK]


def turned_panel(info, blocks):
    return pl.pallas_call(
        turn_kernel,
        in_specs=[SMEM] + [HBM] * 8,
        out_specs=VMEM,
        out_shape=jax.ShapeDtypeStruct((SHARE, AROUND), BF16),
        scratch_shapes=[panel_shape(WIDE), pltpu.VMEM((WIDE, ROWS), BF16), pltpu.SemaphoreType.DMA((8,))],
        compiler_params=pltpu.CompilerParams(vmem_limit_bytes=24 * MIB),
        cost_estimate=cost(0, 1.2e7),
    )(info, *blocks)


SOURCES = ((0, 0), (0, 3), (0, 1), (1, 0), (1, 1), (1, 3), (0, 2), (1, 2))


def apply_kernel(info, *refs):
    own, ends, swapped = refs[:7], refs[7:10], refs[10:14]
    turned = refs[14]
    out, near_direct, near_flipped, rest_direct, rest_flipped, all_mixed, scales = refs[15:22]
    direct, flipped, mixed, stage, extra, sems, out_sems, keep_sems = refs[22:]
    panel = turned
    c = info[0]
    pieces = [(c, ref, 0, rel) for ref, rel in zip(own, SOURCES)]
    pieces += [(1 - c, swapped[0], 0, SOURCES[0]), (1 - c, swapped[3], 0, SOURCES[7])]
    pieces += [(1 - c, swapped[1 + n // 3], n % 3 * CHUNK, SOURCES[1 + n]) for n in range(6)]
    for n, (core, ref, row, rel) in enumerate(pieces):
        d = chip_at(info, *rel)

        @pl.loop(0, HALF_BLOCKS)
        def _(b):
            i = (core * HALF_BLOCKS + b + d) % BLOCKS
            src = ref.at[pl.ds(pl.multiple_of(row + b * SIDE, SIDE), SIDE)]
            pltpu.make_async_copy(src, direct.at[i, pl.ds(pl.multiple_of((7 - d) * SIDE, SIDE), SIDE)], sems.at[n]).start()

    d = chip_at(info, *SOURCES[7])
    last = []
    for ref, (row, size) in zip(ends, PARTS):
        for b in range(HALF_BLOCKS):
            low, high = max(row, b * SIDE), min(row + size, (b + 1) * SIDE)
            if low < high:
                i = (c * HALF_BLOCKS + b + d) % BLOCKS
                start = pl.multiple_of((7 - d) * SIDE + low - b * SIDE, 16)
                src = ref.at[low - row : high - row]
                last.append(pltpu.make_async_copy(src, direct.at[i, pl.ds(start, high - low)], sems.at[15 + len(last)]))
    for copy in last:
        copy.start()
    for n in range(15):
        whole = direct.at[0:HALF_BLOCKS, 0:SIDE]
        pltpu.make_async_copy(whole, whole, sems.at[n]).wait()
    for copy in last:
        copy.wait()

    near = near_start(info, 1)
    other = (1 - c) * HALF_BLOCKS
    keeps = [
        pltpu.make_async_copy(direct.at[pl.ds(near, 4)], near_direct, keep_sems.at[0]),
        pltpu.make_async_copy(direct.at[pl.ds(other, HALF_BLOCKS)], rest_direct, keep_sems.at[1]),
    ]
    for copy in keeps:
        copy.start()
    on = lax.broadcasted_iota(jnp.int32, (SIDE, SIDE), 0) == lax.broadcasted_iota(jnp.int32, (SIDE, SIDE), 1)
    diagonal = jnp.zeros((SIDE, SIDE), F32)
    for i in range(BLOCKS):
        diagonal += direct[i, 7 * SIDE :, :].astype(F32)
    total = jnp.sum(jnp.where(on, diagonal, 0.0))
    total = jnp.full((1, SIDE), total, F32)
    factor = math.sqrt(ROWS) / (2.0 * (jnp.sqrt(total) + EPSILON))
    square = factor * factor

    def product(i, x):
        return gram_times(i, x, direct.at[i], flipped.at[i]) * square

    @pl.loop(0, BLOCKS)
    def _(i):
        for e in range(1, 7):
            far = (i + e) % BLOCKS
            flipped[i, (e - 1) * SIDE : e * SIDE, :] = direct[far, (7 - e) * SIDE : (8 - e) * SIDE, :].T
        columns = pl.ds(pl.multiple_of(i * SIDE, SIDE), SIDE)
        mix = COEF_CUBIC * panel[:, columns].astype(F32) + COEF_QUINTIC * product(i, panel)
        mix = mix.astype(BF16)
        mixed[:, columns] = mix

        @pl.when(i < HALF_BLOCKS)
        def _():
            mixed[:, pl.ds(pl.multiple_of(i * SIDE + ROWS, SIDE), SIDE)] = mix

    scale = math.sqrt(COLS) * factor
    scales[...] = jnp.concatenate([scale] * 4 + [square] * 4)
    more = [
        pltpu.make_async_copy(flipped.at[pl.ds(near, 4)], near_flipped, keep_sems.at[2]),
        pltpu.make_async_copy(flipped.at[pl.ds(other, HALF_BLOCKS)], rest_flipped, keep_sems.at[3]),
        pltpu.make_async_copy(mixed, all_mixed, keep_sems.at[4]),
    ]
    for copy in more:
        copy.start()

    @pl.loop(0, 4)
    def _(b):
        i = near_start(info, 0) + b
        columns = pl.ds(pl.multiple_of(i * SIDE, SIDE), SIDE)
        result = scale * (COEF_LINEAR * panel[:, columns].astype(F32) + product(i, mixed))
        stage[pl.ds(pl.multiple_of(b * SIDE, SIDE), SIDE)] = result.astype(BF16).T

    send_back(stage, extra, [(info[2] * TILE, out)], out_sems)
    for copy in keeps + more:
        copy.wait()


def near_start(info, side):
    a = info[2]
    return info[0] * HALF_BLOCKS + 3 * (1 - a if side else a)


def gram_times(i, x, direct, flipped):
    first = pl.ds(pl.multiple_of((i + 7) % BLOCKS * SIDE, SIDE), 8 * SIDE)
    rest = pl.ds(pl.multiple_of((i + 1) % BLOCKS * SIDE, SIDE), 6 * SIDE)
    result = jnp.dot(x[:, first], direct[...], preferred_element_type=F32)
    return result + jnp.dot(x[:, rest], flipped[...], preferred_element_type=F32)


def send_back(stage, extra, outs, sems):
    sends = []
    for n, (start, out) in enumerate(outs):
        for j in range(4):
            rows = pl.ds(pl.multiple_of(start, 128), HEIGHT)
            sends.append((stage.at[rows, j * TILE : (j + 1) * TILE], out.at[pl.ds(j * HEIGHT, HEIGHT)]))
        halves = [stage[pl.ds(pl.multiple_of(start + row, 64), 448), 512:] for row in (0, 448)]
        extra[n] = jnp.concatenate(halves, axis=1)
        sends.append((extra.at[n], out.at[pl.ds(4 * HEIGHT, 448)]))
    load_all(sends, sems)


def rest_start(near, info):
    return near_start(info, 1) if near else (1 - info[0]) * HALF_BLOCKS


def rest_kernel(near, info, direct, flipped, panel, all_mixed, scales, *refs):
    outs, (mixed, stage, extra, sems) = refs[:-4], refs[-4:]
    b = pl.program_id(0)

    @pl.when(b == 0)
    def _():
        load_all([(all_mixed, mixed)], sems)

    i = rest_start(near, info) + b
    product = gram_times(i, mixed, direct.at[0], flipped.at[0]) * scales[4:5]
    result = scales[0:1] * (COEF_LINEAR * panel[...].astype(F32) + product)
    stage[pl.ds(pl.multiple_of(b * SIDE, SIDE), SIDE)] = result.astype(BF16).T

    @pl.when(b == pl.num_programs(0) - 1)
    def _():
        a = info[2]
        starts = [(1 - a) * TILE] if near else [a * HEIGHT, (1 - a) * HEIGHT]
        send_back(stage, extra, list(zip(starts, outs)), sems)


def apply_rest(near, info, direct, flipped, mixed, scales, turned):
    n = direct.shape[0]
    count = 1 if near else 2
    return pl.pallas_call(
        lambda *refs: rest_kernel(near, *refs),
        grid_spec=pltpu.PrefetchScalarGridSpec(
            num_scalar_prefetch=1,
            grid=(n,),
            in_specs=[
                pl.BlockSpec((1, 8 * SIDE, SIDE), lambda b, s: (b, 0, 0)),
                pl.BlockSpec((1, 6 * SIDE, SIDE), lambda b, s: (b, 0, 0)),
                pl.BlockSpec((SHARE, SIDE), lambda b, s: (0, rest_start(near, s) + b)),
                HBM,
                VMEM,
            ],
            out_specs=[HBM] * count,
            scratch_shapes=[
                pltpu.VMEM((SHARE, AROUND), BF16),
                pltpu.VMEM((n * SIDE, SHARE), BF16),
                pltpu.VMEM((2, 448, TILE), BF16),
                pltpu.SemaphoreType.DMA((10,)),
            ],
        ),
        out_shape=[jax.ShapeDtypeStruct((BACK_ROWS, TILE), BF16)] * count,
        compiler_params=pltpu.CompilerParams(vmem_limit_bytes=62 * MIB),
        cost_estimate=cost(n * 2 * SIDE * ROWS * SHARE, 2e7),
    )(info, direct, flipped, turned, mixed, scales)


def apply_poly(info, own, ends, swapped, turned):
    return pl.pallas_call(
        apply_kernel,
        in_specs=[SMEM] + [ANY] * 14 + [VMEM],
        out_specs=[HBM] * 6 + [VMEM],
        out_shape=[
            jax.ShapeDtypeStruct((BACK_ROWS, TILE), BF16),
            jax.ShapeDtypeStruct((4, 8 * SIDE, SIDE), BF16),
            jax.ShapeDtypeStruct((4, 6 * SIDE, SIDE), BF16),
            jax.ShapeDtypeStruct((HALF_BLOCKS, 8 * SIDE, SIDE), BF16),
            jax.ShapeDtypeStruct((HALF_BLOCKS, 6 * SIDE, SIDE), BF16),
            jax.ShapeDtypeStruct((SHARE, AROUND), BF16),
            jax.ShapeDtypeStruct((8, SIDE), F32),
        ],
        scratch_shapes=[
            pltpu.VMEM((BLOCKS, 8 * SIDE, SIDE), BF16),
            pltpu.VMEM((BLOCKS, 6 * SIDE, SIDE), BF16),
            pltpu.VMEM((SHARE, AROUND), BF16),
            pltpu.VMEM((4 * SIDE, SHARE), BF16),
            pltpu.VMEM((1, 448, TILE), BF16),
            pltpu.SemaphoreType.DMA((32,)),
            pltpu.SemaphoreType.DMA((5,)),
            pltpu.SemaphoreType.DMA((5,)),
        ],
        compiler_params=pltpu.CompilerParams(vmem_limit_bytes=44 * MIB),
        cost_estimate=cost(3 * ROWS * ROWS * SHARE, 4e7),
    )(info, *own, *ends, *swapped, turned)


def unpack_kernel(info, r0, r1, r2, r3, update):
    m, a = info[1], info[2]
    for s, got in enumerate((r0, r1, r2, r3)):
        core = 1 - m if s >= 2 else m
        side = 1 - a if s % 2 else a
        for j in range(4):
            start = pl.multiple_of((9 * side + j + 5 * core) * TILE, TILE)
            update[:, pl.ds(start, TILE)] = got[j * HEIGHT : (j + 1) * HEIGHT]
    for s, (one, two) in enumerate(((r0, r2), (r1, r3))):
        side = 1 - a if s else a
        one, two = one[4 * HEIGHT :], two[4 * HEIGHT :]
        low, high = jnp.where(m == 0, one, two), jnp.where(m == 0, two, one)
        tile = pl.ds(pl.multiple_of((9 * side + 4) * TILE, TILE), TILE)
        update[:448, tile] = jnp.concatenate([low[:, :64], high[:, :64]], axis=1)
        update[448:, tile] = jnp.concatenate([low[:, 64:], high[:, 64:]], axis=1)


def unpack(info, parts):
    return pl.pallas_call(
        unpack_kernel,
        in_specs=[SMEM] + [VMEM] * 4,
        out_specs=VMEM,
        out_shape=jax.ShapeDtypeStruct((HEIGHT, 2304), BF16),
        compiler_params=pltpu.CompilerParams(vmem_limit_bytes=32 * MIB),
        cost_estimate=cost(0, 8.3e6),
    )(info, *parts)


def on_device(grad_tiles, tile_ids, momentum):
    core, zm, zl, y = (lax.axis_index(name) for name in AXES[1:])
    info = jnp.stack([core, zm, zl, y]).astype(jnp.int32)
    tile_count = grad_tiles.shape[0]

    upper, lower = pack(tile_ids, grad_tiles)
    upper = lax.all_to_all(upper, PLANE, split_axis=0, concat_axis=0, tiled=True)
    lower, _ = lax.optimization_barrier((lower, upper))
    lower = lax.all_to_all(lower, PLANE, split_axis=0, concat_axis=0, tiled=True)

    got_labels = upper[:, -1, 0].astype(jnp.int32)
    found = got_labels[None, :] == jnp.arange(tile_count, dtype=jnp.int32)[:, None]
    sources = jnp.sum(jnp.where(found, jnp.arange(16, dtype=jnp.int32)[None, :], 0), axis=1)
    details = jnp.concatenate([sources, zl[None].astype(jnp.int32)])
    new_momentum, *halves0 = update_momentum(details, upper, momentum, 0, None)
    new_momentum, *halves1 = update_momentum(details, lower, momentum, 1, new_momentum)

    def to_panel(halves):
        half0, half1 = halves
        return (
            move(half0, lambda c, m, a, y: (m, c, a, y)),
            move(half1, lambda c, m, a, y: (m, c, 1 - a, y)),
        )

    got0, got1 = to_panel(halves0), to_panel(halves1)
    blocks = (got0[0], got1[0], got0[1], got1[1])
    blocks += tuple(swap(x) for x in blocks)

    far = gram_chunks(info, blocks, ((1, 2),), [chunk(BF16, size) for _, size in PARTS])
    far0, far1, far2 = up(far[0]), down(far[1]), across(far[2])
    terms = gram_chunks(info, blocks, ((1, 1), (1, 3), (0, 2)), [chunk(F32)] * 3)
    q1, q2, q3 = in_vmem(second_sums_kernel, [chunk()] * 3, *terms, far0, far1, far2)
    g1, g2, g3 = across(q1), down(q2), up(q3)
    later, _ = lax.optimization_barrier((blocks, q1))
    nearest, beside, below, center = gram_chunks(
        info, later, ((0, 1), (1, 0), (0, 3), (0, 0)), [chunk(F32), chunk(F32), chunk(), chunk(F32)]
    )
    near = down(below)
    v1, v2 = in_vmem(third_sums_kernel, [chunk()] * 2, nearest, beside, g1, g2, g3)
    w1, w2 = up(v1), across(v2)
    later, _ = lax.optimization_barrier((blocks, v1))
    turned = turned_panel(info, later)
    (mine,) = in_vmem(last_sums_kernel, [chunk()], center, w1, w2, near, after=(turned,))

    low, high, pair = up(mine), down(mine), across(mine)
    a1, a2, a3 = across(high), up(pair), down(high)
    ends = tuple(
        send(x[row : row + size]) for send, x, (row, size) in zip((down, up, across), (a1, a2, a3), PARTS)
    )
    swapped = (
        swap(mine),
        swap(jnp.concatenate([low, high, pair])),
        swap(jnp.concatenate([a1, a2, a3])),
        swap(jnp.concatenate(ends)),
    )
    first, *near_rows, rest_direct, rest_flipped, mixed, scales = apply_poly(
        info, (mine, low, high, pair, a1, a2, a3), ends, swapped, turned
    )
    (second,) = apply_rest(True, info, *near_rows, mixed, scales, turned)
    later, _ = lax.optimization_barrier((mixed, second))
    sent = (first, second, *apply_rest(False, info, rest_direct, rest_flipped, later, scales, turned))

    parts = (
        move(sent[0], lambda c, m, a, y: (m, c, a, y)),
        move(sent[1], lambda c, m, a, y: (m, c, 1 - a, y)),
        move(sent[2], lambda c, m, a, y: (m, 1 - c, a, y)),
        move(sent[3], lambda c, m, a, y: (m, 1 - c, 1 - a, y)),
    )
    return new_momentum, unpack(info, parts)


def solution(mesh):
    fine = Mesh(mesh.devices.reshape(4, 2, 2, 2, 4), AXES)
    tall = P(("x", "core", "zm", "zl"), "y")
    return jax.shard_map(
        on_device,
        mesh=fine,
        in_specs=(P(AXES, None, None), P(AXES), tall),
        out_specs=(tall, tall),
        check_vma=False,
    )
```

```python
import math

import jax
import jax.numpy as jnp
from jax import lax
from jax.experimental import pallas as pl
from jax.experimental.pallas import tpu as pltpu
from jax.sharding import Mesh
from jax.sharding import PartitionSpec as P

ROWS = 3584
COLS = 9216
MOMENTUM_RATE = 0.95
COEF_LINEAR = 3.4445
COEF_CUBIC = -4.775
COEF_QUINTIC = 2.0315
EPSILON = 1e-06

HEIGHT = 896
HALF = 1152
TILE = 128
SPLIT = ((0, 80), (80, 48))
LABEL = 16
SIDE = 256
BLOCKS = ROWS // SIDE
HALF_BLOCKS = BLOCKS // 2
CHUNK = HALF_BLOCKS * SIDE
PARTS = ((0, 608), (608, 592), (1200, 592))
WIDE = 640
SHARES = (320, 256)
AROUND = ROWS + CHUNK
BACK_ROWS = (2240, 1792)

AXES = ("x", "core", "zm", "zl", "y")
PLANE = ("zm", "zl", "y")
BF16 = jnp.bfloat16
F32 = jnp.float32
MIB = 1 << 20
ANY = pl.BlockSpec(memory_space=pl.ANY)
HBM = pl.BlockSpec(memory_space=pltpu.HBM)
VMEM = pl.BlockSpec(memory_space=pltpu.VMEM)
SMEM = pl.BlockSpec(memory_space=pltpu.SMEM)


def cost(flops, size):
    return pl.CostEstimate(flops=int(flops), bytes_accessed=int(size), transcendentals=0)


def move(x, route):
    pairs = []
    for c in range(2):
        for m in range(2):
            for a in range(2):
                for y in range(4):
                    c2, m2, a2, y2 = route(c, m, a, y)
                    pairs.append((((c * 2 + m) * 2 + a) * 4 + y, ((c2 * 2 + m2) * 2 + a2) * 4 + y2 % 4))
    return lax.ppermute(x, AXES[1:], pairs)


def up(x):
    return move(x, lambda c, m, a, y: (c, m, a, y + 1))


def down(x):
    return move(x, lambda c, m, a, y: (c, m, a, y + 3))


def across(x):
    return move(x, lambda c, m, a, y: (c, m, 1 - a, y))


def swap(x):
    return move(x, lambda c, m, a, y: (1 - c, m, a, y))


def pack_kernel(ids, tiles, upper, lower, slots, places, held, first, second, sems, out_sems):
    n = tiles.shape[0]
    loads = [pltpu.make_async_copy(tiles.at[i], held.at[i], sems.at[i]) for i in range(n)]
    for load in loads:
        load.start()
    for o in range(upper.shape[0]):
        slots[o] = 0
        places[o] = -1

    @pl.loop(0, n)
    def _(i):
        row, column = ids[i] // 8, ids[i] % 8
        owner = row // 7 * 4 + column // 2
        slots[owner] = i
        places[owner] = row % 7 * 2 + column % 2

    for load in loads:
        load.wait()

    def copies(o):
        return (
            pltpu.make_async_copy(first.at[o], upper.at[o], out_sems.at[0, o]),
            pltpu.make_async_copy(second.at[o], lower.at[o], out_sems.at[1, o]),
        )

    @pl.loop(0, upper.shape[0])
    def _(o):
        slot = slots[o]
        for j in range(HALF // TILE):
            piece = held[slot, :, j * TILE : (j + 1) * TILE]
            for (row, size), out in zip(SPLIT, (first, second)):
                out[o, j * size : (j + 1) * size, :] = piece[row : row + size]
        place = jnp.full((LABEL, TILE), places[o], jnp.int32)
        first[o, first.shape[1] - LABEL :, :] = place.astype(F32).astype(BF16)
        for copy in copies(o):
            copy.start()

    @pl.loop(0, upper.shape[0])
    def _(o):
        for copy in copies(o):
            copy.wait()


def pack(ids, tiles):
    n = 16
    rows = [HALF // TILE * size for _, size in SPLIT]
    shapes = [(n, rows[0] + LABEL, TILE), (n, rows[1], TILE)]
    return pl.pallas_call(
        pack_kernel,
        in_specs=[SMEM, HBM],
        out_specs=[HBM] * 2,
        out_shape=[jax.ShapeDtypeStruct(shape, BF16) for shape in shapes],
        scratch_shapes=[pltpu.SMEM((n,), jnp.int32)] * 2
        + [pltpu.VMEM(tiles.shape, BF16)]
        + [pltpu.VMEM(shape, BF16) for shape in shapes]
        + [pltpu.SemaphoreType.DMA((tiles.shape[0],)), pltpu.SemaphoreType.DMA((2, n))],
        compiler_params=pltpu.CompilerParams(vmem_limit_bytes=62 * MIB),
        cost_estimate=cost(0, 4 * tiles.size),
    )(ids, tiles)


def momentum_kernel(part, info, arrived, momentum, *refs):
    new, half0, half1, tile, old, fresh, rounded, in_sems, out_sems = refs[-9:]
    n = HEIGHT // TILE
    row, size = SPLIT[part]

    def place(t, r):
        half = (t + info[14]) % 2
        columns = pl.ds(pl.multiple_of(half * HALF, TILE), HALF)
        return pl.ds(pl.multiple_of(r * TILE + row, 16), size), columns

    def reads(t, r):
        source = info[2 * r + (t + info[14]) % 2]
        i = t * n + r
        return (
            pltpu.make_async_copy(momentum.at[place(t, r)], old.at[i], in_sems.at[0, i]),
            pltpu.make_async_copy(arrived.at[source, 0 : HALF // TILE * size], tile.at[i], in_sems.at[1, i]),
        )

    def writes(t, r):
        i = t * n + r
        out = (half0, half1)[t].at[r]
        return (
            pltpu.make_async_copy(fresh.at[i], new.at[place(t, r)], out_sems.at[0, i]),
            pltpu.make_async_copy(rounded.at[i], out, out_sems.at[1, i]),
        )

    for t in range(2):
        for r in range(n):
            for copy in reads(t, r):
                copy.start()
    for t in range(2):

        @pl.loop(0, n)
        def _(r):
            i = t * n + r
            for copy in reads(t, r):
                copy.wait()
            for j in range(HALF // TILE):
                columns = slice(j * TILE, (j + 1) * TILE)
                g = tile[i, j * size : (j + 1) * size, :].astype(F32)
                later = MOMENTUM_RATE * old[i, :, columns] + g
                fresh[i, :, columns] = later
                rounded[i, :, columns] = (g + MOMENTUM_RATE * later).astype(BF16)
            for copy in writes(t, r):
                copy.start()

    for t in range(2):

        @pl.loop(0, n)
        def _(r):
            for copy in writes(t, r):
                copy.wait()


def update_momentum(info, arrived, momentum, part, so_far):
    more = () if so_far is None else (so_far,)
    n = 2 * HEIGHT // TILE
    size = SPLIT[part][1]
    return pl.pallas_call(
        lambda *refs: momentum_kernel(part, *refs),
        in_specs=[SMEM] + [HBM] * (2 + len(more)),
        out_specs=[HBM] * 3,
        out_shape=[
            jax.ShapeDtypeStruct(momentum.shape, F32),
            jax.ShapeDtypeStruct((n // 2, size, HALF), BF16),
            jax.ShapeDtypeStruct((n // 2, size, HALF), BF16),
        ],
        scratch_shapes=[
            pltpu.VMEM((n, HALF // TILE * size, TILE), BF16),
            pltpu.VMEM((n, size, HALF), F32),
            pltpu.VMEM((n, size, HALF), F32),
            pltpu.VMEM((n, size, HALF), BF16),
            pltpu.SemaphoreType.DMA((2, n)),
            pltpu.SemaphoreType.DMA((2, n)),
        ],
        input_output_aliases={3: 0} if more else {},
        compiler_params=pltpu.CompilerParams(vmem_limit_bytes=62 * MIB),
        cost_estimate=cost(0, HEIGHT * HALF * 12),
    )(info, arrived, momentum, *more)


def panel_copies(info, blocks, panel, columns=None):
    c, a = info[0], info[2]
    copies = []
    for i, block in enumerate(blocks):
        other, t, part = i // 4, i // 2 % 2, i % 2
        core = 1 - c if other else c
        z = 2 * core + (a + t) % 2
        src = block if columns is None else block.at[:, :, columns]
        row, size = SPLIT[part]
        rows = pl.ds(z * (HEIGHT // TILE), HEIGHT // TILE)
        copies.append((src, panel.at[rows, row : row + size]))
    return copies


def panel_shape(width):
    return pltpu.VMEM((ROWS // TILE, TILE, width), BF16)


def chip_at(info, flip, dy):
    a, y = info[2], info[3]
    return (1 - a if flip else a) * 4 + (y + dy) % 4


def load_all(copies, sems):
    copies = [pltpu.make_async_copy(src, dst, sems.at[i]) for i, (src, dst) in enumerate(copies)]
    for copy in copies:
        copy.start()
    for copy in copies:
        copy.wait()


def gram_kernel(dests, info, *refs):
    blocks, outs = refs[:8], refs[8:-2]
    panel, sems = refs[-2:]
    load_all(panel_copies(info, blocks, panel), sems)

    def term(b, d):
        left = panel[pl.ds(2 * b, 2)].reshape(SIDE, HALF)
        right = panel[pl.ds(2 * ((b + d) % BLOCKS), 2)].reshape(SIDE, HALF)
        return lax.dot_general(left, right, (((1,), (1,)), ((), ())), preferred_element_type=F32)

    base = HALF_BLOCKS * info[0]
    if len(dests) == 1:
        d = chip_at(info, *dests[0])
        for b in range(HALF_BLOCKS):
            block = term(base + b, d).astype(BF16)
            for out, (row, size) in zip(outs, PARTS):
                low, high = max(row, b * SIDE), min(row + size, (b + 1) * SIDE)
                if low < high:
                    out[low - row : high - row] = block[low - b * SIDE : high - b * SIDE]
    else:

        @pl.loop(0, HALF_BLOCKS)
        def _(b):
            for dest, out in zip(dests, outs):
                block = term(base + b, chip_at(info, *dest))
                out[pl.ds(pl.multiple_of(b * SIDE, SIDE), SIDE)] = block.astype(out.dtype)


def gram_chunks(info, blocks, dests, shapes):
    return pl.pallas_call(
        lambda *refs: gram_kernel(dests, *refs),
        in_specs=[SMEM] + [HBM] * 8,
        out_specs=[VMEM] * len(shapes),
        out_shape=shapes,
        scratch_shapes=[panel_shape(HALF), pltpu.SemaphoreType.DMA((8,))],
        compiler_params=pltpu.CompilerParams(vmem_limit_bytes=24 * MIB),
        cost_estimate=cost(len(dests) * 2 * CHUNK * SIDE * HALF, 8.3e6 + len(dests) * CHUNK * SIDE * 4),
    )(info, *blocks)


def chunk(dtype=BF16, rows=CHUNK):
    return jax.ShapeDtypeStruct((rows, SIDE), dtype)


def second_sums_kernel(p1, p2, p3, r1, r2, r3, q1, q2, q3):
    for own, got, out, (row, size) in zip((p1, p2, p3), (r1, r2, r3), (q1, q2, q3), PARTS):
        if row:
            out[:row] = own[:row].astype(BF16)
        out[row : row + size] = (own[row : row + size] + got[...].astype(F32)).astype(BF16)
        if row + size < CHUNK:
            out[row + size :] = own[row + size :].astype(BF16)


def third_sums_kernel(p1, p2, g1, g2, g3, v1, v2):
    v1[...] = (p1[...] + (g1[...].astype(F32) + g3[...].astype(F32))).astype(BF16)
    v2[...] = (p2[...] + g2[...].astype(F32)).astype(BF16)


def last_sums_kernel(p, v1, v2, v3, first, second, out):
    total = p[...] + (v1[...].astype(F32) + v2[...].astype(F32) + v3[...].astype(F32))
    out[...] = total.astype(BF16)


def in_vmem(kernel, shapes, *args, after=()):
    size = sum(x.size * x.dtype.itemsize for x in args)
    return pl.pallas_call(
        kernel,
        in_specs=[VMEM] * len(args) + [ANY] * len(after),
        out_specs=[VMEM] * len(shapes),
        out_shape=shapes,
        compiler_params=pltpu.CompilerParams(vmem_limit_bytes=16 * MIB),
        cost_estimate=cost(0, size),
    )(*args, *after)


def turn_kernel(info, *refs):
    blocks, (first, second, held, flat, sems) = refs[:8], refs[8:]
    c = info[0]
    shift = pl.multiple_of(512 * c, TILE)
    load_all(panel_copies(info, blocks, held, pl.ds(shift, WIDE)), sems)
    for r in range(ROWS // TILE):
        flat[:, r * TILE : (r + 1) * TILE] = held[r].T
    start = 128 * c
    first[: 2 * TILE, :ROWS] = flat[pl.ds(pl.multiple_of(start, 128), 2 * TILE), :]
    first[2 * TILE :, :ROWS] = flat[pl.ds(pl.multiple_of(512 - 448 * c, 64), 64), :]
    second[:, :ROWS] = flat[pl.ds(pl.multiple_of(start + 2 * TILE, 128), 2 * TILE), :]
    for out in (first, second):
        out[:, ROWS:] = out[:, :CHUNK]


def turned_panel(info, blocks):
    return pl.pallas_call(
        turn_kernel,
        in_specs=[SMEM] + [HBM] * 8,
        out_specs=[VMEM] * 2,
        out_shape=[jax.ShapeDtypeStruct((share, AROUND), BF16) for share in SHARES],
        scratch_shapes=[panel_shape(WIDE), pltpu.VMEM((WIDE, ROWS), BF16), pltpu.SemaphoreType.DMA((8,))],
        compiler_params=pltpu.CompilerParams(vmem_limit_bytes=24 * MIB),
        cost_estimate=cost(0, 1.2e7),
    )(info, *blocks)


SOURCES = ((0, 0), (0, 3), (0, 1), (1, 0), (1, 1), (1, 3), (0, 2), (1, 2))


def apply_kernel(info, *refs):
    own, ends, swapped = refs[:7], refs[7:10], refs[10:14]
    turned = refs[14]
    outs, all_direct, all_flipped, scales = refs[15:19], *refs[19:22]
    direct, flipped, panel, mixed, stage, extra, sems, panel_sem, out_sems, keep_sems = refs[22:]
    c = info[0]
    panel_copy = pltpu.make_async_copy(turned, panel, panel_sem)
    panel_copy.start()
    pieces = [(c, ref, 0, rel) for ref, rel in zip(own, SOURCES)]
    pieces += [(1 - c, swapped[0], 0, SOURCES[0]), (1 - c, swapped[3], 0, SOURCES[7])]
    pieces += [(1 - c, swapped[1 + n // 3], n % 3 * CHUNK, SOURCES[1 + n]) for n in range(6)]
    for n, (core, ref, row, rel) in enumerate(pieces):
        d = chip_at(info, *rel)

        @pl.loop(0, HALF_BLOCKS)
        def _(b):
            i = (core * HALF_BLOCKS + b + d) % BLOCKS
            src = ref.at[pl.ds(pl.multiple_of(row + b * SIDE, SIDE), SIDE)]
            pltpu.make_async_copy(src, direct.at[i, pl.ds(pl.multiple_of((7 - d) * SIDE, SIDE), SIDE)], sems.at[n]).start()

    d = chip_at(info, *SOURCES[7])
    last = []
    for ref, (row, size) in zip(ends, PARTS):
        for b in range(HALF_BLOCKS):
            low, high = max(row, b * SIDE), min(row + size, (b + 1) * SIDE)
            if low < high:
                i = (c * HALF_BLOCKS + b + d) % BLOCKS
                start = pl.multiple_of((7 - d) * SIDE + low - b * SIDE, 16)
                src = ref.at[low - row : high - row]
                last.append(pltpu.make_async_copy(src, direct.at[i, pl.ds(start, high - low)], sems.at[15 + len(last)]))
    for copy in last:
        copy.start()
    for n in range(15):
        whole = direct.at[0:HALF_BLOCKS, 0:SIDE]
        pltpu.make_async_copy(whole, whole, sems.at[n]).wait()
    for copy in last:
        copy.wait()
    panel_copy.wait()

    total = jnp.zeros((), F32)
    on = lax.broadcasted_iota(jnp.int32, (SIDE, SIDE), 0) == lax.broadcasted_iota(jnp.int32, (SIDE, SIDE), 1)
    diagonal = jnp.zeros((SIDE, SIDE), F32)
    for i in range(BLOCKS):
        diagonal += direct[i, 7 * SIDE :, :].astype(F32)
    total = jnp.sum(jnp.where(on, diagonal, 0.0))
    total = jnp.full((1, SIDE), total, F32)
    factor = math.sqrt(ROWS) / (2.0 * (jnp.sqrt(total) + EPSILON))
    square = factor * factor

    scale = math.sqrt(COLS) * factor
    scales[...] = jnp.concatenate([scale] * 4 + [square] * 4)
    keep = pltpu.make_async_copy(direct, all_direct, keep_sems.at[0])
    keep.start()

    def flip(i):
        for e in range(1, 7):
            far = (i + e) % BLOCKS
            flipped[i, (e - 1) * SIDE : e * SIDE, :] = direct[far, (7 - e) * SIDE : (8 - e) * SIDE, :].T

    first_product(square, panel, direct, flipped, mixed, flip)
    keep_more = pltpu.make_async_copy(flipped, all_flipped, keep_sems.at[1])
    keep_more.start()
    second_product(info, scale, square, panel, direct, flipped, mixed, stage, extra, outs, out_sems)
    keep.wait()
    keep_more.wait()


def gram_times(i, x, direct, flipped):
    first = pl.ds(pl.multiple_of((i + 7) % BLOCKS * SIDE, SIDE), 8 * SIDE)
    rest = pl.ds(pl.multiple_of((i + 1) % BLOCKS * SIDE, SIDE), 6 * SIDE)
    result = jnp.dot(x[:, first], direct[i], preferred_element_type=F32)
    return result + jnp.dot(x[:, rest], flipped[i], preferred_element_type=F32)


def first_product(square, panel, direct, flipped, mixed, ready):
    @pl.loop(0, BLOCKS)
    def _(i):
        ready(i)
        columns = pl.ds(pl.multiple_of(i * SIDE, SIDE), SIDE)
        product = gram_times(i, panel, direct, flipped) * square
        mix = (COEF_CUBIC * panel[:, columns].astype(F32) + COEF_QUINTIC * product).astype(BF16)
        mixed[:, columns] = mix

        @pl.when(i < HALF_BLOCKS)
        def _():
            mixed[:, pl.ds(pl.multiple_of(i * SIDE + ROWS, SIDE), SIDE)] = mix


def second_product(info, scale, square, panel, direct, flipped, mixed, stage, extra, outs, sems):
    c, a = info[0], info[2]
    sends = []
    for turn in range(2):
        half = 1 - c if turn else c

        @pl.loop(0, HALF_BLOCKS)
        def _(b):
            i = half * HALF_BLOCKS + b
            columns = pl.ds(pl.multiple_of(i * SIDE, SIDE), SIDE)
            product = gram_times(i, mixed, direct, flipped) * square
            result = scale * (COEF_LINEAR * panel[:, columns].astype(F32) + product)
            stage[turn, pl.ds(pl.multiple_of(b * SIDE, SIDE), SIDE)] = result.astype(BF16).T

        for side in range(2):
            out = outs[2 * turn + side]
            start = pl.multiple_of((1 - a if side else a) * HEIGHT, 128)
            pieces = [
                (stage.at[turn, pl.ds(start, HEIGHT), j * TILE : (j + 1) * TILE], out.at[pl.ds(j * HEIGHT, HEIGHT)])
                for j in range(2)
            ]
            if extra is not None:
                halves = [stage[turn, pl.ds(pl.multiple_of(start + row, 64), 448), 2 * TILE :] for row in (0, 448)]
                extra[2 * turn + side] = jnp.concatenate(halves, axis=1)
                pieces.append((extra.at[2 * turn + side], out.at[pl.ds(2 * HEIGHT, 448)]))
            for piece in pieces:
                sends.append(pltpu.make_async_copy(*piece, sems.at[len(sends)]))
                sends[-1].start()
    for send in sends:
        send.wait()


def rest_kernel(info, all_direct, all_flipped, turned, scales, *refs):
    outs, (direct, flipped, panel, mixed, stage, sems, panel_sem, out_sems) = refs[:4], refs[4:]

    def loads(i):
        return (
            pltpu.make_async_copy(all_direct.at[i], direct.at[i], sems.at[0, i]),
            pltpu.make_async_copy(all_flipped.at[i], flipped.at[i], sems.at[1, i]),
        )

    panel_copy = pltpu.make_async_copy(turned, panel, panel_sem)
    panel_copy.start()
    for i in range(BLOCKS):
        for load in loads(i):
            load.start()
    panel_copy.wait()
    scale, square = scales[0:1], scales[4:5]

    def arrive(i):
        for load in loads(i):
            load.wait()

    first_product(square, panel, direct, flipped, mixed, arrive)
    second_product(info, scale, square, panel, direct, flipped, mixed, stage, None, outs, out_sems)


def apply_rest(info, direct, flipped, scales, turned):
    share = SHARES[1]
    return pl.pallas_call(
        rest_kernel,
        in_specs=[SMEM] + [HBM] * 3 + [VMEM],
        out_specs=[HBM] * 4,
        out_shape=[jax.ShapeDtypeStruct((BACK_ROWS[1], TILE), BF16)] * 4,
        scratch_shapes=[
            pltpu.VMEM((BLOCKS, 8 * SIDE, SIDE), BF16),
            pltpu.VMEM((BLOCKS, 6 * SIDE, SIDE), BF16),
            pltpu.VMEM((share, AROUND), BF16),
            pltpu.VMEM((share, AROUND), BF16),
            pltpu.VMEM((2, CHUNK, share), BF16),
            pltpu.SemaphoreType.DMA((2, BLOCKS)),
            pltpu.SemaphoreType.DMA,
            pltpu.SemaphoreType.DMA((8,)),
        ],
        compiler_params=pltpu.CompilerParams(vmem_limit_bytes=58 * MIB),
        cost_estimate=cost(4 * ROWS * ROWS * share, 3e7),
    )(info, direct, flipped, turned, scales)


def apply_poly(info, own, ends, swapped, turned):
    share = SHARES[0]
    return pl.pallas_call(
        apply_kernel,
        in_specs=[SMEM] + [HBM] * 15,
        out_specs=[HBM] * 6 + [VMEM],
        out_shape=[jax.ShapeDtypeStruct((BACK_ROWS[0], TILE), BF16)] * 4
        + [
            jax.ShapeDtypeStruct((BLOCKS, 8 * SIDE, SIDE), BF16),
            jax.ShapeDtypeStruct((BLOCKS, 6 * SIDE, SIDE), BF16),
            jax.ShapeDtypeStruct((8, SIDE), F32),
        ],
        scratch_shapes=[
            pltpu.VMEM((BLOCKS, 8 * SIDE, SIDE), BF16),
            pltpu.VMEM((BLOCKS, 6 * SIDE, SIDE), BF16),
            pltpu.VMEM((share, AROUND), BF16),
            pltpu.VMEM((share, AROUND), BF16),
            pltpu.VMEM((2, CHUNK, share), BF16),
            pltpu.VMEM((4, 448, TILE), BF16),
            pltpu.SemaphoreType.DMA((32,)),
            pltpu.SemaphoreType.DMA,
            pltpu.SemaphoreType.DMA((12,)),
            pltpu.SemaphoreType.DMA((2,)),
        ],
        compiler_params=pltpu.CompilerParams(vmem_limit_bytes=58 * MIB),
        cost_estimate=cost(4 * ROWS * ROWS * share, 4e7),
    )(info, *own, *ends, *swapped, turned)


def unpack_kernel(info, *refs):
    firsts, seconds, update = refs[:4], refs[4:8], refs[8]
    m, a = info[1], info[2]
    for s in range(4):
        core = 1 - m if s >= 2 else m
        side = 1 - a if s % 2 else a
        for j in range(4):
            start = pl.multiple_of((9 * side + j + 5 * core) * TILE, TILE)
            got = (firsts, seconds)[j // 2][s]
            update[:, pl.ds(start, TILE)] = got[j % 2 * HEIGHT : (j % 2 + 1) * HEIGHT]
    for s in range(2):
        side = 1 - a if s else a
        one, two = firsts[s][2 * HEIGHT :], firsts[s + 2][2 * HEIGHT :]
        low, high = jnp.where(m == 0, one, two), jnp.where(m == 0, two, one)
        tile = pl.ds(pl.multiple_of((9 * side + 4) * TILE, TILE), TILE)
        update[:448, tile] = jnp.concatenate([low[:, :64], high[:, :64]], axis=1)
        update[448:, tile] = jnp.concatenate([low[:, 64:], high[:, 64:]], axis=1)


def unpack(info, parts):
    return pl.pallas_call(
        unpack_kernel,
        in_specs=[SMEM] + [VMEM] * 8,
        out_specs=VMEM,
        out_shape=jax.ShapeDtypeStruct((HEIGHT, 2304), BF16),
        compiler_params=pltpu.CompilerParams(vmem_limit_bytes=32 * MIB),
        cost_estimate=cost(0, 8.3e6),
    )(info, *parts)


def on_device(grad_tiles, tile_ids, momentum):
    core, zm, zl, y = (lax.axis_index(name) for name in AXES[1:])
    info = jnp.stack([core, zm, zl, y]).astype(jnp.int32)
    tile_count = grad_tiles.shape[0]

    upper, lower = pack(tile_ids, grad_tiles)
    upper = lax.all_to_all(upper, PLANE, split_axis=0, concat_axis=0, tiled=True)
    lower, _ = lax.optimization_barrier((lower, upper))
    lower = lax.all_to_all(lower, PLANE, split_axis=0, concat_axis=0, tiled=True)

    got_labels = upper[:, -1, 0].astype(jnp.int32)
    found = got_labels[None, :] == jnp.arange(tile_count, dtype=jnp.int32)[:, None]
    sources = jnp.sum(jnp.where(found, jnp.arange(16, dtype=jnp.int32)[None, :], 0), axis=1)
    details = jnp.concatenate([sources, zl[None].astype(jnp.int32)])
    new_momentum, *halves0 = update_momentum(details, upper, momentum, 0, None)
    new_momentum, *halves1 = update_momentum(details, lower, momentum, 1, new_momentum)

    def to_panel(halves):
        half0, half1 = halves
        return (
            move(half0, lambda c, m, a, y: (m, c, a, y)),
            move(half1, lambda c, m, a, y: (m, c, 1 - a, y)),
        )

    got0, got1 = to_panel(halves0), to_panel(halves1)
    blocks = (got0[0], got1[0], got0[1], got1[1])
    blocks += tuple(swap(x) for x in blocks)

    far = gram_chunks(info, blocks, ((1, 2),), [chunk(BF16, size) for _, size in PARTS])
    far0, far1, far2 = up(far[0]), down(far[1]), across(far[2])
    terms = gram_chunks(info, blocks, ((1, 1), (1, 3), (0, 2)), [chunk(F32)] * 3)
    q1, q2, q3 = in_vmem(second_sums_kernel, [chunk()] * 3, *terms, far0, far1, far2)
    g1, g2, g3 = across(q1), down(q2), up(q3)
    later, _ = lax.optimization_barrier((blocks, q1))
    nearest, beside, below, center = gram_chunks(
        info, later, ((0, 1), (1, 0), (0, 3), (0, 0)), [chunk(F32), chunk(F32), chunk(), chunk(F32)]
    )
    near = down(below)
    v1, v2 = in_vmem(third_sums_kernel, [chunk()] * 2, nearest, beside, g1, g2, g3)
    w1, w2 = up(v1), across(v2)
    later, _ = lax.optimization_barrier((blocks, v1))
    turned = turned_panel(info, later)
    (mine,) = in_vmem(last_sums_kernel, [chunk()], center, w1, w2, near, after=turned)

    low, high, pair = up(mine), down(mine), across(mine)
    a1, a2, a3 = across(high), up(pair), down(high)
    ends = tuple(
        send(x[row : row + size]) for send, x, (row, size) in zip((down, up, across), (a1, a2, a3), PARTS)
    )
    swapped = (
        swap(mine),
        swap(jnp.concatenate([low, high, pair])),
        swap(jnp.concatenate([a1, a2, a3])),
        swap(jnp.concatenate(ends)),
    )
    *sent, direct, flipped, scales = apply_poly(
        info, (mine, low, high, pair, a1, a2, a3), ends, swapped, turned[0]
    )

    def to_owners(sent):
        return (
            move(sent[0], lambda c, m, a, y: (m, c, a, y)),
            move(sent[1], lambda c, m, a, y: (m, c, 1 - a, y)),
            move(sent[2], lambda c, m, a, y: (m, 1 - c, a, y)),
            move(sent[3], lambda c, m, a, y: (m, 1 - c, 1 - a, y)),
        )

    firsts = to_owners(sent)
    sent = apply_rest(info, direct, flipped, scales, turned[1])
    sent, firsts = lax.optimization_barrier((sent, firsts))
    return new_momentum, unpack(info, firsts + to_owners(sent))


def solution(mesh):
    fine = Mesh(mesh.devices.reshape(4, 2, 2, 2, 4), AXES)
    tall = P(("x", "core", "zm", "zl"), "y")
    return jax.shard_map(
        on_device,
        mesh=fine,
        in_specs=(P(AXES, None, None), P(AXES), tall),
        out_specs=(tall, tall),
        check_vma=False,
    )
```

```python
import math

import jax
import jax.numpy as jnp
from jax import lax
from jax.experimental import pallas as pl
from jax.experimental.pallas import tpu as pltpu
from jax.sharding import Mesh
from jax.sharding import PartitionSpec as P

ROWS = 3584
COLS = 9216
MOMENTUM_RATE = 0.95
COEF_LINEAR = 3.4445
COEF_CUBIC = -4.775
COEF_QUINTIC = 2.0315
EPSILON = 1e-06

HEIGHT = 896
HALF = 1152
TILE = 128
SPLIT = ((0, 80), (80, 48))
LABEL = 16
SIDE = 256
BLOCKS = ROWS // SIDE
HALF_BLOCKS = BLOCKS // 2
CHUNK = HALF_BLOCKS * SIDE
PARTS = ((0, 608), (608, 592), (1200, 592))
WIDE = 640
SHARE = 576
AROUND = ROWS + CHUNK
BACK_ROWS = 4032

AXES = ("x", "core", "zm", "zl", "y")
PLANE = ("zm", "zl", "y")
BF16 = jnp.bfloat16
F32 = jnp.float32
MIB = 1 << 20
ANY = pl.BlockSpec(memory_space=pl.ANY)
HBM = pl.BlockSpec(memory_space=pltpu.HBM)
VMEM = pl.BlockSpec(memory_space=pltpu.VMEM)
SMEM = pl.BlockSpec(memory_space=pltpu.SMEM)


def cost(flops, size):
    return pl.CostEstimate(flops=int(flops), bytes_accessed=int(size), transcendentals=0)


def move(x, route):
    pairs = []
    for c in range(2):
        for m in range(2):
            for a in range(2):
                for y in range(4):
                    c2, m2, a2, y2 = route(c, m, a, y)
                    pairs.append((((c * 2 + m) * 2 + a) * 4 + y, ((c2 * 2 + m2) * 2 + a2) * 4 + y2 % 4))
    return lax.ppermute(x, AXES[1:], pairs)


def up(x):
    return move(x, lambda c, m, a, y: (c, m, a, y + 1))


def down(x):
    return move(x, lambda c, m, a, y: (c, m, a, y + 3))


def across(x):
    return move(x, lambda c, m, a, y: (c, m, 1 - a, y))


def swap(x):
    return move(x, lambda c, m, a, y: (1 - c, m, a, y))


def pack_kernel(ids, tiles, upper, lower, slots, places, held, first, second, sems, out_sems):
    n = tiles.shape[0]
    loads = [pltpu.make_async_copy(tiles.at[i], held.at[i], sems.at[i]) for i in range(n)]
    for load in loads:
        load.start()
    for o in range(upper.shape[0]):
        slots[o] = 0
        places[o] = -1

    @pl.loop(0, n)
    def _(i):
        row, column = ids[i] // 8, ids[i] % 8
        owner = row // 7 * 4 + column // 2
        slots[owner] = i
        places[owner] = row % 7 * 2 + column % 2

    for load in loads:
        load.wait()

    def copies(o):
        return (
            pltpu.make_async_copy(first.at[o], upper.at[o], out_sems.at[0, o]),
            pltpu.make_async_copy(second.at[o], lower.at[o], out_sems.at[1, o]),
        )

    @pl.loop(0, upper.shape[0])
    def _(o):
        slot = slots[o]
        for j in range(HALF // TILE):
            piece = held[slot, :, j * TILE : (j + 1) * TILE]
            for (row, size), out in zip(SPLIT, (first, second)):
                out[o, j * size : (j + 1) * size, :] = piece[row : row + size]
        place = jnp.full((LABEL, TILE), places[o], jnp.int32)
        first[o, first.shape[1] - LABEL :, :] = place.astype(F32).astype(BF16)
        for copy in copies(o):
            copy.start()

    @pl.loop(0, upper.shape[0])
    def _(o):
        for copy in copies(o):
            copy.wait()


def pack(ids, tiles):
    n = 16
    rows = [HALF // TILE * size for _, size in SPLIT]
    shapes = [(n, rows[0] + LABEL, TILE), (n, rows[1], TILE)]
    return pl.pallas_call(
        pack_kernel,
        in_specs=[SMEM, HBM],
        out_specs=[HBM] * 2,
        out_shape=[jax.ShapeDtypeStruct(shape, BF16) for shape in shapes],
        scratch_shapes=[pltpu.SMEM((n,), jnp.int32)] * 2
        + [pltpu.VMEM(tiles.shape, BF16)]
        + [pltpu.VMEM(shape, BF16) for shape in shapes]
        + [pltpu.SemaphoreType.DMA((tiles.shape[0],)), pltpu.SemaphoreType.DMA((2, n))],
        compiler_params=pltpu.CompilerParams(vmem_limit_bytes=62 * MIB),
        cost_estimate=cost(0, 4 * tiles.size),
    )(ids, tiles)


def momentum_kernel(part, info, arrived, momentum, *refs):
    new, half0, half1, tile, old, fresh, rounded, in_sems, out_sems = refs[-9:]
    n = HEIGHT // TILE
    row, size = SPLIT[part]

    def place(t, r):
        half = (t + info[14]) % 2
        columns = pl.ds(pl.multiple_of(half * HALF, TILE), HALF)
        return pl.ds(pl.multiple_of(r * TILE + row, 16), size), columns

    def reads(t, r):
        source = info[2 * r + (t + info[14]) % 2]
        i = t * n + r
        return (
            pltpu.make_async_copy(momentum.at[place(t, r)], old.at[i], in_sems.at[0, i]),
            pltpu.make_async_copy(arrived.at[source, 0 : HALF // TILE * size], tile.at[i], in_sems.at[1, i]),
        )

    def writes(t, r):
        i = t * n + r
        out = (half0, half1)[t].at[r]
        return (
            pltpu.make_async_copy(fresh.at[i], new.at[place(t, r)], out_sems.at[0, i]),
            pltpu.make_async_copy(rounded.at[i], out, out_sems.at[1, i]),
        )

    for t in range(2):
        for r in range(n):
            for copy in reads(t, r):
                copy.start()
    for t in range(2):

        @pl.loop(0, n)
        def _(r):
            i = t * n + r
            for copy in reads(t, r):
                copy.wait()
            for j in range(HALF // TILE):
                columns = slice(j * TILE, (j + 1) * TILE)
                g = tile[i, j * size : (j + 1) * size, :].astype(F32)
                later = MOMENTUM_RATE * old[i, :, columns] + g
                fresh[i, :, columns] = later
                rounded[i, :, columns] = (g + MOMENTUM_RATE * later).astype(BF16)
            for copy in writes(t, r):
                copy.start()

    for t in range(2):

        @pl.loop(0, n)
        def _(r):
            for copy in writes(t, r):
                copy.wait()


def update_momentum(info, arrived, momentum, part, so_far):
    more = () if so_far is None else (so_far,)
    n = 2 * HEIGHT // TILE
    size = SPLIT[part][1]
    return pl.pallas_call(
        lambda *refs: momentum_kernel(part, *refs),
        in_specs=[SMEM] + [HBM] * (2 + len(more)),
        out_specs=[HBM] * 3,
        out_shape=[
            jax.ShapeDtypeStruct(momentum.shape, F32),
            jax.ShapeDtypeStruct((n // 2, size, HALF), BF16),
            jax.ShapeDtypeStruct((n // 2, size, HALF), BF16),
        ],
        scratch_shapes=[
            pltpu.VMEM((n, HALF // TILE * size, TILE), BF16),
            pltpu.VMEM((n, size, HALF), F32),
            pltpu.VMEM((n, size, HALF), F32),
            pltpu.VMEM((n, size, HALF), BF16),
            pltpu.SemaphoreType.DMA((2, n)),
            pltpu.SemaphoreType.DMA((2, n)),
        ],
        input_output_aliases={3: 0} if more else {},
        compiler_params=pltpu.CompilerParams(vmem_limit_bytes=62 * MIB),
        cost_estimate=cost(0, HEIGHT * HALF * 12),
    )(info, arrived, momentum, *more)


def panel_copies(info, blocks, panel, columns=None):
    c, a = info[0], info[2]
    copies = []
    for i, block in enumerate(blocks):
        other, t, part = i // 4, i // 2 % 2, i % 2
        core = 1 - c if other else c
        z = 2 * core + (a + t) % 2
        src = block if columns is None else block.at[:, :, columns]
        row, size = SPLIT[part]
        rows = pl.ds(z * (HEIGHT // TILE), HEIGHT // TILE)
        copies.append((src, panel.at[rows, row : row + size]))
    return copies


def panel_shape(width):
    return pltpu.VMEM((ROWS // TILE, TILE, width), BF16)


def chip_at(info, flip, dy):
    a, y = info[2], info[3]
    return (1 - a if flip else a) * 4 + (y + dy) % 4


def load_all(copies, sems):
    copies = [pltpu.make_async_copy(src, dst, sems.at[i]) for i, (src, dst) in enumerate(copies)]
    for copy in copies:
        copy.start()
    for copy in copies:
        copy.wait()


def gram_kernel(dests, info, *refs):
    blocks, outs = refs[:8], refs[8:-2]
    panel, sems = refs[-2:]
    load_all(panel_copies(info, blocks, panel), sems)

    def term(b, d):
        left = panel[pl.ds(2 * b, 2)].reshape(SIDE, HALF)
        right = panel[pl.ds(2 * ((b + d) % BLOCKS), 2)].reshape(SIDE, HALF)
        return lax.dot_general(left, right, (((1,), (1,)), ((), ())), preferred_element_type=F32)

    base = HALF_BLOCKS * info[0]
    if len(dests) == 1:
        d = chip_at(info, *dests[0])
        for b in range(HALF_BLOCKS):
            block = term(base + b, d).astype(BF16)
            for out, (row, size) in zip(outs, PARTS):
                low, high = max(row, b * SIDE), min(row + size, (b + 1) * SIDE)
                if low < high:
                    out[low - row : high - row] = block[low - b * SIDE : high - b * SIDE]
    else:

        @pl.loop(0, HALF_BLOCKS)
        def _(b):
            for dest, out in zip(dests, outs):
                block = term(base + b, chip_at(info, *dest))
                out[pl.ds(pl.multiple_of(b * SIDE, SIDE), SIDE)] = block.astype(out.dtype)


def gram_chunks(info, blocks, dests, shapes):
    return pl.pallas_call(
        lambda *refs: gram_kernel(dests, *refs),
        in_specs=[SMEM] + [HBM] * 8,
        out_specs=[VMEM] * len(shapes),
        out_shape=shapes,
        scratch_shapes=[panel_shape(HALF), pltpu.SemaphoreType.DMA((8,))],
        compiler_params=pltpu.CompilerParams(vmem_limit_bytes=24 * MIB),
        cost_estimate=cost(len(dests) * 2 * CHUNK * SIDE * HALF, 8.3e6 + len(dests) * CHUNK * SIDE * 4),
    )(info, *blocks)


def chunk(dtype=BF16, rows=CHUNK):
    return jax.ShapeDtypeStruct((rows, SIDE), dtype)


def second_sums_kernel(p1, p2, p3, r1, r2, r3, q1, q2, q3):
    for own, got, out, (row, size) in zip((p1, p2, p3), (r1, r2, r3), (q1, q2, q3), PARTS):
        if row:
            out[:row] = own[:row].astype(BF16)
        out[row : row + size] = (own[row : row + size] + got[...].astype(F32)).astype(BF16)
        if row + size < CHUNK:
            out[row + size :] = own[row + size :].astype(BF16)


def third_sums_kernel(p1, p2, g1, g2, g3, v1, v2):
    v1[...] = (p1[...] + (g1[...].astype(F32) + g3[...].astype(F32))).astype(BF16)
    v2[...] = (p2[...] + g2[...].astype(F32)).astype(BF16)


def last_sums_kernel(p, v1, v2, v3, turned, out):
    total = p[...] + (v1[...].astype(F32) + v2[...].astype(F32) + v3[...].astype(F32))
    out[...] = total.astype(BF16)


def in_vmem(kernel, shapes, *args, after=()):
    size = sum(x.size * x.dtype.itemsize for x in args)
    return pl.pallas_call(
        kernel,
        in_specs=[VMEM] * len(args) + [ANY] * len(after),
        out_specs=[VMEM] * len(shapes),
        out_shape=shapes,
        compiler_params=pltpu.CompilerParams(vmem_limit_bytes=16 * MIB),
        cost_estimate=cost(0, size),
    )(*args, *after)


def turn_kernel(info, *refs):
    blocks, out, held, flat, sems = refs[:8], *refs[8:]
    c = info[0]
    shift = pl.multiple_of(512 * c, TILE)
    load_all(panel_copies(info, blocks, held, pl.ds(shift, WIDE)), sems)
    for r in range(ROWS // TILE):
        flat[:, r * TILE : (r + 1) * TILE] = held[r].T
    out[:512, :ROWS] = flat[pl.ds(pl.multiple_of(128 * c, 64), 512), :]
    out[512:, :ROWS] = flat[pl.ds(pl.multiple_of(512 - 448 * c, 64), 64), :]
    out[:, ROWS:] = out[:, :CHUNK]


def turned_panel(info, blocks):
    return pl.pallas_call(
        turn_kernel,
        in_specs=[SMEM] + [HBM] * 8,
        out_specs=VMEM,
        out_shape=jax.ShapeDtypeStruct((SHARE, AROUND), BF16),
        scratch_shapes=[panel_shape(WIDE), pltpu.VMEM((WIDE, ROWS), BF16), pltpu.SemaphoreType.DMA((8,))],
        compiler_params=pltpu.CompilerParams(vmem_limit_bytes=24 * MIB),
        cost_estimate=cost(0, 1.2e7),
    )(info, *blocks)


SOURCES = ((0, 0), (0, 3), (0, 1), (1, 0), (1, 1), (1, 3), (0, 2), (1, 2))


def apply_kernel(info, *refs):
    own, ends, swapped = refs[:7], refs[7:10], refs[10:14]
    turned = refs[14]
    outs, rest_direct, rest_flipped, all_mixed, scales = refs[15:17], *refs[17:21]
    direct, flipped, panel, mixed, stage, extra, sems, panel_sem, out_sems, keep_sems = refs[21:]
    c = info[0]
    panel_copy = pltpu.make_async_copy(turned, panel, panel_sem)
    panel_copy.start()
    pieces = [(c, ref, 0, rel) for ref, rel in zip(own, SOURCES)]
    pieces += [(1 - c, swapped[0], 0, SOURCES[0]), (1 - c, swapped[3], 0, SOURCES[7])]
    pieces += [(1 - c, swapped[1 + n // 3], n % 3 * CHUNK, SOURCES[1 + n]) for n in range(6)]
    for n, (core, ref, row, rel) in enumerate(pieces):
        d = chip_at(info, *rel)

        @pl.loop(0, HALF_BLOCKS)
        def _(b):
            i = (core * HALF_BLOCKS + b + d) % BLOCKS
            src = ref.at[pl.ds(pl.multiple_of(row + b * SIDE, SIDE), SIDE)]
            pltpu.make_async_copy(src, direct.at[i, pl.ds(pl.multiple_of((7 - d) * SIDE, SIDE), SIDE)], sems.at[n]).start()

    d = chip_at(info, *SOURCES[7])
    last = []
    for ref, (row, size) in zip(ends, PARTS):
        for b in range(HALF_BLOCKS):
            low, high = max(row, b * SIDE), min(row + size, (b + 1) * SIDE)
            if low < high:
                i = (c * HALF_BLOCKS + b + d) % BLOCKS
                start = pl.multiple_of((7 - d) * SIDE + low - b * SIDE, 16)
                src = ref.at[low - row : high - row]
                last.append(pltpu.make_async_copy(src, direct.at[i, pl.ds(start, high - low)], sems.at[15 + len(last)]))
    for copy in last:
        copy.start()
    for n in range(15):
        whole = direct.at[0:HALF_BLOCKS, 0:SIDE]
        pltpu.make_async_copy(whole, whole, sems.at[n]).wait()
    for copy in last:
        copy.wait()
    panel_copy.wait()

    total = jnp.zeros((), F32)
    on = lax.broadcasted_iota(jnp.int32, (SIDE, SIDE), 0) == lax.broadcasted_iota(jnp.int32, (SIDE, SIDE), 1)
    diagonal = jnp.zeros((SIDE, SIDE), F32)
    for i in range(BLOCKS):
        diagonal += direct[i, 7 * SIDE :, :].astype(F32)
    total = jnp.sum(jnp.where(on, diagonal, 0.0))
    total = jnp.full((1, SIDE), total, F32)
    factor = math.sqrt(ROWS) / (2.0 * (jnp.sqrt(total) + EPSILON))
    square = factor * factor

    def product(i, x):
        return gram_times(i, x, direct.at[i], flipped.at[i]) * square

    @pl.loop(0, BLOCKS)
    def _(i):
        for e in range(1, 7):
            far = (i + e) % BLOCKS
            flipped[i, (e - 1) * SIDE : e * SIDE, :] = direct[far, (7 - e) * SIDE : (8 - e) * SIDE, :].T
        columns = pl.ds(pl.multiple_of(i * SIDE, SIDE), SIDE)
        mix = COEF_CUBIC * panel[:, columns].astype(F32) + COEF_QUINTIC * product(i, panel)
        mix = mix.astype(BF16)
        mixed[:, columns] = mix

        @pl.when(i < HALF_BLOCKS)
        def _():
            mixed[:, pl.ds(pl.multiple_of(i * SIDE + ROWS, SIDE), SIDE)] = mix

    other = (1 - c) * HALF_BLOCKS
    scale = math.sqrt(COLS) * factor
    scales[...] = jnp.concatenate([scale] * 4 + [square] * 4)
    keeps = [
        pltpu.make_async_copy(direct.at[pl.ds(other, HALF_BLOCKS)], rest_direct, keep_sems.at[0]),
        pltpu.make_async_copy(flipped.at[pl.ds(other, HALF_BLOCKS)], rest_flipped, keep_sems.at[1]),
        pltpu.make_async_copy(mixed, all_mixed, keep_sems.at[2]),
    ]
    for copy in keeps:
        copy.start()

    @pl.loop(0, HALF_BLOCKS)
    def _(b):
        i = c * HALF_BLOCKS + b
        columns = pl.ds(pl.multiple_of(i * SIDE, SIDE), SIDE)
        result = scale * (COEF_LINEAR * panel[:, columns].astype(F32) + product(i, mixed))
        stage[pl.ds(pl.multiple_of(b * SIDE, SIDE), SIDE)] = result.astype(BF16).T

    send_back(info, stage, extra, outs, out_sems)
    for copy in keeps:
        copy.wait()


def gram_times(i, x, direct, flipped):
    first = pl.ds(pl.multiple_of((i + 7) % BLOCKS * SIDE, SIDE), 8 * SIDE)
    rest = pl.ds(pl.multiple_of((i + 1) % BLOCKS * SIDE, SIDE), 6 * SIDE)
    result = jnp.dot(x[:, first], direct[...], preferred_element_type=F32)
    return result + jnp.dot(x[:, rest], flipped[...], preferred_element_type=F32)


def send_back(info, stage, extra, outs, sems):
    a = info[2]
    sends = []
    for side, out in enumerate(outs):
        owner = 1 - a if side else a
        start = pl.multiple_of(owner * HEIGHT, 128)
        for j in range(4):
            rows = pl.ds(start, HEIGHT)
            sends.append((stage.at[rows, j * TILE : (j + 1) * TILE], out.at[pl.ds(j * HEIGHT, HEIGHT)]))
        halves = [stage[pl.ds(pl.multiple_of(start + row, 64), 448), 512:] for row in (0, 448)]
        extra[side] = jnp.concatenate(halves, axis=1)
        sends.append((extra.at[side], out.at[pl.ds(4 * HEIGHT, 448)]))
    load_all(sends, sems)


def rest_kernel(info, direct, flipped, panel, all_mixed, scales, out0, out1, mixed, stage, extra, sems):
    b = pl.program_id(0)

    @pl.when(b == 0)
    def _():
        load_all([(all_mixed, mixed)], sems)

    i = (1 - info[0]) * HALF_BLOCKS + b
    product = gram_times(i, mixed, direct.at[0], flipped.at[0]) * scales[4:5]
    result = scales[0:1] * (COEF_LINEAR * panel[...].astype(F32) + product)
    stage[pl.ds(pl.multiple_of(b * SIDE, SIDE), SIDE)] = result.astype(BF16).T

    @pl.when(b == HALF_BLOCKS - 1)
    def _():
        send_back(info, stage, extra, (out0, out1), sems)


def apply_rest(info, direct, flipped, mixed, scales, turned):
    return pl.pallas_call(
        rest_kernel,
        grid_spec=pltpu.PrefetchScalarGridSpec(
            num_scalar_prefetch=1,
            grid=(HALF_BLOCKS,),
            in_specs=[
                pl.BlockSpec((1, 8 * SIDE, SIDE), lambda b, s: (b, 0, 0)),
                pl.BlockSpec((1, 6 * SIDE, SIDE), lambda b, s: (b, 0, 0)),
                pl.BlockSpec((SHARE, SIDE), lambda b, s: (0, (1 - s[0]) * HALF_BLOCKS + b)),
                HBM,
                VMEM,
            ],
            out_specs=[HBM] * 2,
            scratch_shapes=[
                pltpu.VMEM((SHARE, AROUND), BF16),
                pltpu.VMEM((CHUNK, SHARE), BF16),
                pltpu.VMEM((2, 448, TILE), BF16),
                pltpu.SemaphoreType.DMA((10,)),
            ],
        ),
        out_shape=[jax.ShapeDtypeStruct((BACK_ROWS, TILE), BF16)] * 2,
        compiler_params=pltpu.CompilerParams(vmem_limit_bytes=62 * MIB),
        cost_estimate=cost(ROWS * ROWS * SHARE, 2e7),
    )(info, direct, flipped, turned, mixed, scales)


def apply_poly(info, own, ends, swapped, turned):
    return pl.pallas_call(
        apply_kernel,
        in_specs=[SMEM] + [HBM] * 15,
        out_specs=[HBM] * 5 + [VMEM],
        out_shape=[jax.ShapeDtypeStruct((BACK_ROWS, TILE), BF16)] * 2
        + [
            jax.ShapeDtypeStruct((HALF_BLOCKS, 8 * SIDE, SIDE), BF16),
            jax.ShapeDtypeStruct((HALF_BLOCKS, 6 * SIDE, SIDE), BF16),
            jax.ShapeDtypeStruct((SHARE, AROUND), BF16),
            jax.ShapeDtypeStruct((8, SIDE), F32),
        ],
        scratch_shapes=[
            pltpu.VMEM((BLOCKS, 8 * SIDE, SIDE), BF16),
            pltpu.VMEM((BLOCKS, 6 * SIDE, SIDE), BF16),
            pltpu.VMEM((SHARE, AROUND), BF16),
            pltpu.VMEM((SHARE, AROUND), BF16),
            pltpu.VMEM((CHUNK, SHARE), BF16),
            pltpu.VMEM((2, 448, TILE), BF16),
            pltpu.SemaphoreType.DMA((32,)),
            pltpu.SemaphoreType.DMA,
            pltpu.SemaphoreType.DMA((10,)),
            pltpu.SemaphoreType.DMA((3,)),
        ],
        compiler_params=pltpu.CompilerParams(vmem_limit_bytes=58 * MIB),
        cost_estimate=cost(3 * ROWS * ROWS * SHARE, 4e7),
    )(info, *own, *ends, *swapped, turned)


def unpack_kernel(info, r0, r1, r2, r3, update):
    m, a = info[1], info[2]
    for s, got in enumerate((r0, r1, r2, r3)):
        core = 1 - m if s >= 2 else m
        side = 1 - a if s % 2 else a
        for j in range(4):
            start = pl.multiple_of((9 * side + j + 5 * core) * TILE, TILE)
            update[:, pl.ds(start, TILE)] = got[j * HEIGHT : (j + 1) * HEIGHT]
    for s, (one, two) in enumerate(((r0, r2), (r1, r3))):
        side = 1 - a if s else a
        one, two = one[4 * HEIGHT :], two[4 * HEIGHT :]
        low, high = jnp.where(m == 0, one, two), jnp.where(m == 0, two, one)
        tile = pl.ds(pl.multiple_of((9 * side + 4) * TILE, TILE), TILE)
        update[:448, tile] = jnp.concatenate([low[:, :64], high[:, :64]], axis=1)
        update[448:, tile] = jnp.concatenate([low[:, 64:], high[:, 64:]], axis=1)


def unpack(info, parts):
    return pl.pallas_call(
        unpack_kernel,
        in_specs=[SMEM] + [VMEM] * 4,
        out_specs=VMEM,
        out_shape=jax.ShapeDtypeStruct((HEIGHT, 2304), BF16),
        compiler_params=pltpu.CompilerParams(vmem_limit_bytes=32 * MIB),
        cost_estimate=cost(0, 8.3e6),
    )(info, *parts)


def on_device(grad_tiles, tile_ids, momentum):
    core, zm, zl, y = (lax.axis_index(name) for name in AXES[1:])
    info = jnp.stack([core, zm, zl, y]).astype(jnp.int32)
    tile_count = grad_tiles.shape[0]

    upper, lower = pack(tile_ids, grad_tiles)
    upper = lax.all_to_all(upper, PLANE, split_axis=0, concat_axis=0, tiled=True)
    lower, _ = lax.optimization_barrier((lower, upper))
    lower = lax.all_to_all(lower, PLANE, split_axis=0, concat_axis=0, tiled=True)

    got_labels = upper[:, -1, 0].astype(jnp.int32)
    found = got_labels[None, :] == jnp.arange(tile_count, dtype=jnp.int32)[:, None]
    sources = jnp.sum(jnp.where(found, jnp.arange(16, dtype=jnp.int32)[None, :], 0), axis=1)
    details = jnp.concatenate([sources, zl[None].astype(jnp.int32)])
    new_momentum, *halves0 = update_momentum(details, upper, momentum, 0, None)
    new_momentum, *halves1 = update_momentum(details, lower, momentum, 1, new_momentum)

    def to_panel(halves):
        half0, half1 = halves
        return (
            move(half0, lambda c, m, a, y: (m, c, a, y)),
            move(half1, lambda c, m, a, y: (m, c, 1 - a, y)),
        )

    got0, got1 = to_panel(halves0), to_panel(halves1)
    blocks = (got0[0], got1[0], got0[1], got1[1])
    blocks += tuple(swap(x) for x in blocks)

    far = gram_chunks(info, blocks, ((1, 2),), [chunk(BF16, size) for _, size in PARTS])
    far0, far1, far2 = up(far[0]), down(far[1]), across(far[2])
    terms = gram_chunks(info, blocks, ((1, 1), (1, 3), (0, 2)), [chunk(F32)] * 3)
    q1, q2, q3 = in_vmem(second_sums_kernel, [chunk()] * 3, *terms, far0, far1, far2)
    g1, g2, g3 = across(q1), down(q2), up(q3)
    later, _ = lax.optimization_barrier((blocks, q1))
    nearest, beside, below, center = gram_chunks(
        info, later, ((0, 1), (1, 0), (0, 3), (0, 0)), [chunk(F32), chunk(F32), chunk(), chunk(F32)]
    )
    near = down(below)
    v1, v2 = in_vmem(third_sums_kernel, [chunk()] * 2, nearest, beside, g1, g2, g3)
    w1, w2 = up(v1), across(v2)
    later, _ = lax.optimization_barrier((blocks, v1))
    turned = turned_panel(info, later)
    (mine,) = in_vmem(last_sums_kernel, [chunk()], center, w1, w2, near, after=(turned,))

    low, high, pair = up(mine), down(mine), across(mine)
    a1, a2, a3 = across(high), up(pair), down(high)
    swap_mine, swap_near = swap(mine), swap(jnp.concatenate([low, high, pair]))
    a1, a2, a3, swap_near = lax.optimization_barrier((a1, a2, a3, swap_near))
    ends = tuple(
        send(x[row : row + size]) for send, x, (row, size) in zip((down, up, across), (a1, a2, a3), PARTS)
    )
    swap_far = swap(jnp.concatenate([a1, a2, a3]))
    ends, swap_far = lax.optimization_barrier((ends, swap_far))
    swapped = (swap_mine, swap_near, swap_far, swap(jnp.concatenate(ends)))
    *sent, direct, flipped, mixed, scales = apply_poly(info, (mine, low, high, pair, a1, a2, a3), ends, swapped, turned)
    sent += apply_rest(info, direct, flipped, mixed, scales, turned)

    parts = (
        move(sent[0], lambda c, m, a, y: (m, c, a, y)),
        move(sent[1], lambda c, m, a, y: (m, c, 1 - a, y)),
        move(sent[2], lambda c, m, a, y: (m, 1 - c, a, y)),
        move(sent[3], lambda c, m, a, y: (m, 1 - c, 1 - a, y)),
    )
    return new_momentum, unpack(info, parts)


def solution(mesh):
    fine = Mesh(mesh.devices.reshape(4, 2, 2, 2, 4), AXES)
    tall = P(("x", "core", "zm", "zl"), "y")
    return jax.shard_map(
        on_device,
        mesh=fine,
        in_specs=(P(AXES, None, None), P(AXES), tall),
        out_specs=(tall, tall),
        check_vma=False,
    )
```

```python
import math

import jax
import jax.numpy as jnp
from jax import lax
from jax.experimental import pallas as pl
from jax.experimental.pallas import tpu as pltpu
from jax.sharding import Mesh
from jax.sharding import PartitionSpec as P

ROWS = 3584
COLS = 9216
MOMENTUM_RATE = 0.95
COEF_LINEAR = 3.4445
COEF_CUBIC = -4.775
COEF_QUINTIC = 2.0315
EPSILON = 1e-06

HEIGHT = 896
HALF = 1152
TILE = 128
SPLIT = ((0, 80), (80, 48))
LABEL = 16
SIDE = 256
BLOCKS = ROWS // SIDE
HALF_BLOCKS = BLOCKS // 2
CHUNK = HALF_BLOCKS * SIDE
PARTS = ((0, 608), (608, 592), (1200, 592))
WIDE = 640
SHARE = 576
AROUND = ROWS + CHUNK
BACK_ROWS = 4032

AXES = ("x", "core", "zm", "zl", "y")
PLANE = ("zm", "zl", "y")
BF16 = jnp.bfloat16
F32 = jnp.float32
MIB = 1 << 20
ANY = pl.BlockSpec(memory_space=pl.ANY)
HBM = pl.BlockSpec(memory_space=pltpu.HBM)
VMEM = pl.BlockSpec(memory_space=pltpu.VMEM)
SMEM = pl.BlockSpec(memory_space=pltpu.SMEM)


def cost(flops, size):
    return pl.CostEstimate(flops=int(flops), bytes_accessed=int(size), transcendentals=0)


def move(x, route):
    pairs = []
    for c in range(2):
        for m in range(2):
            for a in range(2):
                for y in range(4):
                    c2, m2, a2, y2 = route(c, m, a, y)
                    pairs.append((((c * 2 + m) * 2 + a) * 4 + y, ((c2 * 2 + m2) * 2 + a2) * 4 + y2 % 4))
    return lax.ppermute(x, AXES[1:], pairs)


def up(x):
    return move(x, lambda c, m, a, y: (c, m, a, y + 1))


def down(x):
    return move(x, lambda c, m, a, y: (c, m, a, y + 3))


def across(x):
    return move(x, lambda c, m, a, y: (c, m, 1 - a, y))


def swap(x):
    return move(x, lambda c, m, a, y: (1 - c, m, a, y))


def pack_kernel(ids, tiles, upper, lower, slots, places, held, first, second, sems, out_sems):
    n = tiles.shape[0]
    loads = [pltpu.make_async_copy(tiles.at[i], held.at[i], sems.at[i]) for i in range(n)]
    for load in loads:
        load.start()
    for o in range(upper.shape[0]):
        slots[o] = 0
        places[o] = -1

    @pl.loop(0, n)
    def _(i):
        row, column = ids[i] // 8, ids[i] % 8
        owner = row // 7 * 4 + column // 2
        slots[owner] = i
        places[owner] = row % 7 * 2 + column % 2

    for load in loads:
        load.wait()

    def copies(o):
        return (
            pltpu.make_async_copy(first.at[o], upper.at[o], out_sems.at[0, o]),
            pltpu.make_async_copy(second.at[o], lower.at[o], out_sems.at[1, o]),
        )

    @pl.loop(0, upper.shape[0])
    def _(o):
        slot = slots[o]
        for j in range(HALF // TILE):
            piece = held[slot, :, j * TILE : (j + 1) * TILE]
            for (row, size), out in zip(SPLIT, (first, second)):
                out[o, j * size : (j + 1) * size, :] = piece[row : row + size]
        place = jnp.full((LABEL, TILE), places[o], jnp.int32)
        first[o, first.shape[1] - LABEL :, :] = place.astype(F32).astype(BF16)
        for copy in copies(o):
            copy.start()

    @pl.loop(0, upper.shape[0])
    def _(o):
        for copy in copies(o):
            copy.wait()


def pack(ids, tiles):
    n = 16
    rows = [HALF // TILE * size for _, size in SPLIT]
    shapes = [(n, rows[0] + LABEL, TILE), (n, rows[1], TILE)]
    return pl.pallas_call(
        pack_kernel,
        in_specs=[SMEM, HBM],
        out_specs=[HBM] * 2,
        out_shape=[jax.ShapeDtypeStruct(shape, BF16) for shape in shapes],
        scratch_shapes=[pltpu.SMEM((n,), jnp.int32)] * 2
        + [pltpu.VMEM(tiles.shape, BF16)]
        + [pltpu.VMEM(shape, BF16) for shape in shapes]
        + [pltpu.SemaphoreType.DMA((tiles.shape[0],)), pltpu.SemaphoreType.DMA((2, n))],
        compiler_params=pltpu.CompilerParams(vmem_limit_bytes=62 * MIB),
        cost_estimate=cost(0, 4 * tiles.size),
    )(ids, tiles)


def momentum_kernel(part, info, arrived, momentum, *refs):
    new, half0, half1, tile, old, fresh, rounded, in_sems, out_sems = refs[-9:]
    n = HEIGHT // TILE
    row, size = SPLIT[part]

    def place(t, r):
        half = (t + info[14]) % 2
        columns = pl.ds(pl.multiple_of(half * HALF, TILE), HALF)
        return pl.ds(pl.multiple_of(r * TILE + row, 16), size), columns

    def reads(t, r):
        source = info[2 * r + (t + info[14]) % 2]
        i = t * n + r
        return (
            pltpu.make_async_copy(momentum.at[place(t, r)], old.at[i], in_sems.at[0, i]),
            pltpu.make_async_copy(arrived.at[source, 0 : HALF // TILE * size], tile.at[i], in_sems.at[1, i]),
        )

    def writes(t, r):
        i = t * n + r
        out = (half0, half1)[t].at[r]
        return (
            pltpu.make_async_copy(fresh.at[i], new.at[place(t, r)], out_sems.at[0, i]),
            pltpu.make_async_copy(rounded.at[i], out, out_sems.at[1, i]),
        )

    for t in range(2):
        for r in range(n):
            for copy in reads(t, r):
                copy.start()
    for t in range(2):

        @pl.loop(0, n)
        def _(r):
            i = t * n + r
            for copy in reads(t, r):
                copy.wait()
            for j in range(HALF // TILE):
                columns = slice(j * TILE, (j + 1) * TILE)
                g = tile[i, j * size : (j + 1) * size, :].astype(F32)
                later = MOMENTUM_RATE * old[i, :, columns] + g
                fresh[i, :, columns] = later
                rounded[i, :, columns] = (g + MOMENTUM_RATE * later).astype(BF16)
            for copy in writes(t, r):
                copy.start()

    for t in range(2):

        @pl.loop(0, n)
        def _(r):
            for copy in writes(t, r):
                copy.wait()


def update_momentum(info, arrived, momentum, part, so_far):
    more = () if so_far is None else (so_far,)
    n = 2 * HEIGHT // TILE
    size = SPLIT[part][1]
    return pl.pallas_call(
        lambda *refs: momentum_kernel(part, *refs),
        in_specs=[SMEM] + [HBM] * (2 + len(more)),
        out_specs=[HBM] * 3,
        out_shape=[
            jax.ShapeDtypeStruct(momentum.shape, F32),
            jax.ShapeDtypeStruct((n // 2, size, HALF), BF16),
            jax.ShapeDtypeStruct((n // 2, size, HALF), BF16),
        ],
        scratch_shapes=[
            pltpu.VMEM((n, HALF // TILE * size, TILE), BF16),
            pltpu.VMEM((n, size, HALF), F32),
            pltpu.VMEM((n, size, HALF), F32),
            pltpu.VMEM((n, size, HALF), BF16),
            pltpu.SemaphoreType.DMA((2, n)),
            pltpu.SemaphoreType.DMA((2, n)),
        ],
        input_output_aliases={3: 0} if more else {},
        compiler_params=pltpu.CompilerParams(vmem_limit_bytes=62 * MIB),
        cost_estimate=cost(0, HEIGHT * HALF * 12),
    )(info, arrived, momentum, *more)


def panel_copies(info, blocks, panel, columns=None):
    c, a = info[0], info[2]
    copies = []
    for i, block in enumerate(blocks):
        other, t, part = i // 4, i // 2 % 2, i % 2
        core = 1 - c if other else c
        z = 2 * core + (a + t) % 2
        src = block if columns is None else block.at[:, :, columns]
        row, size = SPLIT[part]
        rows = pl.ds(z * (HEIGHT // TILE), HEIGHT // TILE)
        copies.append((src, panel.at[rows, row : row + size]))
    return copies


def panel_shape(width):
    return pltpu.VMEM((ROWS // TILE, TILE, width), BF16)


def chip_at(info, flip, dy):
    a, y = info[2], info[3]
    return (1 - a if flip else a) * 4 + (y + dy) % 4


def load_all(copies, sems):
    copies = [pltpu.make_async_copy(src, dst, sems.at[i]) for i, (src, dst) in enumerate(copies)]
    for copy in copies:
        copy.start()
    for copy in copies:
        copy.wait()


def gram_kernel(dests, info, *refs):
    blocks, outs = refs[:8], refs[8:-2]
    panel, sems = refs[-2:]
    load_all(panel_copies(info, blocks, panel), sems)

    def term(b, d):
        left = panel[pl.ds(2 * b, 2)].reshape(SIDE, HALF)
        right = panel[pl.ds(2 * ((b + d) % BLOCKS), 2)].reshape(SIDE, HALF)
        return lax.dot_general(left, right, (((1,), (1,)), ((), ())), preferred_element_type=F32)

    base = HALF_BLOCKS * info[0]
    if len(dests) == 1:
        d = chip_at(info, *dests[0])
        for b in range(HALF_BLOCKS):
            block = term(base + b, d).astype(BF16)
            for out, (row, size) in zip(outs, PARTS):
                low, high = max(row, b * SIDE), min(row + size, (b + 1) * SIDE)
                if low < high:
                    out[low - row : high - row] = block[low - b * SIDE : high - b * SIDE]
    else:

        @pl.loop(0, HALF_BLOCKS)
        def _(b):
            for dest, out in zip(dests, outs):
                block = term(base + b, chip_at(info, *dest))
                out[pl.ds(pl.multiple_of(b * SIDE, SIDE), SIDE)] = block.astype(out.dtype)


def gram_chunks(info, blocks, dests, shapes):
    return pl.pallas_call(
        lambda *refs: gram_kernel(dests, *refs),
        in_specs=[SMEM] + [HBM] * 8,
        out_specs=[VMEM] * len(shapes),
        out_shape=shapes,
        scratch_shapes=[panel_shape(HALF), pltpu.SemaphoreType.DMA((8,))],
        compiler_params=pltpu.CompilerParams(vmem_limit_bytes=24 * MIB),
        cost_estimate=cost(len(dests) * 2 * CHUNK * SIDE * HALF, 8.3e6 + len(dests) * CHUNK * SIDE * 4),
    )(info, *blocks)


def chunk(dtype=BF16, rows=CHUNK):
    return jax.ShapeDtypeStruct((rows, SIDE), dtype)


def second_sums_kernel(p1, p2, p3, r1, r2, r3, q1, q2, q3):
    for own, got, out, (row, size) in zip((p1, p2, p3), (r1, r2, r3), (q1, q2, q3), PARTS):
        if row:
            out[:row] = own[:row].astype(BF16)
        out[row : row + size] = (own[row : row + size] + got[...].astype(F32)).astype(BF16)
        if row + size < CHUNK:
            out[row + size :] = own[row + size :].astype(BF16)


def third_sums_kernel(p1, p2, g1, g2, g3, v1, v2):
    v1[...] = (p1[...] + (g1[...].astype(F32) + g3[...].astype(F32))).astype(BF16)
    v2[...] = (p2[...] + g2[...].astype(F32)).astype(BF16)


def last_sums_kernel(p, v1, v2, v3, turned, out):
    total = p[...] + (v1[...].astype(F32) + v2[...].astype(F32) + v3[...].astype(F32))
    out[...] = total.astype(BF16)


def in_vmem(kernel, shapes, *args, after=()):
    size = sum(x.size * x.dtype.itemsize for x in args)
    return pl.pallas_call(
        kernel,
        in_specs=[VMEM] * len(args) + [ANY] * len(after),
        out_specs=[VMEM] * len(shapes),
        out_shape=shapes,
        compiler_params=pltpu.CompilerParams(vmem_limit_bytes=16 * MIB),
        cost_estimate=cost(0, size),
    )(*args, *after)


def turn_kernel(info, *refs):
    blocks, out, held, flat, sems = refs[:8], *refs[8:]
    c = info[0]
    shift = pl.multiple_of(512 * c, TILE)
    load_all(panel_copies(info, blocks, held, pl.ds(shift, WIDE)), sems)
    for r in range(ROWS // TILE):
        flat[:, r * TILE : (r + 1) * TILE] = held[r].T
    out[:512, :ROWS] = flat[pl.ds(pl.multiple_of(128 * c, 64), 512), :]
    out[512:, :ROWS] = flat[pl.ds(pl.multiple_of(512 - 448 * c, 64), 64), :]
    out[:, ROWS:] = out[:, :CHUNK]


def turned_panel(info, blocks):
    return pl.pallas_call(
        turn_kernel,
        in_specs=[SMEM] + [HBM] * 8,
        out_specs=VMEM,
        out_shape=jax.ShapeDtypeStruct((SHARE, AROUND), BF16),
        scratch_shapes=[panel_shape(WIDE), pltpu.VMEM((WIDE, ROWS), BF16), pltpu.SemaphoreType.DMA((8,))],
        compiler_params=pltpu.CompilerParams(vmem_limit_bytes=24 * MIB),
        cost_estimate=cost(0, 1.2e7),
    )(info, *blocks)


SOURCES = ((0, 0), (0, 3), (0, 1), (1, 0), (1, 1), (1, 3), (0, 2), (1, 2))


def apply_kernel(info, *refs):
    own, ends, swapped = refs[:7], refs[7:10], refs[10:14]
    turned = refs[14]
    outs, rest_direct, rest_flipped, all_mixed, scales = refs[15:17], *refs[17:21]
    direct, flipped, panel, mixed, stage, extra, sems, panel_sem, out_sems, keep_sems = refs[21:]
    c = info[0]
    panel_copy = pltpu.make_async_copy(turned, panel, panel_sem)
    panel_copy.start()
    pieces = [(c, ref, 0, rel) for ref, rel in zip(own, SOURCES)]
    pieces += [(1 - c, swapped[0], 0, SOURCES[0]), (1 - c, swapped[3], 0, SOURCES[7])]
    pieces += [(1 - c, swapped[1 + n // 3], n % 3 * CHUNK, SOURCES[1 + n]) for n in range(6)]
    for n, (core, ref, row, rel) in enumerate(pieces):
        d = chip_at(info, *rel)

        @pl.loop(0, HALF_BLOCKS)
        def _(b):
            i = (core * HALF_BLOCKS + b + d) % BLOCKS
            src = ref.at[pl.ds(pl.multiple_of(row + b * SIDE, SIDE), SIDE)]
            pltpu.make_async_copy(src, direct.at[i, pl.ds(pl.multiple_of((7 - d) * SIDE, SIDE), SIDE)], sems.at[n]).start()

    d = chip_at(info, *SOURCES[7])
    last = []
    for ref, (row, size) in zip(ends, PARTS):
        for b in range(HALF_BLOCKS):
            low, high = max(row, b * SIDE), min(row + size, (b + 1) * SIDE)
            if low < high:
                i = (c * HALF_BLOCKS + b + d) % BLOCKS
                start = pl.multiple_of((7 - d) * SIDE + low - b * SIDE, 16)
                src = ref.at[low - row : high - row]
                last.append(pltpu.make_async_copy(src, direct.at[i, pl.ds(start, high - low)], sems.at[15 + len(last)]))
    for copy in last:
        copy.start()
    for n in range(15):
        whole = direct.at[0:HALF_BLOCKS, 0:SIDE]
        pltpu.make_async_copy(whole, whole, sems.at[n]).wait()
    for copy in last:
        copy.wait()
    panel_copy.wait()

    total = jnp.zeros((), F32)
    on = lax.broadcasted_iota(jnp.int32, (SIDE, SIDE), 0) == lax.broadcasted_iota(jnp.int32, (SIDE, SIDE), 1)
    diagonal = jnp.zeros((SIDE, SIDE), F32)
    for i in range(BLOCKS):
        diagonal += direct[i, 7 * SIDE :, :].astype(F32)
    total = jnp.sum(jnp.where(on, diagonal, 0.0))
    total = jnp.full((1, SIDE), total, F32)
    factor = math.sqrt(ROWS) / (2.0 * (jnp.sqrt(total) + EPSILON))
    square = factor * factor

    def product(i, x):
        return gram_times(i, x, direct.at[i], flipped.at[i]) * square

    @pl.loop(0, BLOCKS)
    def _(i):
        for e in range(1, 7):
            far = (i + e) % BLOCKS
            flipped[i, (e - 1) * SIDE : e * SIDE, :] = direct[far, (7 - e) * SIDE : (8 - e) * SIDE, :].T
        columns = pl.ds(pl.multiple_of(i * SIDE, SIDE), SIDE)
        mix = COEF_CUBIC * panel[:, columns].astype(F32) + COEF_QUINTIC * product(i, panel)
        mix = mix.astype(BF16)
        mixed[:, columns] = mix

        @pl.when(i < HALF_BLOCKS)
        def _():
            mixed[:, pl.ds(pl.multiple_of(i * SIDE + ROWS, SIDE), SIDE)] = mix

    other = (1 - c) * HALF_BLOCKS
    scale = math.sqrt(COLS) * factor
    scales[...] = jnp.concatenate([scale] * 4 + [square] * 4)
    keeps = [
        pltpu.make_async_copy(direct.at[pl.ds(other, HALF_BLOCKS)], rest_direct, keep_sems.at[0]),
        pltpu.make_async_copy(flipped.at[pl.ds(other, HALF_BLOCKS)], rest_flipped, keep_sems.at[1]),
        pltpu.make_async_copy(mixed, all_mixed, keep_sems.at[2]),
    ]
    for copy in keeps:
        copy.start()

    @pl.loop(0, HALF_BLOCKS)
    def _(b):
        i = c * HALF_BLOCKS + b
        columns = pl.ds(pl.multiple_of(i * SIDE, SIDE), SIDE)
        result = scale * (COEF_LINEAR * panel[:, columns].astype(F32) + product(i, mixed))
        stage[pl.ds(pl.multiple_of(b * SIDE, SIDE), SIDE)] = result.astype(BF16).T

    send_back(info, stage, extra, outs, out_sems)
    for copy in keeps:
        copy.wait()


def gram_times(i, x, direct, flipped):
    first = pl.ds(pl.multiple_of((i + 7) % BLOCKS * SIDE, SIDE), 8 * SIDE)
    rest = pl.ds(pl.multiple_of((i + 1) % BLOCKS * SIDE, SIDE), 6 * SIDE)
    result = jnp.dot(x[:, first], direct[...], preferred_element_type=F32)
    return result + jnp.dot(x[:, rest], flipped[...], preferred_element_type=F32)


def send_back(info, stage, extra, outs, sems):
    a = info[2]
    sends = []
    for side, out in enumerate(outs):
        owner = 1 - a if side else a
        start = pl.multiple_of(owner * HEIGHT, 128)
        for j in range(4):
            rows = pl.ds(start, HEIGHT)
            sends.append((stage.at[rows, j * TILE : (j + 1) * TILE], out.at[pl.ds(j * HEIGHT, HEIGHT)]))
        halves = [stage[pl.ds(pl.multiple_of(start + row, 64), 448), 512:] for row in (0, 448)]
        extra[side] = jnp.concatenate(halves, axis=1)
        sends.append((extra.at[side], out.at[pl.ds(4 * HEIGHT, 448)]))
    load_all(sends, sems)


def rest_kernel(info, direct, flipped, panel, all_mixed, scales, out0, out1, mixed, stage, extra, sems):
    b = pl.program_id(0)

    @pl.when(b == 0)
    def _():
        load_all([(all_mixed, mixed)], sems)

    i = (1 - info[0]) * HALF_BLOCKS + b
    product = gram_times(i, mixed, direct.at[0], flipped.at[0]) * scales[4:5]
    result = scales[0:1] * (COEF_LINEAR * panel[...].astype(F32) + product)
    stage[pl.ds(pl.multiple_of(b * SIDE, SIDE), SIDE)] = result.astype(BF16).T

    @pl.when(b == HALF_BLOCKS - 1)
    def _():
        send_back(info, stage, extra, (out0, out1), sems)


def apply_rest(info, direct, flipped, mixed, scales, turned):
    return pl.pallas_call(
        rest_kernel,
        grid_spec=pltpu.PrefetchScalarGridSpec(
            num_scalar_prefetch=1,
            grid=(HALF_BLOCKS,),
            in_specs=[
                pl.BlockSpec((1, 8 * SIDE, SIDE), lambda b, s: (b, 0, 0)),
                pl.BlockSpec((1, 6 * SIDE, SIDE), lambda b, s: (b, 0, 0)),
                pl.BlockSpec((SHARE, SIDE), lambda b, s: (0, (1 - s[0]) * HALF_BLOCKS + b)),
                HBM,
                VMEM,
            ],
            out_specs=[HBM] * 2,
            scratch_shapes=[
                pltpu.VMEM((SHARE, AROUND), BF16),
                pltpu.VMEM((CHUNK, SHARE), BF16),
                pltpu.VMEM((2, 448, TILE), BF16),
                pltpu.SemaphoreType.DMA((10,)),
            ],
        ),
        out_shape=[jax.ShapeDtypeStruct((BACK_ROWS, TILE), BF16)] * 2,
        compiler_params=pltpu.CompilerParams(vmem_limit_bytes=62 * MIB),
        cost_estimate=cost(ROWS * ROWS * SHARE, 2e7),
    )(info, direct, flipped, turned, mixed, scales)


def apply_poly(info, own, ends, swapped, turned):
    return pl.pallas_call(
        apply_kernel,
        in_specs=[SMEM] + [HBM] * 15,
        out_specs=[HBM] * 5 + [VMEM],
        out_shape=[jax.ShapeDtypeStruct((BACK_ROWS, TILE), BF16)] * 2
        + [
            jax.ShapeDtypeStruct((HALF_BLOCKS, 8 * SIDE, SIDE), BF16),
            jax.ShapeDtypeStruct((HALF_BLOCKS, 6 * SIDE, SIDE), BF16),
            jax.ShapeDtypeStruct((SHARE, AROUND), BF16),
            jax.ShapeDtypeStruct((8, SIDE), F32),
        ],
        scratch_shapes=[
            pltpu.VMEM((BLOCKS, 8 * SIDE, SIDE), BF16),
            pltpu.VMEM((BLOCKS, 6 * SIDE, SIDE), BF16),
            pltpu.VMEM((SHARE, AROUND), BF16),
            pltpu.VMEM((SHARE, AROUND), BF16),
            pltpu.VMEM((CHUNK, SHARE), BF16),
            pltpu.VMEM((2, 448, TILE), BF16),
            pltpu.SemaphoreType.DMA((32,)),
            pltpu.SemaphoreType.DMA,
            pltpu.SemaphoreType.DMA((10,)),
            pltpu.SemaphoreType.DMA((3,)),
        ],
        compiler_params=pltpu.CompilerParams(vmem_limit_bytes=58 * MIB),
        cost_estimate=cost(3 * ROWS * ROWS * SHARE, 4e7),
    )(info, *own, *ends, *swapped, turned)


def unpack_kernel(info, r0, r1, r2, r3, update):
    m, a = info[1], info[2]
    for s, got in enumerate((r0, r1, r2, r3)):
        core = 1 - m if s >= 2 else m
        side = 1 - a if s % 2 else a
        for j in range(4):
            start = pl.multiple_of((9 * side + j + 5 * core) * TILE, TILE)
            update[:, pl.ds(start, TILE)] = got[j * HEIGHT : (j + 1) * HEIGHT]
    for s, (one, two) in enumerate(((r0, r2), (r1, r3))):
        side = 1 - a if s else a
        one, two = one[4 * HEIGHT :], two[4 * HEIGHT :]
        low, high = jnp.where(m == 0, one, two), jnp.where(m == 0, two, one)
        tile = pl.ds(pl.multiple_of((9 * side + 4) * TILE, TILE), TILE)
        update[:448, tile] = jnp.concatenate([low[:, :64], high[:, :64]], axis=1)
        update[448:, tile] = jnp.concatenate([low[:, 64:], high[:, 64:]], axis=1)


def unpack(info, parts):
    return pl.pallas_call(
        unpack_kernel,
        in_specs=[SMEM] + [VMEM] * 4,
        out_specs=VMEM,
        out_shape=jax.ShapeDtypeStruct((HEIGHT, 2304), BF16),
        compiler_params=pltpu.CompilerParams(vmem_limit_bytes=32 * MIB),
        cost_estimate=cost(0, 8.3e6),
    )(info, *parts)


def on_device(grad_tiles, tile_ids, momentum):
    core, zm, zl, y = (lax.axis_index(name) for name in AXES[1:])
    info = jnp.stack([core, zm, zl, y]).astype(jnp.int32)
    tile_count = grad_tiles.shape[0]

    upper, lower = pack(tile_ids, grad_tiles)
    upper = lax.all_to_all(upper, PLANE, split_axis=0, concat_axis=0, tiled=True)
    lower, _ = lax.optimization_barrier((lower, upper))
    lower = lax.all_to_all(lower, PLANE, split_axis=0, concat_axis=0, tiled=True)

    got_labels = upper[:, -1, 0].astype(jnp.int32)
    found = got_labels[None, :] == jnp.arange(tile_count, dtype=jnp.int32)[:, None]
    sources = jnp.sum(jnp.where(found, jnp.arange(16, dtype=jnp.int32)[None, :], 0), axis=1)
    details = jnp.concatenate([sources, zl[None].astype(jnp.int32)])
    new_momentum, *halves0 = update_momentum(details, upper, momentum, 0, None)
    new_momentum, *halves1 = update_momentum(details, lower, momentum, 1, new_momentum)

    def to_panel(halves):
        half0, half1 = halves
        return (
            move(half0, lambda c, m, a, y: (m, c, a, y)),
            move(half1, lambda c, m, a, y: (m, c, 1 - a, y)),
        )

    got0, got1 = to_panel(halves0), to_panel(halves1)
    blocks = (got0[0], got1[0], got0[1], got1[1])
    blocks += tuple(swap(x) for x in blocks)

    far = gram_chunks(info, blocks, ((1, 2),), [chunk(BF16, size) for _, size in PARTS])
    far0, far1, far2 = up(far[0]), down(far[1]), across(far[2])
    terms = gram_chunks(info, blocks, ((1, 1), (1, 3), (0, 2)), [chunk(F32)] * 3)
    q1, q2, q3 = in_vmem(second_sums_kernel, [chunk()] * 3, *terms, far0, far1, far2)
    g1, g2, g3 = across(q1), down(q2), up(q3)
    later, _ = lax.optimization_barrier((blocks, q1))
    nearest, beside, below, center = gram_chunks(
        info, later, ((0, 1), (1, 0), (0, 3), (0, 0)), [chunk(F32), chunk(F32), chunk(), chunk(F32)]
    )
    near = down(below)
    v1, v2 = in_vmem(third_sums_kernel, [chunk()] * 2, nearest, beside, g1, g2, g3)
    w1, w2 = up(v1), across(v2)
    later, _ = lax.optimization_barrier((blocks, v1))
    turned = turned_panel(info, later)
    (mine,) = in_vmem(last_sums_kernel, [chunk()], center, w1, w2, near, after=(turned,))

    low, high, pair = up(mine), down(mine), across(mine)
    a1, a2, a3 = across(high), up(pair), down(high)
    ends = tuple(
        send(x[row : row + size]) for send, x, (row, size) in zip((down, up, across), (a1, a2, a3), PARTS)
    )
    swapped = (swap(mine), swap(jnp.concatenate([low, high, pair])), swap(jnp.concatenate([a1, a2, a3])))
    ends, swapped = lax.optimization_barrier((ends, swapped))
    swapped += (swap(jnp.concatenate(ends)),)
    *sent, direct, flipped, mixed, scales = apply_poly(info, (mine, low, high, pair, a1, a2, a3), ends, swapped, turned)
    sent += apply_rest(info, direct, flipped, mixed, scales, turned)

    parts = (
        move(sent[0], lambda c, m, a, y: (m, c, a, y)),
        move(sent[1], lambda c, m, a, y: (m, c, 1 - a, y)),
        move(sent[2], lambda c, m, a, y: (m, 1 - c, a, y)),
        move(sent[3], lambda c, m, a, y: (m, 1 - c, 1 - a, y)),
    )
    return new_momentum, unpack(info, parts)


def solution(mesh):
    fine = Mesh(mesh.devices.reshape(4, 2, 2, 2, 4), AXES)
    tall = P(("x", "core", "zm", "zl"), "y")
    return jax.shard_map(
        on_device,
        mesh=fine,
        in_specs=(P(AXES, None, None), P(AXES), tall),
        out_specs=(tall, tall),
        check_vma=False,
    )
```

```python
import math

import jax
import jax.numpy as jnp
from jax import lax
from jax.experimental import pallas as pl
from jax.experimental.pallas import tpu as pltpu
from jax.sharding import Mesh
from jax.sharding import PartitionSpec as P

ROWS = 3584
COLS = 9216
MOMENTUM_RATE = 0.95
COEF_LINEAR = 3.4445
COEF_CUBIC = -4.775
COEF_QUINTIC = 2.0315
EPSILON = 1e-06

HEIGHT = 896
HALF = 1152
TILE = 128
SPLIT = ((0, 80), (80, 48))
LABEL = 16
SIDE = 256
BLOCKS = ROWS // SIDE
HALF_BLOCKS = BLOCKS // 2
CHUNK = HALF_BLOCKS * SIDE
PARTS = ((0, 608), (608, 592), (1200, 592))
WIDE = 640
SHARE = 576
AROUND = ROWS + CHUNK
BACK_ROWS = 4032

AXES = ("x", "core", "zm", "zl", "y")
PLANE = ("zm", "zl", "y")
BF16 = jnp.bfloat16
F32 = jnp.float32
MIB = 1 << 20
ANY = pl.BlockSpec(memory_space=pl.ANY)
HBM = pl.BlockSpec(memory_space=pltpu.HBM)
VMEM = pl.BlockSpec(memory_space=pltpu.VMEM)
SMEM = pl.BlockSpec(memory_space=pltpu.SMEM)


def cost(flops, size):
    return pl.CostEstimate(flops=int(flops), bytes_accessed=int(size), transcendentals=0)


def move(x, route):
    pairs = []
    for c in range(2):
        for m in range(2):
            for a in range(2):
                for y in range(4):
                    c2, m2, a2, y2 = route(c, m, a, y)
                    pairs.append((((c * 2 + m) * 2 + a) * 4 + y, ((c2 * 2 + m2) * 2 + a2) * 4 + y2 % 4))
    return lax.ppermute(x, AXES[1:], pairs)


def up(x):
    return move(x, lambda c, m, a, y: (c, m, a, y + 1))


def down(x):
    return move(x, lambda c, m, a, y: (c, m, a, y + 3))


def across(x):
    return move(x, lambda c, m, a, y: (c, m, 1 - a, y))


def swap(x):
    return move(x, lambda c, m, a, y: (1 - c, m, a, y))


def pack_kernel(ids, tiles, upper, lower, slots, places, held, first, second, sems, out_sems):
    n = tiles.shape[0]
    loads = [pltpu.make_async_copy(tiles.at[i], held.at[i], sems.at[i]) for i in range(n)]
    for load in loads:
        load.start()
    for o in range(upper.shape[0]):
        slots[o] = 0
        places[o] = -1

    @pl.loop(0, n)
    def _(i):
        row, column = ids[i] // 8, ids[i] % 8
        owner = row // 7 * 4 + column // 2
        slots[owner] = i
        places[owner] = row % 7 * 2 + column % 2

    for load in loads:
        load.wait()

    def copies(o):
        return (
            pltpu.make_async_copy(first.at[o], upper.at[o], out_sems.at[0, o]),
            pltpu.make_async_copy(second.at[o], lower.at[o], out_sems.at[1, o]),
        )

    @pl.loop(0, upper.shape[0])
    def _(o):
        slot = slots[o]
        for j in range(HALF // TILE):
            piece = held[slot, :, j * TILE : (j + 1) * TILE]
            for (row, size), out in zip(SPLIT, (first, second)):
                out[o, j * size : (j + 1) * size, :] = piece[row : row + size]
        place = jnp.full((LABEL, TILE), places[o], jnp.int32)
        first[o, first.shape[1] - LABEL :, :] = place.astype(F32).astype(BF16)
        for copy in copies(o):
            copy.start()

    @pl.loop(0, upper.shape[0])
    def _(o):
        for copy in copies(o):
            copy.wait()


def pack(ids, tiles):
    n = 16
    rows = [HALF // TILE * size for _, size in SPLIT]
    shapes = [(n, rows[0] + LABEL, TILE), (n, rows[1], TILE)]
    return pl.pallas_call(
        pack_kernel,
        in_specs=[SMEM, HBM],
        out_specs=[HBM] * 2,
        out_shape=[jax.ShapeDtypeStruct(shape, BF16) for shape in shapes],
        scratch_shapes=[pltpu.SMEM((n,), jnp.int32)] * 2
        + [pltpu.VMEM(tiles.shape, BF16)]
        + [pltpu.VMEM(shape, BF16) for shape in shapes]
        + [pltpu.SemaphoreType.DMA((tiles.shape[0],)), pltpu.SemaphoreType.DMA((2, n))],
        compiler_params=pltpu.CompilerParams(vmem_limit_bytes=62 * MIB),
        cost_estimate=cost(0, 4 * tiles.size),
    )(ids, tiles)


def momentum_kernel(part, info, arrived, momentum, *refs):
    new, half0, half1, tile, old, fresh, rounded, in_sems, out_sems = refs[-9:]
    n = HEIGHT // TILE
    row, size = SPLIT[part]

    def place(t, r):
        half = (t + info[14]) % 2
        columns = pl.ds(pl.multiple_of(half * HALF, TILE), HALF)
        return pl.ds(pl.multiple_of(r * TILE + row, 16), size), columns

    def reads(t, r):
        source = info[2 * r + (t + info[14]) % 2]
        i = t * n + r
        return (
            pltpu.make_async_copy(momentum.at[place(t, r)], old.at[i], in_sems.at[0, i]),
            pltpu.make_async_copy(arrived.at[source, 0 : HALF // TILE * size], tile.at[i], in_sems.at[1, i]),
        )

    def writes(t, r):
        i = t * n + r
        out = (half0, half1)[t].at[r]
        return (
            pltpu.make_async_copy(fresh.at[i], new.at[place(t, r)], out_sems.at[0, i]),
            pltpu.make_async_copy(rounded.at[i], out, out_sems.at[1, i]),
        )

    for t in range(2):
        for r in range(n):
            for copy in reads(t, r):
                copy.start()
    for t in range(2):

        @pl.loop(0, n)
        def _(r):
            i = t * n + r
            for copy in reads(t, r):
                copy.wait()
            for j in range(HALF // TILE):
                columns = slice(j * TILE, (j + 1) * TILE)
                g = tile[i, j * size : (j + 1) * size, :].astype(F32)
                later = MOMENTUM_RATE * old[i, :, columns] + g
                fresh[i, :, columns] = later
                rounded[i, :, columns] = (g + MOMENTUM_RATE * later).astype(BF16)
            for copy in writes(t, r):
                copy.start()

    for t in range(2):

        @pl.loop(0, n)
        def _(r):
            for copy in writes(t, r):
                copy.wait()


def update_momentum(info, arrived, momentum, part, so_far):
    more = () if so_far is None else (so_far,)
    n = 2 * HEIGHT // TILE
    size = SPLIT[part][1]
    return pl.pallas_call(
        lambda *refs: momentum_kernel(part, *refs),
        in_specs=[SMEM] + [HBM] * (2 + len(more)),
        out_specs=[HBM] * 3,
        out_shape=[
            jax.ShapeDtypeStruct(momentum.shape, F32),
            jax.ShapeDtypeStruct((n // 2, size, HALF), BF16),
            jax.ShapeDtypeStruct((n // 2, size, HALF), BF16),
        ],
        scratch_shapes=[
            pltpu.VMEM((n, HALF // TILE * size, TILE), BF16),
            pltpu.VMEM((n, size, HALF), F32),
            pltpu.VMEM((n, size, HALF), F32),
            pltpu.VMEM((n, size, HALF), BF16),
            pltpu.SemaphoreType.DMA((2, n)),
            pltpu.SemaphoreType.DMA((2, n)),
        ],
        input_output_aliases={3: 0} if more else {},
        compiler_params=pltpu.CompilerParams(vmem_limit_bytes=62 * MIB),
        cost_estimate=cost(0, HEIGHT * HALF * 12),
    )(info, arrived, momentum, *more)


def panel_copies(info, blocks, panel, columns=None):
    c, a = info[0], info[2]
    copies = []
    for i, block in enumerate(blocks):
        other, t, part = i // 4, i // 2 % 2, i % 2
        core = 1 - c if other else c
        z = 2 * core + (a + t) % 2
        src = block if columns is None else block.at[:, :, columns]
        row, size = SPLIT[part]
        rows = pl.ds(z * (HEIGHT // TILE), HEIGHT // TILE)
        copies.append((src, panel.at[rows, row : row + size]))
    return copies


def panel_shape(width):
    return pltpu.VMEM((ROWS // TILE, TILE, width), BF16)


def chip_at(info, flip, dy):
    a, y = info[2], info[3]
    return (1 - a if flip else a) * 4 + (y + dy) % 4


def load_all(copies, sems):
    copies = [pltpu.make_async_copy(src, dst, sems.at[i]) for i, (src, dst) in enumerate(copies)]
    for copy in copies:
        copy.start()
    for copy in copies:
        copy.wait()


def gram_kernel(dests, info, *refs):
    blocks, outs = refs[:8], refs[8:-2]
    panel, sems = refs[-2:]
    load_all(panel_copies(info, blocks, panel), sems)

    def term(b, d):
        left = panel[pl.ds(2 * b, 2)].reshape(SIDE, HALF)
        right = panel[pl.ds(2 * ((b + d) % BLOCKS), 2)].reshape(SIDE, HALF)
        return lax.dot_general(left, right, (((1,), (1,)), ((), ())), preferred_element_type=F32)

    base = HALF_BLOCKS * info[0]
    if len(dests) == 1:
        d = chip_at(info, *dests[0])
        for b in range(HALF_BLOCKS):
            block = term(base + b, d).astype(BF16)
            for out, (row, size) in zip(outs, PARTS):
                low, high = max(row, b * SIDE), min(row + size, (b + 1) * SIDE)
                if low < high:
                    out[low - row : high - row] = block[low - b * SIDE : high - b * SIDE]
    else:

        @pl.loop(0, HALF_BLOCKS)
        def _(b):
            for dest, out in zip(dests, outs):
                block = term(base + b, chip_at(info, *dest))
                out[pl.ds(pl.multiple_of(b * SIDE, SIDE), SIDE)] = block.astype(out.dtype)


def gram_chunks(info, blocks, dests, shapes):
    return pl.pallas_call(
        lambda *refs: gram_kernel(dests, *refs),
        in_specs=[SMEM] + [HBM] * 8,
        out_specs=[VMEM] * len(shapes),
        out_shape=shapes,
        scratch_shapes=[panel_shape(HALF), pltpu.SemaphoreType.DMA((8,))],
        compiler_params=pltpu.CompilerParams(vmem_limit_bytes=24 * MIB),
        cost_estimate=cost(len(dests) * 2 * CHUNK * SIDE * HALF, 8.3e6 + len(dests) * CHUNK * SIDE * 4),
    )(info, *blocks)


def chunk(dtype=BF16, rows=CHUNK):
    return jax.ShapeDtypeStruct((rows, SIDE), dtype)


def second_sums_kernel(p1, p2, p3, r1, r2, r3, q1, q2, q3):
    for own, got, out, (row, size) in zip((p1, p2, p3), (r1, r2, r3), (q1, q2, q3), PARTS):
        if row:
            out[:row] = own[:row].astype(BF16)
        out[row : row + size] = (own[row : row + size] + got[...].astype(F32)).astype(BF16)
        if row + size < CHUNK:
            out[row + size :] = own[row + size :].astype(BF16)


def third_sums_kernel(p1, p2, g1, g2, g3, v1, v2):
    v1[...] = (p1[...] + (g1[...].astype(F32) + g3[...].astype(F32))).astype(BF16)
    v2[...] = (p2[...] + g2[...].astype(F32)).astype(BF16)


def last_sums_kernel(p, v1, v2, v3, turned, out):
    total = p[...] + (v1[...].astype(F32) + v2[...].astype(F32) + v3[...].astype(F32))
    out[...] = total.astype(BF16)


def in_vmem(kernel, shapes, *args, after=()):
    size = sum(x.size * x.dtype.itemsize for x in args)
    return pl.pallas_call(
        kernel,
        in_specs=[VMEM] * len(args) + [ANY] * len(after),
        out_specs=[VMEM] * len(shapes),
        out_shape=shapes,
        compiler_params=pltpu.CompilerParams(vmem_limit_bytes=16 * MIB),
        cost_estimate=cost(0, size),
    )(*args, *after)


def turn_kernel(info, *refs):
    blocks, out, held, flat, sems = refs[:8], *refs[8:]
    c = info[0]
    shift = pl.multiple_of(512 * c, TILE)
    load_all(panel_copies(info, blocks, held, pl.ds(shift, WIDE)), sems)
    for r in range(ROWS // TILE):
        flat[:, r * TILE : (r + 1) * TILE] = held[r].T
    out[:512, :ROWS] = flat[pl.ds(pl.multiple_of(128 * c, 64), 512), :]
    out[512:, :ROWS] = flat[pl.ds(pl.multiple_of(512 - 448 * c, 64), 64), :]
    out[:, ROWS:] = out[:, :CHUNK]


def turned_panel(info, blocks):
    return pl.pallas_call(
        turn_kernel,
        in_specs=[SMEM] + [HBM] * 8,
        out_specs=VMEM,
        out_shape=jax.ShapeDtypeStruct((SHARE, AROUND), BF16),
        scratch_shapes=[panel_shape(WIDE), pltpu.VMEM((WIDE, ROWS), BF16), pltpu.SemaphoreType.DMA((8,))],
        compiler_params=pltpu.CompilerParams(vmem_limit_bytes=24 * MIB),
        cost_estimate=cost(0, 1.2e7),
    )(info, *blocks)


SOURCES = ((0, 0), (0, 3), (0, 1), (1, 0), (1, 1), (1, 3), (0, 2), (1, 2))


def apply_kernel(info, *refs):
    own, ends, swapped = refs[:7], refs[7:10], refs[10:13]
    turned = refs[13]
    outs, rest_direct, rest_flipped, all_mixed, scales = refs[14:16], *refs[16:20]
    direct, flipped, panel, mixed, stage, extra, sems, panel_sem, out_sems, keep_sems = refs[20:]
    c = info[0]
    panel_copy = pltpu.make_async_copy(turned, panel, panel_sem)
    panel_copy.start()
    pieces = [(c, ref, 0, rel) for ref, rel in zip(own, SOURCES)]
    pieces += [(1 - c, swapped[n // 4], n % 4 * CHUNK, SOURCES[n]) for n in range(7)]
    pieces.append((1 - c, swapped[2], 0, SOURCES[7]))
    for n, (core, ref, row, rel) in enumerate(pieces):
        d = chip_at(info, *rel)

        @pl.loop(0, HALF_BLOCKS)
        def _(b):
            i = (core * HALF_BLOCKS + b + d) % BLOCKS
            src = ref.at[pl.ds(pl.multiple_of(row + b * SIDE, SIDE), SIDE)]
            pltpu.make_async_copy(src, direct.at[i, pl.ds(pl.multiple_of((7 - d) * SIDE, SIDE), SIDE)], sems.at[n]).start()

    d = chip_at(info, *SOURCES[7])
    last = []
    for ref, (row, size) in zip(ends, PARTS):
        for b in range(HALF_BLOCKS):
            low, high = max(row, b * SIDE), min(row + size, (b + 1) * SIDE)
            if low < high:
                i = (c * HALF_BLOCKS + b + d) % BLOCKS
                start = pl.multiple_of((7 - d) * SIDE + low - b * SIDE, 16)
                src = ref.at[low - row : high - row]
                last.append(pltpu.make_async_copy(src, direct.at[i, pl.ds(start, high - low)], sems.at[15 + len(last)]))
    for copy in last:
        copy.start()
    for n in range(15):
        whole = direct.at[0:HALF_BLOCKS, 0:SIDE]
        pltpu.make_async_copy(whole, whole, sems.at[n]).wait()
    for copy in last:
        copy.wait()
    panel_copy.wait()

    total = jnp.zeros((), F32)
    on = lax.broadcasted_iota(jnp.int32, (SIDE, SIDE), 0) == lax.broadcasted_iota(jnp.int32, (SIDE, SIDE), 1)
    diagonal = jnp.zeros((SIDE, SIDE), F32)
    for i in range(BLOCKS):
        diagonal += direct[i, 7 * SIDE :, :].astype(F32)
    total = jnp.sum(jnp.where(on, diagonal, 0.0))
    total = jnp.full((1, SIDE), total, F32)
    factor = math.sqrt(ROWS) / (2.0 * (jnp.sqrt(total) + EPSILON))
    square = factor * factor

    def product(i, x):
        return gram_times(i, x, direct.at[i], flipped.at[i]) * square

    @pl.loop(0, BLOCKS)
    def _(i):
        for e in range(1, 7):
            far = (i + e) % BLOCKS
            flipped[i, (e - 1) * SIDE : e * SIDE, :] = direct[far, (7 - e) * SIDE : (8 - e) * SIDE, :].T
        columns = pl.ds(pl.multiple_of(i * SIDE, SIDE), SIDE)
        mix = COEF_CUBIC * panel[:, columns].astype(F32) + COEF_QUINTIC * product(i, panel)
        mix = mix.astype(BF16)
        mixed[:, columns] = mix

        @pl.when(i < HALF_BLOCKS)
        def _():
            mixed[:, pl.ds(pl.multiple_of(i * SIDE + ROWS, SIDE), SIDE)] = mix

    other = (1 - c) * HALF_BLOCKS
    scale = math.sqrt(COLS) * factor
    scales[...] = jnp.concatenate([scale] * 4 + [square] * 4)
    keeps = [
        pltpu.make_async_copy(direct.at[pl.ds(other, HALF_BLOCKS)], rest_direct, keep_sems.at[0]),
        pltpu.make_async_copy(flipped.at[pl.ds(other, HALF_BLOCKS)], rest_flipped, keep_sems.at[1]),
        pltpu.make_async_copy(mixed, all_mixed, keep_sems.at[2]),
    ]
    for copy in keeps:
        copy.start()

    @pl.loop(0, HALF_BLOCKS)
    def _(b):
        i = c * HALF_BLOCKS + b
        columns = pl.ds(pl.multiple_of(i * SIDE, SIDE), SIDE)
        result = scale * (COEF_LINEAR * panel[:, columns].astype(F32) + product(i, mixed))
        stage[pl.ds(pl.multiple_of(b * SIDE, SIDE), SIDE)] = result.astype(BF16).T

    send_back(info, stage, extra, outs, out_sems)
    for copy in keeps:
        copy.wait()


def gram_times(i, x, direct, flipped):
    first = pl.ds(pl.multiple_of((i + 7) % BLOCKS * SIDE, SIDE), 8 * SIDE)
    rest = pl.ds(pl.multiple_of((i + 1) % BLOCKS * SIDE, SIDE), 6 * SIDE)
    result = jnp.dot(x[:, first], direct[...], preferred_element_type=F32)
    return result + jnp.dot(x[:, rest], flipped[...], preferred_element_type=F32)


def send_back(info, stage, extra, outs, sems):
    a = info[2]
    sends = []
    for side, out in enumerate(outs):
        owner = 1 - a if side else a
        start = pl.multiple_of(owner * HEIGHT, 128)
        for j in range(4):
            rows = pl.ds(start, HEIGHT)
            sends.append((stage.at[rows, j * TILE : (j + 1) * TILE], out.at[pl.ds(j * HEIGHT, HEIGHT)]))
        halves = [stage[pl.ds(pl.multiple_of(start + row, 64), 448), 512:] for row in (0, 448)]
        extra[side] = jnp.concatenate(halves, axis=1)
        sends.append((extra.at[side], out.at[pl.ds(4 * HEIGHT, 448)]))
    load_all(sends, sems)


def rest_kernel(info, direct, flipped, panel, all_mixed, scales, out0, out1, mixed, stage, extra, sems):
    b = pl.program_id(0)

    @pl.when(b == 0)
    def _():
        load_all([(all_mixed, mixed)], sems)

    i = (1 - info[0]) * HALF_BLOCKS + b
    product = gram_times(i, mixed, direct.at[0], flipped.at[0]) * scales[4:5]
    result = scales[0:1] * (COEF_LINEAR * panel[...].astype(F32) + product)
    stage[pl.ds(pl.multiple_of(b * SIDE, SIDE), SIDE)] = result.astype(BF16).T

    @pl.when(b == HALF_BLOCKS - 1)
    def _():
        send_back(info, stage, extra, (out0, out1), sems)


def apply_rest(info, direct, flipped, mixed, scales, turned):
    return pl.pallas_call(
        rest_kernel,
        grid_spec=pltpu.PrefetchScalarGridSpec(
            num_scalar_prefetch=1,
            grid=(HALF_BLOCKS,),
            in_specs=[
                pl.BlockSpec((1, 8 * SIDE, SIDE), lambda b, s: (b, 0, 0)),
                pl.BlockSpec((1, 6 * SIDE, SIDE), lambda b, s: (b, 0, 0)),
                pl.BlockSpec((SHARE, SIDE), lambda b, s: (0, (1 - s[0]) * HALF_BLOCKS + b)),
                HBM,
                VMEM,
            ],
            out_specs=[HBM] * 2,
            scratch_shapes=[
                pltpu.VMEM((SHARE, AROUND), BF16),
                pltpu.VMEM((CHUNK, SHARE), BF16),
                pltpu.VMEM((2, 448, TILE), BF16),
                pltpu.SemaphoreType.DMA((10,)),
            ],
        ),
        out_shape=[jax.ShapeDtypeStruct((BACK_ROWS, TILE), BF16)] * 2,
        compiler_params=pltpu.CompilerParams(vmem_limit_bytes=62 * MIB),
        cost_estimate=cost(ROWS * ROWS * SHARE, 2e7),
    )(info, direct, flipped, turned, mixed, scales)


def apply_poly(info, own, ends, swapped, turned):
    return pl.pallas_call(
        apply_kernel,
        in_specs=[SMEM] + [HBM] * 14,
        out_specs=[HBM] * 5 + [VMEM],
        out_shape=[jax.ShapeDtypeStruct((BACK_ROWS, TILE), BF16)] * 2
        + [
            jax.ShapeDtypeStruct((HALF_BLOCKS, 8 * SIDE, SIDE), BF16),
            jax.ShapeDtypeStruct((HALF_BLOCKS, 6 * SIDE, SIDE), BF16),
            jax.ShapeDtypeStruct((SHARE, AROUND), BF16),
            jax.ShapeDtypeStruct((8, SIDE), F32),
        ],
        scratch_shapes=[
            pltpu.VMEM((BLOCKS, 8 * SIDE, SIDE), BF16),
            pltpu.VMEM((BLOCKS, 6 * SIDE, SIDE), BF16),
            pltpu.VMEM((SHARE, AROUND), BF16),
            pltpu.VMEM((SHARE, AROUND), BF16),
            pltpu.VMEM((CHUNK, SHARE), BF16),
            pltpu.VMEM((2, 448, TILE), BF16),
            pltpu.SemaphoreType.DMA((32,)),
            pltpu.SemaphoreType.DMA,
            pltpu.SemaphoreType.DMA((10,)),
            pltpu.SemaphoreType.DMA((3,)),
        ],
        compiler_params=pltpu.CompilerParams(vmem_limit_bytes=58 * MIB),
        cost_estimate=cost(3 * ROWS * ROWS * SHARE, 4e7),
    )(info, *own, *ends, *swapped, turned)


def unpack_kernel(info, r0, r1, r2, r3, update):
    m, a = info[1], info[2]
    for s, got in enumerate((r0, r1, r2, r3)):
        core = 1 - m if s >= 2 else m
        side = 1 - a if s % 2 else a
        for j in range(4):
            start = pl.multiple_of((9 * side + j + 5 * core) * TILE, TILE)
            update[:, pl.ds(start, TILE)] = got[j * HEIGHT : (j + 1) * HEIGHT]
    for s, (one, two) in enumerate(((r0, r2), (r1, r3))):
        side = 1 - a if s else a
        one, two = one[4 * HEIGHT :], two[4 * HEIGHT :]
        low, high = jnp.where(m == 0, one, two), jnp.where(m == 0, two, one)
        tile = pl.ds(pl.multiple_of((9 * side + 4) * TILE, TILE), TILE)
        update[:448, tile] = jnp.concatenate([low[:, :64], high[:, :64]], axis=1)
        update[448:, tile] = jnp.concatenate([low[:, 64:], high[:, 64:]], axis=1)


def unpack(info, parts):
    return pl.pallas_call(
        unpack_kernel,
        in_specs=[SMEM] + [VMEM] * 4,
        out_specs=VMEM,
        out_shape=jax.ShapeDtypeStruct((HEIGHT, 2304), BF16),
        compiler_params=pltpu.CompilerParams(vmem_limit_bytes=32 * MIB),
        cost_estimate=cost(0, 8.3e6),
    )(info, *parts)


def on_device(grad_tiles, tile_ids, momentum):
    core, zm, zl, y = (lax.axis_index(name) for name in AXES[1:])
    info = jnp.stack([core, zm, zl, y]).astype(jnp.int32)
    tile_count = grad_tiles.shape[0]

    upper, lower = pack(tile_ids, grad_tiles)
    upper = lax.all_to_all(upper, PLANE, split_axis=0, concat_axis=0, tiled=True)
    lower, _ = lax.optimization_barrier((lower, upper))
    lower = lax.all_to_all(lower, PLANE, split_axis=0, concat_axis=0, tiled=True)

    got_labels = upper[:, -1, 0].astype(jnp.int32)
    found = got_labels[None, :] == jnp.arange(tile_count, dtype=jnp.int32)[:, None]
    sources = jnp.sum(jnp.where(found, jnp.arange(16, dtype=jnp.int32)[None, :], 0), axis=1)
    details = jnp.concatenate([sources, zl[None].astype(jnp.int32)])
    new_momentum, *halves0 = update_momentum(details, upper, momentum, 0, None)
    new_momentum, *halves1 = update_momentum(details, lower, momentum, 1, new_momentum)

    def to_panel(halves):
        half0, half1 = halves
        return (
            move(half0, lambda c, m, a, y: (m, c, a, y)),
            move(half1, lambda c, m, a, y: (m, c, 1 - a, y)),
        )

    got0, got1 = to_panel(halves0), to_panel(halves1)
    blocks = (got0[0], got1[0], got0[1], got1[1])
    blocks += tuple(swap(x) for x in blocks)

    far = gram_chunks(info, blocks, ((1, 2),), [chunk(BF16, size) for _, size in PARTS])
    far0, far1, far2 = up(far[0]), down(far[1]), across(far[2])
    terms = gram_chunks(info, blocks, ((1, 1), (1, 3), (0, 2)), [chunk(F32)] * 3)
    q1, q2, q3 = in_vmem(second_sums_kernel, [chunk()] * 3, *terms, far0, far1, far2)
    g1, g2, g3 = across(q1), down(q2), up(q3)
    later, _ = lax.optimization_barrier((blocks, q1))
    nearest, beside, below, center = gram_chunks(
        info, later, ((0, 1), (1, 0), (0, 3), (0, 0)), [chunk(F32), chunk(F32), chunk(), chunk(F32)]
    )
    near = down(below)
    v1, v2 = in_vmem(third_sums_kernel, [chunk()] * 2, nearest, beside, g1, g2, g3)
    w1, w2 = up(v1), across(v2)
    later, _ = lax.optimization_barrier((blocks, v1))
    turned = turned_panel(info, later)
    (mine,) = in_vmem(last_sums_kernel, [chunk()], center, w1, w2, near, after=(turned,))

    low, high, pair = up(mine), down(mine), across(mine)
    a1, a2, a3 = across(high), up(pair), down(high)
    ends = tuple(
        send(x[row : row + size]) for send, x, (row, size) in zip((down, up, across), (a1, a2, a3), PARTS)
    )
    swapped = (swap(jnp.concatenate([mine, low, high, pair])), swap(jnp.concatenate([a1, a2, a3])))
    ends, swapped = lax.optimization_barrier((ends, swapped))
    swapped += (swap(jnp.concatenate(ends)),)
    *sent, direct, flipped, mixed, scales = apply_poly(info, (mine, low, high, pair, a1, a2, a3), ends, swapped, turned)
    sent += apply_rest(info, direct, flipped, mixed, scales, turned)

    parts = (
        move(sent[0], lambda c, m, a, y: (m, c, a, y)),
        move(sent[1], lambda c, m, a, y: (m, c, 1 - a, y)),
        move(sent[2], lambda c, m, a, y: (m, 1 - c, a, y)),
        move(sent[3], lambda c, m, a, y: (m, 1 - c, 1 - a, y)),
    )
    return new_momentum, unpack(info, parts)


def solution(mesh):
    fine = Mesh(mesh.devices.reshape(4, 2, 2, 2, 4), AXES)
    tall = P(("x", "core", "zm", "zl"), "y")
    return jax.shard_map(
        on_device,
        mesh=fine,
        in_specs=(P(AXES, None, None), P(AXES), tall),
        out_specs=(tall, tall),
        check_vma=False,
    )
```

```python
import math

import jax
import jax.numpy as jnp
from jax import lax
from jax.experimental import pallas as pl
from jax.experimental.pallas import tpu as pltpu
from jax.sharding import Mesh
from jax.sharding import PartitionSpec as P

ROWS = 3584
COLS = 9216
MOMENTUM_RATE = 0.95
COEF_LINEAR = 3.4445
COEF_CUBIC = -4.775
COEF_QUINTIC = 2.0315
EPSILON = 1e-06

HEIGHT = 896
HALF = 1152
TILE = 128
SPLIT = ((0, 80), (80, 48))
LABEL = 16
SIDE = 256
BLOCKS = ROWS // SIDE
HALF_BLOCKS = BLOCKS // 2
CHUNK = HALF_BLOCKS * SIDE
PARTS = ((0, 608), (608, 592), (1200, 592))
WIDE = 640
SHARE = 576
AROUND = ROWS + CHUNK
BACK_ROWS = 4032

AXES = ("x", "core", "zm", "zl", "y")
PLANE = ("zm", "zl", "y")
BF16 = jnp.bfloat16
F32 = jnp.float32
MIB = 1 << 20
ANY = pl.BlockSpec(memory_space=pl.ANY)
HBM = pl.BlockSpec(memory_space=pltpu.HBM)
VMEM = pl.BlockSpec(memory_space=pltpu.VMEM)
SMEM = pl.BlockSpec(memory_space=pltpu.SMEM)


def cost(flops, size):
    return pl.CostEstimate(flops=int(flops), bytes_accessed=int(size), transcendentals=0)


def move(x, route):
    pairs = []
    for c in range(2):
        for m in range(2):
            for a in range(2):
                for y in range(4):
                    c2, m2, a2, y2 = route(c, m, a, y)
                    pairs.append((((c * 2 + m) * 2 + a) * 4 + y, ((c2 * 2 + m2) * 2 + a2) * 4 + y2 % 4))
    return lax.ppermute(x, AXES[1:], pairs)


def up(x):
    return move(x, lambda c, m, a, y: (c, m, a, y + 1))


def down(x):
    return move(x, lambda c, m, a, y: (c, m, a, y + 3))


def across(x):
    return move(x, lambda c, m, a, y: (c, m, 1 - a, y))


def swap(x):
    return move(x, lambda c, m, a, y: (1 - c, m, a, y))


def pack_kernel(ids, tiles, upper, lower, slots, places, held, first, second, sems, out_sems):
    n = tiles.shape[0]
    loads = [pltpu.make_async_copy(tiles.at[i], held.at[i], sems.at[i]) for i in range(n)]
    for load in loads:
        load.start()
    for o in range(upper.shape[0]):
        slots[o] = 0
        places[o] = -1

    @pl.loop(0, n)
    def _(i):
        row, column = ids[i] // 8, ids[i] % 8
        owner = row // 7 * 4 + column // 2
        slots[owner] = i
        places[owner] = row % 7 * 2 + column % 2

    for load in loads:
        load.wait()

    def copies(o):
        return (
            pltpu.make_async_copy(first.at[o], upper.at[o], out_sems.at[0, o]),
            pltpu.make_async_copy(second.at[o], lower.at[o], out_sems.at[1, o]),
        )

    @pl.loop(0, upper.shape[0])
    def _(o):
        slot = slots[o]
        for j in range(HALF // TILE):
            piece = held[slot, :, j * TILE : (j + 1) * TILE]
            for (row, size), out in zip(SPLIT, (first, second)):
                out[o, j * size : (j + 1) * size, :] = piece[row : row + size]
        place = jnp.full((LABEL, TILE), places[o], jnp.int32)
        first[o, first.shape[1] - LABEL :, :] = place.astype(F32).astype(BF16)
        for copy in copies(o):
            copy.start()

    @pl.loop(0, upper.shape[0])
    def _(o):
        for copy in copies(o):
            copy.wait()


def pack(ids, tiles):
    n = 16
    rows = [HALF // TILE * size for _, size in SPLIT]
    shapes = [(n, rows[0] + LABEL, TILE), (n, rows[1], TILE)]
    return pl.pallas_call(
        pack_kernel,
        in_specs=[SMEM, HBM],
        out_specs=[HBM] * 2,
        out_shape=[jax.ShapeDtypeStruct(shape, BF16) for shape in shapes],
        scratch_shapes=[pltpu.SMEM((n,), jnp.int32)] * 2
        + [pltpu.VMEM(tiles.shape, BF16)]
        + [pltpu.VMEM(shape, BF16) for shape in shapes]
        + [pltpu.SemaphoreType.DMA((tiles.shape[0],)), pltpu.SemaphoreType.DMA((2, n))],
        compiler_params=pltpu.CompilerParams(vmem_limit_bytes=62 * MIB),
        cost_estimate=cost(0, 4 * tiles.size),
    )(ids, tiles)


def momentum_kernel(part, info, arrived, momentum, *refs):
    new, half0, half1, tile, old, fresh, rounded, in_sems, out_sems = refs[-9:]
    n = HEIGHT // TILE
    row, size = SPLIT[part]

    def place(t, r):
        half = (t + info[14]) % 2
        columns = pl.ds(pl.multiple_of(half * HALF, TILE), HALF)
        return pl.ds(pl.multiple_of(r * TILE + row, 16), size), columns

    def reads(t, r):
        source = info[2 * r + (t + info[14]) % 2]
        i = t * n + r
        return (
            pltpu.make_async_copy(momentum.at[place(t, r)], old.at[i], in_sems.at[0, i]),
            pltpu.make_async_copy(arrived.at[source, 0 : HALF // TILE * size], tile.at[i], in_sems.at[1, i]),
        )

    def writes(t, r):
        i = t * n + r
        out = (half0, half1)[t].at[r]
        return (
            pltpu.make_async_copy(fresh.at[i], new.at[place(t, r)], out_sems.at[0, i]),
            pltpu.make_async_copy(rounded.at[i], out, out_sems.at[1, i]),
        )

    for t in range(2):
        for r in range(n):
            for copy in reads(t, r):
                copy.start()
    for t in range(2):

        @pl.loop(0, n)
        def _(r):
            i = t * n + r
            for copy in reads(t, r):
                copy.wait()
            for j in range(HALF // TILE):
                columns = slice(j * TILE, (j + 1) * TILE)
                g = tile[i, j * size : (j + 1) * size, :].astype(F32)
                later = MOMENTUM_RATE * old[i, :, columns] + g
                fresh[i, :, columns] = later
                rounded[i, :, columns] = (g + MOMENTUM_RATE * later).astype(BF16)
            for copy in writes(t, r):
                copy.start()

    for t in range(2):

        @pl.loop(0, n)
        def _(r):
            for copy in writes(t, r):
                copy.wait()


def update_momentum(info, arrived, momentum, part, so_far):
    more = () if so_far is None else (so_far,)
    n = 2 * HEIGHT // TILE
    size = SPLIT[part][1]
    return pl.pallas_call(
        lambda *refs: momentum_kernel(part, *refs),
        in_specs=[SMEM] + [HBM] * (2 + len(more)),
        out_specs=[HBM] * 3,
        out_shape=[
            jax.ShapeDtypeStruct(momentum.shape, F32),
            jax.ShapeDtypeStruct((n // 2, size, HALF), BF16),
            jax.ShapeDtypeStruct((n // 2, size, HALF), BF16),
        ],
        scratch_shapes=[
            pltpu.VMEM((n, HALF // TILE * size, TILE), BF16),
            pltpu.VMEM((n, size, HALF), F32),
            pltpu.VMEM((n, size, HALF), F32),
            pltpu.VMEM((n, size, HALF), BF16),
            pltpu.SemaphoreType.DMA((2, n)),
            pltpu.SemaphoreType.DMA((2, n)),
        ],
        input_output_aliases={3: 0} if more else {},
        compiler_params=pltpu.CompilerParams(vmem_limit_bytes=62 * MIB),
        cost_estimate=cost(0, HEIGHT * HALF * 12),
    )(info, arrived, momentum, *more)


def panel_copies(info, blocks, panel, columns=None):
    c, a = info[0], info[2]
    copies = []
    for i, block in enumerate(blocks):
        other, t, part = i // 4, i // 2 % 2, i % 2
        core = 1 - c if other else c
        z = 2 * core + (a + t) % 2
        src = block if columns is None else block.at[:, :, columns]
        row, size = SPLIT[part]
        rows = pl.ds(z * (HEIGHT // TILE), HEIGHT // TILE)
        copies.append((src, panel.at[rows, row : row + size]))
    return copies


def panel_shape(width):
    return pltpu.VMEM((ROWS // TILE, TILE, width), BF16)


def chip_at(info, flip, dy):
    a, y = info[2], info[3]
    return (1 - a if flip else a) * 4 + (y + dy) % 4


def load_all(copies, sems):
    copies = [pltpu.make_async_copy(src, dst, sems.at[i]) for i, (src, dst) in enumerate(copies)]
    for copy in copies:
        copy.start()
    for copy in copies:
        copy.wait()


def gram_kernel(dests, info, *refs):
    blocks, outs = refs[:8], refs[8:-2]
    panel, sems = refs[-2:]
    load_all(panel_copies(info, blocks, panel), sems)

    def term(b, d):
        left = panel[pl.ds(2 * b, 2)].reshape(SIDE, HALF)
        right = panel[pl.ds(2 * ((b + d) % BLOCKS), 2)].reshape(SIDE, HALF)
        return lax.dot_general(left, right, (((1,), (1,)), ((), ())), preferred_element_type=F32)

    base = HALF_BLOCKS * info[0]
    if len(dests) == 1:
        d = chip_at(info, *dests[0])
        for b in range(HALF_BLOCKS):
            block = term(base + b, d).astype(BF16)
            for out, (row, size) in zip(outs, PARTS):
                low, high = max(row, b * SIDE), min(row + size, (b + 1) * SIDE)
                if low < high:
                    out[low - row : high - row] = block[low - b * SIDE : high - b * SIDE]
    else:

        @pl.loop(0, HALF_BLOCKS)
        def _(b):
            for dest, out in zip(dests, outs):
                block = term(base + b, chip_at(info, *dest))
                out[pl.ds(pl.multiple_of(b * SIDE, SIDE), SIDE)] = block.astype(out.dtype)


def gram_chunks(info, blocks, dests, shapes):
    return pl.pallas_call(
        lambda *refs: gram_kernel(dests, *refs),
        in_specs=[SMEM] + [HBM] * 8,
        out_specs=[VMEM] * len(shapes),
        out_shape=shapes,
        scratch_shapes=[panel_shape(HALF), pltpu.SemaphoreType.DMA((8,))],
        compiler_params=pltpu.CompilerParams(vmem_limit_bytes=24 * MIB),
        cost_estimate=cost(len(dests) * 2 * CHUNK * SIDE * HALF, 8.3e6 + len(dests) * CHUNK * SIDE * 4),
    )(info, *blocks)


def chunk(dtype=BF16, rows=CHUNK):
    return jax.ShapeDtypeStruct((rows, SIDE), dtype)


def second_sums_kernel(p1, p2, p3, r1, r2, r3, q1, q2, q3):
    for own, got, out, (row, size) in zip((p1, p2, p3), (r1, r2, r3), (q1, q2, q3), PARTS):
        if row:
            out[:row] = own[:row].astype(BF16)
        out[row : row + size] = (own[row : row + size] + got[...].astype(F32)).astype(BF16)
        if row + size < CHUNK:
            out[row + size :] = own[row + size :].astype(BF16)


def third_sums_kernel(p1, p2, g1, g2, g3, v1, v2):
    v1[...] = (p1[...] + (g1[...].astype(F32) + g3[...].astype(F32))).astype(BF16)
    v2[...] = (p2[...] + g2[...].astype(F32)).astype(BF16)


def last_sums_kernel(p, v1, v2, v3, turned, out):
    total = p[...] + (v1[...].astype(F32) + v2[...].astype(F32) + v3[...].astype(F32))
    out[...] = total.astype(BF16)


def in_vmem(kernel, shapes, *args, after=()):
    size = sum(x.size * x.dtype.itemsize for x in args)
    return pl.pallas_call(
        kernel,
        in_specs=[VMEM] * len(args) + [ANY] * len(after),
        out_specs=[VMEM] * len(shapes),
        out_shape=shapes,
        compiler_params=pltpu.CompilerParams(vmem_limit_bytes=16 * MIB),
        cost_estimate=cost(0, size),
    )(*args, *after)


def turn_kernel(info, *refs):
    blocks, out, held, flat, sems = refs[:8], *refs[8:]
    c = info[0]
    shift = pl.multiple_of(512 * c, TILE)
    load_all(panel_copies(info, blocks, held, pl.ds(shift, WIDE)), sems)
    for r in range(ROWS // TILE):
        flat[:, r * TILE : (r + 1) * TILE] = held[r].T
    out[:512, :ROWS] = flat[pl.ds(pl.multiple_of(128 * c, 64), 512), :]
    out[512:, :ROWS] = flat[pl.ds(pl.multiple_of(512 - 448 * c, 64), 64), :]
    out[:, ROWS:] = out[:, :CHUNK]


def turned_panel(info, blocks):
    return pl.pallas_call(
        turn_kernel,
        in_specs=[SMEM] + [HBM] * 8,
        out_specs=VMEM,
        out_shape=jax.ShapeDtypeStruct((SHARE, AROUND), BF16),
        scratch_shapes=[panel_shape(WIDE), pltpu.VMEM((WIDE, ROWS), BF16), pltpu.SemaphoreType.DMA((8,))],
        compiler_params=pltpu.CompilerParams(vmem_limit_bytes=24 * MIB),
        cost_estimate=cost(0, 1.2e7),
    )(info, *blocks)


SOURCES = ((0, 0), (0, 3), (0, 1), (1, 0), (1, 1), (1, 3), (0, 2), (1, 2))


def apply_kernel(info, *refs):
    own, ends, swapped = refs[:7], refs[7:10], refs[10:13]
    turned = refs[13]
    outs, rest_direct, rest_flipped, all_mixed, scales = refs[14:16], *refs[16:20]
    direct, flipped, panel, mixed, stage, extra, sems, panel_sem, out_sems, keep_sems = refs[20:]
    c = info[0]
    panel_copy = pltpu.make_async_copy(turned, panel, panel_sem)
    panel_copy.start()
    pieces = [(c, ref, 0, rel) for ref, rel in zip(own, SOURCES)]
    pieces += [(1 - c, swapped[n // 4], n % 4 * CHUNK, SOURCES[n]) for n in range(7)]
    pieces.append((1 - c, swapped[2], 0, SOURCES[7]))
    for n, (core, ref, row, rel) in enumerate(pieces):
        d = chip_at(info, *rel)

        @pl.loop(0, HALF_BLOCKS)
        def _(b):
            i = (core * HALF_BLOCKS + b + d) % BLOCKS
            src = ref.at[pl.ds(pl.multiple_of(row + b * SIDE, SIDE), SIDE)]
            pltpu.make_async_copy(src, direct.at[i, pl.ds(pl.multiple_of((7 - d) * SIDE, SIDE), SIDE)], sems.at[n]).start()

    d = chip_at(info, *SOURCES[7])
    last = []
    for ref, (row, size) in zip(ends, PARTS):
        for b in range(HALF_BLOCKS):
            low, high = max(row, b * SIDE), min(row + size, (b + 1) * SIDE)
            if low < high:
                i = (c * HALF_BLOCKS + b + d) % BLOCKS
                start = pl.multiple_of((7 - d) * SIDE + low - b * SIDE, 16)
                src = ref.at[low - row : high - row]
                last.append(pltpu.make_async_copy(src, direct.at[i, pl.ds(start, high - low)], sems.at[15 + len(last)]))
    for copy in last:
        copy.start()
    for n in range(15):
        whole = direct.at[0:HALF_BLOCKS, 0:SIDE]
        pltpu.make_async_copy(whole, whole, sems.at[n]).wait()
    for copy in last:
        copy.wait()
    panel_copy.wait()

    total = jnp.zeros((), F32)
    on = lax.broadcasted_iota(jnp.int32, (SIDE, SIDE), 0) == lax.broadcasted_iota(jnp.int32, (SIDE, SIDE), 1)
    diagonal = jnp.zeros((SIDE, SIDE), F32)
    for i in range(BLOCKS):
        diagonal += direct[i, 7 * SIDE :, :].astype(F32)
    total = jnp.sum(jnp.where(on, diagonal, 0.0))
    total = jnp.full((1, SIDE), total, F32)
    factor = math.sqrt(ROWS) / (2.0 * (jnp.sqrt(total) + EPSILON))
    square = factor * factor

    def product(i, x):
        return gram_times(i, x, direct.at[i], flipped.at[i]) * square

    @pl.loop(0, BLOCKS)
    def _(i):
        for e in range(1, 7):
            far = (i + e) % BLOCKS
            flipped[i, (e - 1) * SIDE : e * SIDE, :] = direct[far, (7 - e) * SIDE : (8 - e) * SIDE, :].T
        columns = pl.ds(pl.multiple_of(i * SIDE, SIDE), SIDE)
        mix = COEF_CUBIC * panel[:, columns].astype(F32) + COEF_QUINTIC * product(i, panel)
        mix = mix.astype(BF16)
        mixed[:, columns] = mix

        @pl.when(i < HALF_BLOCKS)
        def _():
            mixed[:, pl.ds(pl.multiple_of(i * SIDE + ROWS, SIDE), SIDE)] = mix

    other = (1 - c) * HALF_BLOCKS
    scale = math.sqrt(COLS) * factor
    scales[...] = jnp.concatenate([scale] * 4 + [square] * 4)
    keeps = [
        pltpu.make_async_copy(direct.at[pl.ds(other, HALF_BLOCKS)], rest_direct, keep_sems.at[0]),
        pltpu.make_async_copy(flipped.at[pl.ds(other, HALF_BLOCKS)], rest_flipped, keep_sems.at[1]),
        pltpu.make_async_copy(mixed, all_mixed, keep_sems.at[2]),
    ]
    for copy in keeps:
        copy.start()

    @pl.loop(0, HALF_BLOCKS)
    def _(b):
        i = c * HALF_BLOCKS + b
        columns = pl.ds(pl.multiple_of(i * SIDE, SIDE), SIDE)
        result = scale * (COEF_LINEAR * panel[:, columns].astype(F32) + product(i, mixed))
        stage[pl.ds(pl.multiple_of(b * SIDE, SIDE), SIDE)] = result.astype(BF16).T

    send_back(info, stage, extra, outs, out_sems)
    for copy in keeps:
        copy.wait()


def gram_times(i, x, direct, flipped):
    first = pl.ds(pl.multiple_of((i + 7) % BLOCKS * SIDE, SIDE), 8 * SIDE)
    rest = pl.ds(pl.multiple_of((i + 1) % BLOCKS * SIDE, SIDE), 6 * SIDE)
    result = jnp.dot(x[:, first], direct[...], preferred_element_type=F32)
    return result + jnp.dot(x[:, rest], flipped[...], preferred_element_type=F32)


def send_back(info, stage, extra, outs, sems):
    a = info[2]
    sends = []
    for side, out in enumerate(outs):
        owner = 1 - a if side else a
        start = pl.multiple_of(owner * HEIGHT, 128)
        for j in range(4):
            rows = pl.ds(start, HEIGHT)
            sends.append((stage.at[rows, j * TILE : (j + 1) * TILE], out.at[pl.ds(j * HEIGHT, HEIGHT)]))
        halves = [stage[pl.ds(pl.multiple_of(start + row, 64), 448), 512:] for row in (0, 448)]
        extra[side] = jnp.concatenate(halves, axis=1)
        sends.append((extra.at[side], out.at[pl.ds(4 * HEIGHT, 448)]))
    load_all(sends, sems)


def rest_kernel(info, direct, flipped, panel, all_mixed, scales, out0, out1, mixed, stage, extra, sems):
    b = pl.program_id(0)

    @pl.when(b == 0)
    def _():
        load_all([(all_mixed, mixed)], sems)

    i = (1 - info[0]) * HALF_BLOCKS + b
    product = gram_times(i, mixed, direct.at[0], flipped.at[0]) * scales[4:5]
    result = scales[0:1] * (COEF_LINEAR * panel[...].astype(F32) + product)
    stage[pl.ds(pl.multiple_of(b * SIDE, SIDE), SIDE)] = result.astype(BF16).T

    @pl.when(b == HALF_BLOCKS - 1)
    def _():
        send_back(info, stage, extra, (out0, out1), sems)


def apply_rest(info, direct, flipped, mixed, scales, turned):
    return pl.pallas_call(
        rest_kernel,
        grid_spec=pltpu.PrefetchScalarGridSpec(
            num_scalar_prefetch=1,
            grid=(HALF_BLOCKS,),
            in_specs=[
                pl.BlockSpec((1, 8 * SIDE, SIDE), lambda b, s: (b, 0, 0)),
                pl.BlockSpec((1, 6 * SIDE, SIDE), lambda b, s: (b, 0, 0)),
                pl.BlockSpec((SHARE, SIDE), lambda b, s: (0, (1 - s[0]) * HALF_BLOCKS + b)),
                HBM,
                VMEM,
            ],
            out_specs=[HBM] * 2,
            scratch_shapes=[
                pltpu.VMEM((SHARE, AROUND), BF16),
                pltpu.VMEM((CHUNK, SHARE), BF16),
                pltpu.VMEM((2, 448, TILE), BF16),
                pltpu.SemaphoreType.DMA((10,)),
            ],
        ),
        out_shape=[jax.ShapeDtypeStruct((BACK_ROWS, TILE), BF16)] * 2,
        compiler_params=pltpu.CompilerParams(vmem_limit_bytes=62 * MIB),
        cost_estimate=cost(ROWS * ROWS * SHARE, 2e7),
    )(info, direct, flipped, turned, mixed, scales)


def apply_poly(info, own, ends, swapped, turned):
    return pl.pallas_call(
        apply_kernel,
        in_specs=[SMEM] + [HBM] * 14,
        out_specs=[HBM] * 5 + [VMEM],
        out_shape=[jax.ShapeDtypeStruct((BACK_ROWS, TILE), BF16)] * 2
        + [
            jax.ShapeDtypeStruct((HALF_BLOCKS, 8 * SIDE, SIDE), BF16),
            jax.ShapeDtypeStruct((HALF_BLOCKS, 6 * SIDE, SIDE), BF16),
            jax.ShapeDtypeStruct((SHARE, AROUND), BF16),
            jax.ShapeDtypeStruct((8, SIDE), F32),
        ],
        scratch_shapes=[
            pltpu.VMEM((BLOCKS, 8 * SIDE, SIDE), BF16),
            pltpu.VMEM((BLOCKS, 6 * SIDE, SIDE), BF16),
            pltpu.VMEM((SHARE, AROUND), BF16),
            pltpu.VMEM((SHARE, AROUND), BF16),
            pltpu.VMEM((CHUNK, SHARE), BF16),
            pltpu.VMEM((2, 448, TILE), BF16),
            pltpu.SemaphoreType.DMA((32,)),
            pltpu.SemaphoreType.DMA,
            pltpu.SemaphoreType.DMA((10,)),
            pltpu.SemaphoreType.DMA((3,)),
        ],
        compiler_params=pltpu.CompilerParams(vmem_limit_bytes=58 * MIB),
        cost_estimate=cost(3 * ROWS * ROWS * SHARE, 4e7),
    )(info, *own, *ends, *swapped, turned)


def unpack_kernel(info, r0, r1, r2, r3, update):
    m, a = info[1], info[2]
    for s, got in enumerate((r0, r1, r2, r3)):
        core = 1 - m if s >= 2 else m
        side = 1 - a if s % 2 else a
        for j in range(4):
            start = pl.multiple_of((9 * side + j + 5 * core) * TILE, TILE)
            update[:, pl.ds(start, TILE)] = got[j * HEIGHT : (j + 1) * HEIGHT]
    for s, (one, two) in enumerate(((r0, r2), (r1, r3))):
        side = 1 - a if s else a
        one, two = one[4 * HEIGHT :], two[4 * HEIGHT :]
        low, high = jnp.where(m == 0, one, two), jnp.where(m == 0, two, one)
        tile = pl.ds(pl.multiple_of((9 * side + 4) * TILE, TILE), TILE)
        update[:448, tile] = jnp.concatenate([low[:, :64], high[:, :64]], axis=1)
        update[448:, tile] = jnp.concatenate([low[:, 64:], high[:, 64:]], axis=1)


def unpack(info, parts):
    return pl.pallas_call(
        unpack_kernel,
        in_specs=[SMEM] + [VMEM] * 4,
        out_specs=VMEM,
        out_shape=jax.ShapeDtypeStruct((HEIGHT, 2304), BF16),
        compiler_params=pltpu.CompilerParams(vmem_limit_bytes=32 * MIB),
        cost_estimate=cost(0, 8.3e6),
    )(info, *parts)


def on_device(grad_tiles, tile_ids, momentum):
    core, zm, zl, y = (lax.axis_index(name) for name in AXES[1:])
    info = jnp.stack([core, zm, zl, y]).astype(jnp.int32)
    tile_count = grad_tiles.shape[0]

    upper, lower = pack(tile_ids, grad_tiles)
    upper = lax.all_to_all(upper, PLANE, split_axis=0, concat_axis=0, tiled=True)
    lower, _ = lax.optimization_barrier((lower, upper))
    lower = lax.all_to_all(lower, PLANE, split_axis=0, concat_axis=0, tiled=True)

    got_labels = upper[:, -1, 0].astype(jnp.int32)
    found = got_labels[None, :] == jnp.arange(tile_count, dtype=jnp.int32)[:, None]
    sources = jnp.sum(jnp.where(found, jnp.arange(16, dtype=jnp.int32)[None, :], 0), axis=1)
    details = jnp.concatenate([sources, zl[None].astype(jnp.int32)])
    new_momentum, *halves0 = update_momentum(details, upper, momentum, 0, None)
    new_momentum, *halves1 = update_momentum(details, lower, momentum, 1, new_momentum)

    def to_panel(halves):
        half0, half1 = halves
        return (
            move(half0, lambda c, m, a, y: (m, c, a, y)),
            move(half1, lambda c, m, a, y: (m, c, 1 - a, y)),
        )

    got0, got1 = to_panel(halves0), to_panel(halves1)
    blocks = (got0[0], got1[0], got0[1], got1[1])
    blocks += tuple(swap(x) for x in blocks)

    far = gram_chunks(info, blocks, ((1, 2),), [chunk(BF16, size) for _, size in PARTS])
    far0, far1, far2 = up(far[0]), down(far[1]), across(far[2])
    terms = gram_chunks(info, blocks, ((1, 1), (1, 3), (0, 2)), [chunk(F32)] * 3)
    q1, q2, q3 = in_vmem(second_sums_kernel, [chunk()] * 3, *terms, far0, far1, far2)
    g1, g2, g3 = across(q1), down(q2), up(q3)
    later, _ = lax.optimization_barrier((blocks, q1))
    nearest, beside, below, center = gram_chunks(
        info, later, ((0, 1), (1, 0), (0, 3), (0, 0)), [chunk(F32), chunk(F32), chunk(), chunk(F32)]
    )
    near = down(below)
    v1, v2 = in_vmem(third_sums_kernel, [chunk()] * 2, nearest, beside, g1, g2, g3)
    w1, w2 = up(v1), across(v2)
    later, _ = lax.optimization_barrier((blocks, v1))
    turned = turned_panel(info, later)
    (mine,) = in_vmem(last_sums_kernel, [chunk()], center, w1, w2, near, after=(turned,))

    low, high, pair = up(mine), down(mine), across(mine)
    a1, a2, a3 = across(high), up(pair), down(high)
    ends = tuple(
        send(x[row : row + size]) for send, x, (row, size) in zip((down, up, across), (a1, a2, a3), PARTS)
    )
    swapped = (swap(jnp.concatenate([mine, low, high, pair])), swap(jnp.concatenate([a1, a2, a3])))
    ends, near_swap = lax.optimization_barrier((ends, swapped[0]))
    swapped = (near_swap, swapped[1], swap(jnp.concatenate(ends)))
    *sent, direct, flipped, mixed, scales = apply_poly(info, (mine, low, high, pair, a1, a2, a3), ends, swapped, turned)
    sent += apply_rest(info, direct, flipped, mixed, scales, turned)

    parts = (
        move(sent[0], lambda c, m, a, y: (m, c, a, y)),
        move(sent[1], lambda c, m, a, y: (m, c, 1 - a, y)),
        move(sent[2], lambda c, m, a, y: (m, 1 - c, a, y)),
        move(sent[3], lambda c, m, a, y: (m, 1 - c, 1 - a, y)),
    )
    return new_momentum, unpack(info, parts)


def solution(mesh):
    fine = Mesh(mesh.devices.reshape(4, 2, 2, 2, 4), AXES)
    tall = P(("x", "core", "zm", "zl"), "y")
    return jax.shard_map(
        on_device,
        mesh=fine,
        in_specs=(P(AXES, None, None), P(AXES), tall),
        out_specs=(tall, tall),
        check_vma=False,
    )
```
